256 devices in a mesh: blk: 64 (over z, y, core), rep: 4 (over x).
Axes of the slice: x: 4, y: 4, z: 8, core: 2. Of those that a mesh axis runs over, the one named last changes fastest.
Arguments:
- blocks: bfloat16 [1024, 128, 8192], P(('blk', 'rep')), may hold values from -6 to 6
- coords: int32 [3, 1024], P(None, ('blk', 'rep')), may hold values from 0 to 2047, as said below
- counts: int32 [256], P(('blk', 'rep')), may hold values from 1 to 4, as said below
- factor_b: bfloat16 [131072, 32], P('blk'), may hold values from -2 to 2
- factor_c: bfloat16 [32768, 16], P('blk'), may hold values from -3 to 3
- start: float32 [512, 32], replicated, may hold values from -6 to 6
Outputs:
- factor_a: float32 [262144, 32], P(('blk', 'rep'))
The draws below stay inside these ranges and needn't reach their ends.
Inputs may be any that keep to these rules, and one draw needn't show every extreme that they name: coords[0] of a slot on blk index b lies in b * 32 to (b + 1) * 32 - 1; coords[1] lies below 1024 and coords[2] below 512. Among the 4 slots of one device, at most 2 have coords[1] in the same slab of 16 row blocks, and at most 2 have coords[2] in the same slab of 8 row blocks; every device reaches both bounds. Slots 0 to counts - 1 of a device hold live blocks; some device has all 4 live.
All inputs are finite; a program needn't handle non-finite values.
Results may differ from the reference program's by a relative error of at most 0.003.
Values may be sent and summed in bfloat16 or wider, within the bound.
A program may use at most 128 MiB of HBM per device.

```python
import math
import jax
import jax.numpy as jnp
from jax import lax

BI = 128
BJ = 128
BK = 64
R1 = 32
R2 = 32
R3 = 16
RR = 512
NB = 4
IB_DEV = 32
JB_DEV = 16
KB_DEV = 8
ITERS = 4
GROUPS = 64
REPS = 4
SLOTS = 1024
I_ROWS = 262144
J_ROWS = 131072
K_ROWS = 32768


def slab_owners(owner_key, device_of, column):
    keys = jax.random.split(owner_key, SLOTS // NB)

    def one_order(single_key):
        return jax.random.permutation(single_key, GROUPS)
    orders = jax.vmap(one_order)(keys)
    return orders[device_of, column]


def draw_coords(key, part):
    base = jax.random.fold_in(key, 17)
    key_rows, key_b, key_bl, key_c, key_cl = jax.random.split(base, 5)
    slot_ids = jnp.arange(SLOTS, dtype=jnp.int32)
    device_of = slot_ids // NB
    position = slot_ids % NB
    slab_of = device_of // REPS
    row_block = slab_of * IB_DEV + jax.random.randint(key_rows, (SLOTS,), 0, IB_DEV)
    column = jnp.maximum(position - 1, 0)
    second = slab_owners(key_b, device_of, column) * JB_DEV + jax.random.randint(key_bl, (SLOTS,), 0, JB_DEV)
    third = slab_owners(key_c, device_of, column) * KB_DEV + jax.random.randint(key_cl, (SLOTS,), 0, KB_DEV)
    return jnp.stack([row_block, second, third]).astype(jnp.int32)


def draw_counts(key, part):
    base = jax.random.fold_in(key, 29)
    key_first, key_second = jax.random.split(base, 2)
    devices_all = SLOTS // NB
    drawn = jax.random.randint(key_first, (devices_all,), 1, NB + 1)
    chosen = jax.random.randint(key_second, (), 0, devices_all)
    return jnp.where(jnp.arange(devices_all) == chosen, NB, drawn).astype(jnp.int32)


def column_mix(key_scale, noise_part, common_part, common_share, fan_size, bound_value):
    width = noise_part.shape[1]
    scales = jnp.exp(jax.random.uniform(key_scale, (1, width), jnp.float32, 0.0, math.log(8.0)))
    values = scales * (noise_part + common_share * common_part) / math.sqrt(fan_size)
    return jnp.clip(values, -bound_value, bound_value).astype(jnp.bfloat16)


def draw_factor_b(key, part):
    key = jax.random.fold_in(key, 41)
    key_noise, key_common, key_scale = jax.random.split(key, 3)
    noise_part = jnp.clip(jax.random.normal(key_noise, (J_ROWS, R2), jnp.float32), -4.0, 4.0)
    common_part = jnp.clip(jax.random.normal(key_common, (J_ROWS, 1), jnp.float32), -4.0, 4.0)
    common_share = 0.4
    return column_mix(key_scale, noise_part, common_part, common_share, BJ, 2.0)


def draw_factor_c(key, part):
    key = jax.random.fold_in(key, 53)
    key_noise, key_common, key_scale = jax.random.split(key, 3)
    noise_part = jnp.clip(jax.random.normal(key_noise, (K_ROWS, R3), jnp.float32), -4.0, 4.0)
    common_part = jnp.clip(jax.random.normal(key_common, (K_ROWS, 1), jnp.float32), -4.0, 4.0)
    common_share = 0.4
    return column_mix(key_scale, noise_part, common_part, common_share, BK, 3.0)


def block_scale(stream_key, extent, shards, least, largest):
    level = 1.0
    for dim, shards_of in shards:
        heights = jax.random.uniform(jax.random.fold_in(jax.random.fold_in(stream_key, 6), dim), (shards_of,), jnp.float32, least / len(shards), largest / len(shards))
        level = level * jnp.repeat(jnp.exp(heights), extent[dim] // shards_of).reshape((-1,) + (1,) * (len(extent) - 1 - dim))
    return level


def bell_draw(key, shape, deviation, limit, pieces=(), held_as=jnp.bfloat16):
    values = jax.random.normal(key, shape, jnp.float32) * deviation
    if len(pieces) > 0:
        values = block_scale(key, shape, pieces, -0.22, 0.18) * values
    return jnp.clip(values, min=-limit, max=limit).astype(held_as)


def setup_inputs(seed: int = 0) -> dict:
    seeds = jax.random.split(jax.random.key(seed), 7)
    blocks = bell_draw(seeds[0], (SLOTS, BI, BJ * BK), 1.0, 6.0, ((0, 256),))
    coords = draw_coords(jax.random.fold_in(seeds[6], 71), 0)
    counts = draw_counts(jax.random.fold_in(seeds[6], 71), 0)
    factor_b = draw_factor_b(jax.random.fold_in(seeds[6], 71), 0)
    factor_c = draw_factor_c(jax.random.fold_in(seeds[6], 71), 0)
    start = bell_draw(seeds[5], (RR, R1), 1.0, 6.0, (), jnp.float32)
    return dict(blocks=blocks, coords=coords, counts=counts, factor_b=factor_b, factor_c=factor_c, start=start)


def orthonormal(matrix):
    inner = jnp.dot(matrix.T, matrix, precision=lax.Precision.HIGHEST)
    lower_factor = jnp.linalg.cholesky(inner)
    return jax.scipy.linalg.solve_triangular(lower_factor, matrix.T, lower=True).T

def reference(blocks, coords, counts, factor_b, factor_c, start):
    slot_ids = jnp.arange(SLOTS, dtype=jnp.int32)
    alive = (slot_ids % NB < counts[slot_ids // NB]).astype(jnp.float32)
    rows_b = factor_b.reshape(J_ROWS // BJ, BJ, R2)
    rows_c = factor_c.reshape(K_ROWS // BK, BK, R3)

    def accumulate(total, index):
        cube = blocks[index].reshape(BI, BJ, BK).astype(jnp.float32)
        mode_c = rows_c[coords[2, index]].astype(jnp.float32)
        mode_b = rows_b[coords[1, index]].astype(jnp.float32)
        folded = jnp.einsum('ijk,kr->irj', cube, mode_c, precision=lax.Precision.HIGHEST)
        folded = lax.optimization_barrier(folded.astype(jnp.bfloat16)).astype(jnp.float32)
        partial_rows = jnp.einsum('irj,jq->iqr', folded, mode_b, precision=lax.Precision.HIGHEST)
        partial_rows = partial_rows.reshape(BI, RR) * alive[index]
        top_row = (coords[0, index] * BI).astype(jnp.int32)
        current = lax.dynamic_slice(total, (top_row, jnp.int32(0)), (BI, RR))
        total = lax.dynamic_update_slice(total, current + partial_rows, (top_row, jnp.int32(0)))
        return (total, None)
    unfolded, _ = lax.scan(accumulate, jnp.zeros((I_ROWS, RR), jnp.float32), slot_ids)
    gram_matrix = jnp.dot(unfolded.T, unfolded, precision=lax.Precision.HIGHEST)
    subspace = orthonormal(start)
    for iteration in range(ITERS):
        subspace = orthonormal(jnp.dot(gram_matrix, subspace, precision=lax.Precision.HIGHEST))
    mapped = jnp.dot(unfolded, subspace, precision=lax.Precision.HIGHEST)
    small_gram = jnp.dot(mapped.T, mapped, precision=lax.Precision.HIGHEST)
    lower_factor = jnp.linalg.cholesky(small_gram)
    return jax.scipy.linalg.solve_triangular(lower_factor, mapped.T, lower=True).T
```

```python
import jax
import jax.numpy as jnp
from jax import lax
from jax.experimental import pallas as pl
from jax.experimental.pallas import tpu as pltpu
from jax.sharding import PartitionSpec as P

BI = 128
BJ = 128
BK = 64
R2 = 32
R3 = 16
RR = 512
IB_DEV = 32
ITERS = 4
NX = 4
NY = 4
NZ = 8
PACKED = 1280
HALF = PACKED // 2
PART_X = HALF // NX
PART_Y = PART_X // NY
HIGHEST = lax.Precision.HIGHEST
F32 = jnp.float32
BF16 = jnp.bfloat16
TILES = [(a, b) for a in range(4) for b in range(a, 4)]


def dot_nt(left, right):
    return lax.dot_general(left, right, (((1,), (1,)), ((), ())), preferred_element_type=F32)


def dot_tn(left, right):
    return lax.dot_general(left, right, (((0,), (0,)), ((), ())), preferred_element_type=F32)


def iota(shape, dim):
    return lax.broadcasted_iota(jnp.int32, shape, dim)


def contract_kernel(pick_ref, x_ref, c_ref, b_ref, p_ref, pb_ref):
    slot = pl.program_id(0)
    alive = (slot < pick_ref[5, 0]).astype(F32)
    odd = pick_ref[4, slot] > 0
    pair = c_ref[0, 0].astype(F32)
    mode_c = jnp.where(odd, pair[:, BK:], pair[:, :BK])
    wide = jnp.concatenate([mode_c] * 8, axis=1)
    tall = jnp.concatenate([wide] * 8, axis=0)
    fold_mask = iota((128, 512), 0) // R3 == iota((128, 512), 1) // BK
    fold_t = jnp.where(fold_mask, tall, 0.0).astype(BF16)
    spread_q = (iota((RR, R2), 0) // R3 == iota((RR, R2), 1)).astype(F32).astype(BF16)
    mode_b = jnp.dot(spread_q, b_ref[0, 0], preferred_element_type=F32).astype(BF16)
    keep = (iota((RR, 256), 0) % R3 == iota((RR, 256), 1) % R3).astype(F32)
    total = jnp.zeros((BI, RR), F32)
    for t in range(8):
        folded = jnp.concatenate(
            [
                dot_nt(x_ref[0, :, pl.ds((2 * t + h) * 512, 512)], fold_t).astype(BF16)
                for h in range(2)
            ],
            axis=1,
        )
        spread_j = (iota((BJ, 256), 0) == 16 * t + iota((BJ, 256), 1) // R3).astype(F32).astype(BF16)
        expanded = jnp.dot(mode_b, spread_j, preferred_element_type=F32) * keep
        total += dot_nt(folded, expanded.astype(BF16))
    total = total * alive
    p_ref[0] = total
    pb_ref[0] = total.astype(BF16)


def contract(blocks, picks, fetched):
    slots = blocks.shape[0]
    return pl.pallas_call(
        contract_kernel,
        grid_spec=pltpu.PrefetchScalarGridSpec(
            num_scalar_prefetch=1,
            grid=(slots,),
            in_specs=[
                pl.BlockSpec((1, BI, BJ * BK), lambda s, pick: (s, 0, 0)),
                pl.BlockSpec((1, 1, R3, 128), lambda s, pick: (pick[2, s], pick[3, s], 2, 0)),
                pl.BlockSpec((1, 1, R2, 128), lambda s, pick: (pick[0, s], pick[1, s], 0, 0)),
            ],
            out_specs=[
                pl.BlockSpec((1, BI, RR), lambda s, pick: (s, 0, 0)),
                pl.BlockSpec((1, BI, RR), lambda s, pick: (s, 0, 0)),
            ],
        ),
        out_shape=[
            jax.ShapeDtypeStruct((slots, BI, RR), F32),
            jax.ShapeDtypeStruct((slots, BI, RR), BF16),
        ],
        compiler_params=pltpu.CompilerParams(vmem_limit_bytes=40 * 1024 * 1024),
        name="contract",
    )(picks, blocks, fetched, fetched)


def gram_kernel(pb_ref, code_ref, gram_ref, rows, codes, g, o, from_c, from_x, from_y, from_z, send, recv):
    b = lax.axis_index("blk")
    x = lax.axis_index("rep")
    c = lax.rem(b, 2)
    y = lax.rem(b // 2, NY)
    z = b // (2 * NY)

    def at_x(d):
        return {"blk": b, "rep": lax.rem(x + d, NX)}

    def at_y(d):
        return {"blk": (z * NY + lax.rem(y + d, NY)) * 2 + c, "rep": x}

    def at_z(d):
        return {"blk": (lax.rem(z + d, NZ) * NY + y) * 2 + c, "rep": x}

    at_c = {"blk": b + 1 - 2 * c, "rep": x}
    partners = [at_x(d) for d in range(1, NX)] + [at_y(d) for d in range(1, NY)]
    partners += [at_z(d) for d in range(1, NZ)] + [at_c]
    barrier = pltpu.get_barrier_semaphore()
    for partner in partners:
        pl.semaphore_signal(barrier, inc=1, device_id=partner, device_id_type=pl.DeviceIdType.MESH)
    pl.semaphore_wait(barrier, len(partners))

    started = []

    def push(source, target, device):
        k = len(started)
        copy = pltpu.make_async_remote_copy(
            src_ref=source,
            dst_ref=target,
            send_sem=send.at[k],
            recv_sem=recv.at[k],
            device_id=device,
            device_id_type=pl.DeviceIdType.MESH,
        )
        copy.start()
        started.append(copy)
        return copy

    quarter = BI // NX

    def piece(n, count):
        return pl.ds(pl.multiple_of(n * count, 8), count)

    tags = [push(code_ref, codes.at[x], at_x(d)) for d in range(1, NX)]
    moves = [
        push(pb_ref.at[:, pl.ds(pl.multiple_of(lax.rem(x + d, NX) * quarter, quarter), quarter), :], rows.at[x], at_x(d))
        for d in range(1, NX)
    ]
    codes[x] = code_ref[...]
    rows[x] = pb_ref[:, pl.ds(pl.multiple_of(x * quarter, quarter), quarter), :]
    for copy in tags:
        copy.wait_recv()
    along = jnp.concatenate([codes[n][0:1, :] for n in range(NX)], axis=1)
    down = jnp.concatenate([codes[n].T[:, 0:1] for n in range(NX)], axis=0)
    same = (down == along).astype(F32).astype(BF16)
    for copy in moves:
        copy.wait_recv()
    held = rows[...].reshape(RR, RR)
    summed = jnp.dot(same, held, preferred_element_type=F32)
    high = summed.astype(BF16)
    low = (summed - high.astype(F32)).astype(BF16)
    at = 0
    for a in range(4):
        left = held[:, 128 * a : 128 * a + 128]
        strip = dot_tn(left, high[:, 128 * a :]) + dot_tn(left, low[:, 128 * a :])
        for n in range(4 - a):
            g[pl.ds(128 * at, 128), :] = strip[:, 128 * n : 128 * n + 128]
            at += 1

    base = c * HALF
    copy = push(g.at[piece(1 - c, HALF)], from_c, at_c)
    copy.wait_recv()
    g[piece(c, HALF), :] += from_c[...]

    copies = [
        push(g.at[pl.ds(pl.multiple_of(base + lax.rem(x + d, NX) * PART_X, 8), PART_X)], from_x.at[d - 1], at_x(d))
        for d in range(1, NX)
    ]
    for copy in copies:
        copy.wait_recv()
    base = base + x * PART_X
    mine = pl.ds(pl.multiple_of(base, 8), PART_X)
    g[mine, :] = g[mine, :] + from_x[0] + from_x[1] + from_x[2]

    copies = [
        push(g.at[pl.ds(pl.multiple_of(base + lax.rem(y + d, NY) * PART_Y, 8), PART_Y)], from_y.at[d - 1], at_y(d))
        for d in range(1, NY)
    ]
    for copy in copies:
        copy.wait_recv()
    base = base + y * PART_Y
    mine = pl.ds(pl.multiple_of(base, 8), PART_Y)
    from_z[z] = g[mine, :] + from_y[0] + from_y[1] + from_y[2]

    copies = [push(from_z.at[z], from_z.at[z], at_z(d)) for d in range(1, NZ)]
    for copy in copies:
        copy.wait_recv()
    total = from_z[0]
    for n in range(1, NZ):
        total = total + from_z[n]
    o[mine, :] = total

    copies = [push(o.at[mine], o.at[mine], at_y(d)) for d in range(1, NY)]
    for copy in copies:
        copy.wait_recv()
    mine = pl.ds(pl.multiple_of(c * HALF + x * PART_X, 8), PART_X)
    copies = [push(o.at[mine], o.at[mine], at_x(d)) for d in range(1, NX)]
    for copy in copies:
        copy.wait_recv()
    copy = push(o.at[piece(c, HALF)], o.at[piece(c, HALF)], at_c)
    copy.wait_recv()

    for n, (p, q) in enumerate(TILES):
        tile = o[pl.ds(128 * n, 128), :]
        gram_ref[pl.ds(128 * p, 128), pl.ds(128 * q, 128)] = tile
        if p != q:
            gram_ref[pl.ds(128 * q, 128), pl.ds(128 * p, 128)] = tile.T
    for copy in started:
        copy.wait_send()


def gram_all(pb, code):
    copies = 2 * 3 + 1 + 3 + 3 + 7 + 3 + 3 + 1
    return pl.pallas_call(
        gram_kernel,
        out_shape=jax.ShapeDtypeStruct((RR, RR), F32),
        in_specs=[pl.BlockSpec(memory_space=pltpu.VMEM)] * 2,
        out_specs=pl.BlockSpec(memory_space=pltpu.VMEM),
        scratch_shapes=[
            pltpu.VMEM((NX, 4, BI // NX, RR), BF16),
            pltpu.VMEM((NX, 8, 128), F32),
            pltpu.VMEM((PACKED, 128), F32),
            pltpu.VMEM((PACKED, 128), F32),
            pltpu.VMEM((HALF, 128), F32),
            pltpu.VMEM((NX - 1, PART_X, 128), F32),
            pltpu.VMEM((NY - 1, PART_Y, 128), F32),
            pltpu.VMEM((NZ, PART_Y, 128), F32),
            pltpu.SemaphoreType.DMA((copies,)),
            pltpu.SemaphoreType.DMA((copies,)),
        ],
        compiler_params=pltpu.CompilerParams(
            collective_id=0, has_side_effects=True, vmem_limit_bytes=40 * 1024 * 1024
        ),
        name="gram_all",
    )(pb, code)


def orthonormal(matrix):
    inner = jnp.dot(matrix.T, matrix, precision=HIGHEST)
    lower_factor = jnp.linalg.cholesky(inner)
    return jax.scipy.linalg.solve_triangular(lower_factor, matrix.T, lower=True).T


def route_rows(global_id, per_owner, groups, capacity):
    owner_of = global_id // per_owner
    local_id = global_id % per_owner
    slot_range = jnp.arange(global_id.shape[0], dtype=jnp.int32)
    earlier = (owner_of[:, None] == owner_of[None, :]) & (slot_range[:, None] > slot_range[None, :])
    rank_in = jnp.sum(earlier.astype(jnp.int32), axis=1)
    chosen = (owner_of[:, None, None] == jnp.arange(groups, dtype=jnp.int32)[None, :, None]) & (
        rank_in[:, None, None] == jnp.arange(capacity, dtype=jnp.int32)[None, None, :]
    )
    request_table = jnp.sum(jnp.where(chosen, local_id[:, None, None], 0), axis=0)
    return (owner_of, rank_in, request_table)


def body(blocks, coords, counts, factor_b, factor_c, start):
    groups = lax.axis_size("blk")
    slots = blocks.shape[0]
    slab_b = factor_b.T.reshape(R2, -1, BJ).transpose(1, 0, 2)
    slab_c = factor_c.T.reshape(R3, -1, 2 * BK).transpose(1, 0, 2)
    owner_b, rank_b, request_b = route_rows(coords[1], slab_b.shape[0], groups, 2)
    owner_c, rank_c, request_c = route_rows(coords[2], 2 * slab_c.shape[0], groups, 2)
    request = jnp.concatenate([request_b, request_c], axis=1)
    asked = lax.all_to_all(request, "blk", split_axis=0, concat_axis=0, tiled=True)
    reply = jnp.concatenate([slab_b[asked[:, :2]], slab_c[asked[:, 2:] // 2]], axis=2)
    fetched = lax.all_to_all(reply, "blk", split_axis=0, concat_axis=0, tiled=True)
    picks = jnp.stack([owner_b, rank_b, owner_c, rank_c, coords[2] % 2, jnp.broadcast_to(counts, (slots,))])
    partial_rows, rounded = contract(blocks, picks, fetched)
    local_block = coords[0] % IB_DEV
    code = (local_block[:, None] * 32 + jnp.arange(32, dtype=jnp.int32)[None, :]).astype(F32)
    code = jnp.broadcast_to(code.reshape(1, 128), (8, 128))
    gram_matrix = gram_all(rounded, code)
    subspace = orthonormal(start)
    for iteration in range(ITERS):
        subspace = orthonormal(jnp.dot(gram_matrix, subspace, precision=HIGHEST))
    small_gram = jnp.dot(subspace.T, jnp.dot(gram_matrix, subspace, precision=HIGHEST), precision=HIGHEST)
    small_gram = 0.5 * (small_gram + small_gram.T)
    lower_factor = jnp.linalg.cholesky(small_gram)
    weights = jax.scipy.linalg.solve_triangular(lower_factor, subspace.T, lower=True)
    mapped = jnp.dot(weights, partial_rows.reshape(slots * BI, RR).T, precision=HIGHEST)
    rep = lax.axis_size("rep")
    sent = jnp.broadcast_to(mapped[None], (rep,) + mapped.shape)
    blocks_all = jnp.broadcast_to(local_block[None, :], (rep, slots))
    got = lax.all_to_all(sent, "rep", split_axis=0, concat_axis=0, tiled=True)
    got_blocks = lax.all_to_all(blocks_all, "rep", split_axis=0, concat_axis=0, tiled=True)
    wanted = lax.axis_index("rep") * (IB_DEV // rep) + jnp.arange(IB_DEV // rep, dtype=jnp.int32)
    place = (got_blocks.reshape(1, -1) == wanted[:, None]).astype(F32)
    terms = got.reshape(rep, R2, slots, BI)
    out = jnp.zeros((R2, IB_DEV // rep, BI), F32)
    for n in range(rep):
        for s in range(slots):
            out = out + terms[n, :, s][:, None, :] * place[:, n * slots + s][None, :, None]
    return out.reshape(R2, -1).T


def solution(mesh):
    return jax.shard_map(
        body,
        mesh=mesh,
        in_specs=(
            P(("blk", "rep"), None, None),
            P(None, ("blk", "rep")),
            P(("blk", "rep")),
            P("blk", None),
            P("blk", None),
            P(),
        ),
        out_specs=P(("blk", "rep"), None),
        check_vma=False,
    )
```

```python
import jax
import jax.numpy as jnp
from jax import lax
from jax.experimental import pallas as pl
from jax.experimental.pallas import tpu as pltpu
from jax.sharding import PartitionSpec as P

BI = 128
BJ = 128
BK = 64
R2 = 32
R3 = 16
RR = 512
IB_DEV = 32
ITERS = 4
NX = 4
NY = 4
NZ = 8
PACKED = 1280
HALF = PACKED // 2
PART_X = HALF // NX
PART_Y = PART_X // NY
F32 = jnp.float32
BF16 = jnp.bfloat16
TILES = [(a, b) for a in range(4) for b in range(a, 4)]


def dot_nt(left, right):
    return lax.dot_general(left, right, (((1,), (1,)), ((), ())), preferred_element_type=F32)


def dot_tn(left, right):
    return lax.dot_general(left, right, (((0,), (0,)), ((), ())), preferred_element_type=F32)


def iota(shape, dim):
    return lax.broadcasted_iota(jnp.int32, shape, dim)


def contract_kernel(pick_ref, x_ref, c_ref, b_ref, high_ref, low_ref):
    slot = pl.program_id(0)
    alive = (slot < pick_ref[5, 0]).astype(F32)
    odd = pick_ref[4, slot] > 0
    pair = c_ref[0, 0].astype(F32)
    mode_c = jnp.where(odd, pair[:, BK:], pair[:, :BK])
    wide = jnp.concatenate([mode_c] * 8, axis=1)
    tall = jnp.concatenate([wide] * 8, axis=0)
    fold_mask = iota((128, 512), 0) // R3 == iota((128, 512), 1) // BK
    fold_t = jnp.where(fold_mask, tall, 0.0).astype(BF16)
    spread_q = (iota((RR, R2), 0) // R3 == iota((RR, R2), 1)).astype(F32).astype(BF16)
    mode_b = jnp.dot(spread_q, b_ref[0, 0], preferred_element_type=F32).astype(BF16)
    keep = (iota((RR, 256), 0) % R3 == iota((RR, 256), 1) % R3).astype(F32)
    total = jnp.zeros((BI, RR), F32)
    for t in range(8):
        folded = jnp.concatenate(
            [
                dot_nt(x_ref[0, :, pl.ds((2 * t + h) * 512, 512)], fold_t).astype(BF16)
                for h in range(2)
            ],
            axis=1,
        )
        spread_j = (iota((BJ, 256), 0) == 16 * t + iota((BJ, 256), 1) // R3).astype(F32).astype(BF16)
        expanded = jnp.dot(mode_b, spread_j, preferred_element_type=F32) * keep
        total += dot_nt(folded, expanded.astype(BF16))
    total = total * alive
    high = total.astype(BF16)
    high_ref[0] = high
    low_ref[0] = (total - high.astype(F32)).astype(BF16)


def contract(blocks, picks, fetched):
    slots = blocks.shape[0]
    return pl.pallas_call(
        contract_kernel,
        grid_spec=pltpu.PrefetchScalarGridSpec(
            num_scalar_prefetch=1,
            grid=(slots,),
            in_specs=[
                pl.BlockSpec((1, BI, BJ * BK), lambda s, pick: (s, 0, 0)),
                pl.BlockSpec((1, 1, R3, 128), lambda s, pick: (pick[2, s], pick[3, s], 2, 0)),
                pl.BlockSpec((1, 1, R2, 128), lambda s, pick: (pick[0, s], pick[1, s], 0, 0)),
            ],
            out_specs=[
                pl.BlockSpec((1, BI, RR), lambda s, pick: (s, 0, 0)),
                pl.BlockSpec((1, BI, RR), lambda s, pick: (s, 0, 0)),
            ],
        ),
        out_shape=[
            jax.ShapeDtypeStruct((slots, BI, RR), BF16),
            jax.ShapeDtypeStruct((slots, BI, RR), BF16),
        ],
        compiler_params=pltpu.CompilerParams(vmem_limit_bytes=40 * 1024 * 1024),
        name="contract",
    )(picks, blocks, fetched, fetched)


def split(value):
    high = value.astype(BF16)
    rest = value - high.astype(F32)
    middle = rest.astype(BF16)
    low = (rest - middle.astype(F32)).astype(BF16)
    return high, middle, low


def inner_product(left, right):
    lh, lm, ll = split(left)
    rh, rm, rl = split(right)
    return dot_nt(
        jnp.concatenate([lh, lh, lm, lh, ll, lm], axis=1),
        jnp.concatenate([rh, rm, rh, rl, rh, rm], axis=1),
    )


def fine_dot(left, high, middle, low):
    lh, lm, ll = split(left)
    n = left.shape[0]
    first = jnp.dot(jnp.concatenate([lh, lm, ll], axis=0), high, preferred_element_type=F32)
    second = jnp.dot(jnp.concatenate([lh, lm], axis=0), middle, preferred_element_type=F32)
    third = jnp.dot(lh, low, preferred_element_type=F32)
    small = first[2 * n :] + second[n:] + third
    return first[:n] + (first[n : 2 * n] + second[:n] + small)


def inverse_lower(inner):
    n = inner.shape[0]
    unit = (iota((n, n), 0) == iota((n, n), 1)).astype(F32)
    work = jnp.concatenate([inner, unit], axis=1)
    row = iota((n, 1), 0)
    for k in range(n):
        scale = lax.rsqrt(work[k : k + 1, k : k + 1])
        pivot = work[k : k + 1, :] * scale
        column = jnp.where(row > k, work[:, k : k + 1] * scale, 0.0)
        work = jnp.where(row == k, pivot, work - column * pivot)
    return work[:, n:]


def orthonormal_t(value):
    return fine_dot(inverse_lower(inner_product(value, value)), *split(value))


def factor_kernel(
    pb_ref, low_ref, code_ref, start_ref, out_ref,
    rows, codes, g, o, from_c, from_x, from_y, from_z, gh, gm, gl, space, maps, send, recv,
):
    b = lax.axis_index("blk")
    x = lax.axis_index("rep")
    c = lax.rem(b, 2)
    y = lax.rem(b // 2, NY)
    z = b // (2 * NY)

    def at_x(d):
        return {"blk": b, "rep": lax.rem(x + d, NX)}

    def at_y(d):
        return {"blk": (z * NY + lax.rem(y + d, NY)) * 2 + c, "rep": x}

    def at_z(d):
        return {"blk": (lax.rem(z + d, NZ) * NY + y) * 2 + c, "rep": x}

    at_c = {"blk": b + 1 - 2 * c, "rep": x}
    partners = [at_x(d) for d in range(1, NX)] + [at_y(d) for d in range(1, NY)]
    partners += [at_z(d) for d in range(1, NZ)] + [at_c]
    barrier = pltpu.get_barrier_semaphore()
    for partner in partners:
        pl.semaphore_signal(barrier, inc=1, device_id=partner, device_id_type=pl.DeviceIdType.MESH)
    pl.semaphore_wait(barrier, len(partners))

    started = []

    def push(source, target, device):
        k = len(started)
        copy = pltpu.make_async_remote_copy(
            src_ref=source,
            dst_ref=target,
            send_sem=send.at[k],
            recv_sem=recv.at[k],
            device_id=device,
            device_id_type=pl.DeviceIdType.MESH,
        )
        copy.start()
        started.append(copy)
        return copy

    quarter = BI // NX

    def piece(n, count):
        return pl.ds(pl.multiple_of(n * count, 8), count)

    tags = [push(code_ref, codes.at[x], at_x(d)) for d in range(1, NX)]
    moves = [
        push(pb_ref.at[:, pl.ds(pl.multiple_of(lax.rem(x + d, NX) * quarter, quarter), quarter), :], rows.at[x], at_x(d))
        for d in range(1, NX)
    ]
    codes[x] = code_ref[...]
    rows[x] = pb_ref[:, pl.ds(pl.multiple_of(x * quarter, quarter), quarter), :]
    space[...] = orthonormal_t(start_ref[...])
    for copy in tags:
        copy.wait_recv()
    along = jnp.concatenate([codes[n][0:1, :] for n in range(NX)], axis=1)
    down = jnp.concatenate([codes[n].T[:, 0:1] for n in range(NX)], axis=0)
    same = (down == along).astype(F32).astype(BF16)
    for copy in moves:
        copy.wait_recv()
    held = rows[...].reshape(RR, RR)
    summed = jnp.dot(same, held, preferred_element_type=F32)
    high = summed.astype(BF16)
    low = (summed - high.astype(F32)).astype(BF16)
    at = 0
    for a in range(4):
        left = held[:, 128 * a : 128 * a + 128]
        strip = dot_tn(left, high[:, 128 * a :]) + dot_tn(left, low[:, 128 * a :])
        for n in range(4 - a):
            g[pl.ds(128 * at, 128), :] = strip[:, 128 * n : 128 * n + 128]
            at += 1

    base = c * HALF
    copy = push(g.at[piece(1 - c, HALF)], from_c, at_c)
    copy.wait_recv()
    g[piece(c, HALF), :] += from_c[...]

    copies = [
        push(g.at[pl.ds(pl.multiple_of(base + lax.rem(x + d, NX) * PART_X, 8), PART_X)], from_x.at[d - 1], at_x(d))
        for d in range(1, NX)
    ]
    for copy in copies:
        copy.wait_recv()
    base = base + x * PART_X
    mine = pl.ds(pl.multiple_of(base, 8), PART_X)
    g[mine, :] = g[mine, :] + from_x[0] + from_x[1] + from_x[2]

    copies = [
        push(g.at[pl.ds(pl.multiple_of(base + lax.rem(y + d, NY) * PART_Y, 8), PART_Y)], from_y.at[d - 1], at_y(d))
        for d in range(1, NY)
    ]
    for copy in copies:
        copy.wait_recv()
    base = base + y * PART_Y
    mine = pl.ds(pl.multiple_of(base, 8), PART_Y)
    from_z[z] = g[mine, :] + from_y[0] + from_y[1] + from_y[2]

    copies = [push(from_z.at[z], from_z.at[z], at_z(d)) for d in range(1, NZ)]
    for copy in copies:
        copy.wait_recv()
    total = from_z[0]
    for n in range(1, NZ):
        total = total + from_z[n]
    o[mine, :] = total

    copies = [push(o.at[mine], o.at[mine], at_y(d)) for d in range(1, NY)]
    for copy in copies:
        copy.wait_recv()
    mine = pl.ds(pl.multiple_of(c * HALF + x * PART_X, 8), PART_X)
    copies = [push(o.at[mine], o.at[mine], at_x(d)) for d in range(1, NX)]
    for copy in copies:
        copy.wait_recv()
    copy = push(o.at[piece(c, HALF)], o.at[piece(c, HALF)], at_c)
    copy.wait_recv()

    for n, (p, q) in enumerate(TILES):
        tile = o[pl.ds(128 * n, 128), :]
        for ref, part in zip((gh, gm, gl), split(tile)):
            ref[pl.ds(128 * p, 128), pl.ds(128 * q, 128)] = part
        if p != q:
            for ref, part in zip((gh, gm, gl), split(tile.T)):
                ref[pl.ds(128 * q, 128), pl.ds(128 * p, 128)] = part

    def step(n, carry):
        space[...] = orthonormal_t(fine_dot(space[...], gh[...], gm[...], gl[...]))
        return carry

    lax.fori_loop(0, ITERS, step, 0)
    last = space[...]
    small = inner_product(last, fine_dot(last, gh[...], gm[...], gl[...]))
    wide = fine_dot(inverse_lower(small), *split(last))
    wh, wm, _ = split(wide)
    high = pb_ref[...].reshape(RR, RR)
    low = low_ref[...].reshape(RR, RR)
    both = dot_nt(jnp.concatenate([wh, wm], axis=0), high)
    maps[x] = both[:R2] + (both[R2:] + dot_nt(wh, low))
    copies = [push(maps.at[x], maps.at[x], at_x(d)) for d in range(1, NX)]
    first = (x * (IB_DEV // NX)).astype(F32)
    for copy in copies:
        copy.wait_recv()
    outs = [jnp.zeros((R2, BI), F32) for _ in range(IB_DEV // NX)]
    for n in range(NX):
        for s in range(4):
            label = jnp.broadcast_to(codes[n][0:1, 32 * s : 32 * s + 1], (R2, BI)) * (1.0 / 32.0) - first
            term = maps[n, :, 128 * s : 128 * s + 128]
            for k in range(IB_DEV // NX):
                outs[k] = outs[k] + jnp.where(label == float(k), term, 0.0)
    for k in range(IB_DEV // NX):
        out_ref[:, 128 * k : 128 * k + 128] = outs[k]
    for copy in started:
        copy.wait_send()


def factor(pb, low, code, start_t):
    copies = 2 * 3 + 1 + 3 + 3 + 7 + 3 + 3 + 1 + 3
    return pl.pallas_call(
        factor_kernel,
        out_shape=jax.ShapeDtypeStruct((R2, IB_DEV * BI // NX), F32),
        in_specs=[pl.BlockSpec(memory_space=pltpu.VMEM)] * 4,
        out_specs=pl.BlockSpec(memory_space=pltpu.VMEM),
        scratch_shapes=[
            pltpu.VMEM((NX, 4, BI // NX, RR), BF16),
            pltpu.VMEM((NX, 8, 128), F32),
            pltpu.VMEM((PACKED, 128), F32),
            pltpu.VMEM((PACKED, 128), F32),
            pltpu.VMEM((HALF, 128), F32),
            pltpu.VMEM((NX - 1, PART_X, 128), F32),
            pltpu.VMEM((NY - 1, PART_Y, 128), F32),
            pltpu.VMEM((NZ, PART_Y, 128), F32),
            pltpu.VMEM((RR, RR), BF16),
            pltpu.VMEM((RR, RR), BF16),
            pltpu.VMEM((RR, RR), BF16),
            pltpu.VMEM((R2, RR), F32),
            pltpu.VMEM((NX, R2, RR), F32),
            pltpu.SemaphoreType.DMA((copies,)),
            pltpu.SemaphoreType.DMA((copies,)),
        ],
        compiler_params=pltpu.CompilerParams(
            collective_id=0, has_side_effects=True, vmem_limit_bytes=40 * 1024 * 1024
        ),
        name="factor",
    )(pb, low, code, start_t)


def route_rows(global_id, per_owner, groups, capacity):
    owner_of = global_id // per_owner
    local_id = global_id % per_owner
    slot_range = jnp.arange(global_id.shape[0], dtype=jnp.int32)
    earlier = (owner_of[:, None] == owner_of[None, :]) & (slot_range[:, None] > slot_range[None, :])
    rank_in = jnp.sum(earlier.astype(jnp.int32), axis=1)
    chosen = (owner_of[:, None, None] == jnp.arange(groups, dtype=jnp.int32)[None, :, None]) & (
        rank_in[:, None, None] == jnp.arange(capacity, dtype=jnp.int32)[None, None, :]
    )
    request_table = jnp.sum(jnp.where(chosen, local_id[:, None, None], 0), axis=0)
    return (owner_of, rank_in, request_table)


def body(blocks, coords, counts, factor_b, factor_c, start):
    groups = lax.axis_size("blk")
    slots = blocks.shape[0]
    slab_b = factor_b.T.reshape(R2, -1, BJ).transpose(1, 0, 2)
    slab_c = factor_c.T.reshape(R3, -1, 2 * BK).transpose(1, 0, 2)
    owner_b, rank_b, request_b = route_rows(coords[1], slab_b.shape[0], groups, 2)
    owner_c, rank_c, request_c = route_rows(coords[2], 2 * slab_c.shape[0], groups, 2)
    request = jnp.concatenate([request_b, request_c], axis=1)
    asked = lax.all_to_all(request, "blk", split_axis=0, concat_axis=0, tiled=True)
    reply = jnp.concatenate([slab_b[asked[:, :2]], slab_c[asked[:, 2:] // 2]], axis=2)
    fetched = lax.all_to_all(reply, "blk", split_axis=0, concat_axis=0, tiled=True)
    picks = jnp.stack([owner_b, rank_b, owner_c, rank_c, coords[2] % 2, jnp.broadcast_to(counts, (slots,))])
    high, low = contract(blocks, picks, fetched)
    local_block = coords[0] % IB_DEV
    code = (local_block[:, None] * 32 + jnp.arange(32, dtype=jnp.int32)[None, :]).astype(F32)
    code = jnp.broadcast_to(code.reshape(1, 128), (8, 128))
    return factor(high, low, code, start.T).T


def solution(mesh):
    return jax.shard_map(
        body,
        mesh=mesh,
        in_specs=(
            P(("blk", "rep"), None, None),
            P(None, ("blk", "rep")),
            P(("blk", "rep")),
            P("blk", None),
            P("blk", None),
            P(),
        ),
        out_specs=P(("blk", "rep"), None),
        check_vma=False,
    )
```

```python
import jax
import jax.numpy as jnp
from jax import lax
from jax.experimental import pallas as pl
from jax.experimental.pallas import tpu as pltpu
from jax.sharding import PartitionSpec as P

BI = 128
BJ = 128
BK = 64
R2 = 32
R3 = 16
RR = 512
IB_DEV = 32
NB = 4
ITERS = 4
NX = 4
NY = 4
NZ = 8
PACKED = 1280
HALF = PACKED // 2
PART_X = HALF // NX
PART_Y = PART_X // NY
F32 = jnp.float32
BF16 = jnp.bfloat16
TILES = [(a, b) for a in range(4) for b in range(a, 4)]


def dot_nt(left, right):
    return lax.dot_general(left, right, (((1,), (1,)), ((), ())), preferred_element_type=F32)


def dot_tn(left, right):
    return lax.dot_general(left, right, (((0,), (0,)), ((), ())), preferred_element_type=F32)


def iota(shape, dim):
    return lax.broadcasted_iota(jnp.int32, shape, dim)


def fold_slot(held_x, slot, pair, odd, folded):
    pair = pair.astype(F32)
    mode_c = pair[:, :BK] * (1.0 - odd) + pair[:, BK:] * odd
    wide = jnp.concatenate([mode_c] * 8, axis=1)
    tall = jnp.concatenate([wide] * 8, axis=0)
    fold_mask = iota((128, 512), 0) // R3 == iota((128, 512), 1) // BK
    fold_t = jnp.where(fold_mask, tall, 0.0).astype(BF16)
    for t in range(16):
        part = dot_nt(held_x[slot, :, 512 * t : 512 * t + 512], fold_t)
        folded[slot, :, 128 * t : 128 * t + 128] = part.astype(BF16)


def contract_slot(folded, slot, block_b, alive):
    spread_q = (iota((RR, R2), 0) // R3 == iota((RR, R2), 1)).astype(F32).astype(BF16)
    mode_b = jnp.dot(spread_q, block_b, preferred_element_type=F32).astype(BF16)
    keep = (iota((RR, 256), 0) % R3 == iota((RR, 256), 1) % R3).astype(F32)
    total = jnp.zeros((BI, RR), F32)
    for t in range(8):
        spread_j = (iota((BJ, 256), 0) == 16 * t + iota((BJ, 256), 1) // R3).astype(F32).astype(BF16)
        expanded = jnp.dot(mode_b, spread_j, preferred_element_type=F32) * keep
        total += dot_nt(folded[slot, :, 256 * t : 256 * t + 256], expanded.astype(BF16))
    return total * alive


def split(value):
    high = value.astype(BF16)
    rest = value - high.astype(F32)
    middle = rest.astype(BF16)
    low = (rest - middle.astype(F32)).astype(BF16)
    return high, middle, low


def inner_product(left, right):
    lh, lm, ll = split(left)
    rh, rm, rl = split(right)
    return dot_nt(
        jnp.concatenate([lh, lh, lm, lh, ll, lm], axis=1),
        jnp.concatenate([rh, rm, rh, rl, rh, rm], axis=1),
    )


def fine_dot(left, high, middle, low):
    lh, lm, ll = split(left)
    n = left.shape[0]
    first = jnp.dot(jnp.concatenate([lh, lm, ll], axis=0), high, preferred_element_type=F32)
    second = jnp.dot(jnp.concatenate([lh, lm], axis=0), middle, preferred_element_type=F32)
    third = jnp.dot(lh, low, preferred_element_type=F32)
    small = first[2 * n :] + second[n:] + third
    return first[:n] + (first[n : 2 * n] + second[:n] + small)


def inverse_lower(inner):
    n = inner.shape[0]
    unit = (iota((n, n), 0) == iota((n, n), 1)).astype(F32)
    work = jnp.concatenate([inner, unit], axis=1)
    row = iota((n, 1), 0)
    for k in range(n):
        scale = lax.rsqrt(work[k : k + 1, k : k + 1])
        pivot = work[k : k + 1, :] * scale
        column = jnp.where(row > k, work[:, k : k + 1] * scale, 0.0)
        work = jnp.where(row == k, pivot, work - column * pivot)
    return work[:, n:]


def orthonormal_t(value):
    return fine_dot(inverse_lower(inner_product(value, value)), *split(value))


def factor_kernel(
    blocks_ref, coords_ref, counts_ref, info_ref, fb_ref, fc_ref, start_ref, out_ref,
    held_x, plane_b, plane_c, infos, asked, give_b, give_c, got_b, got_c, folded, high_ref, low_ref,
    rows, codes, g, o, from_c, from_x, from_y, from_z, gh, gm, gl, space, maps, send, recv, load,
):
    b = lax.axis_index("blk")
    x = lax.axis_index("rep")
    c = lax.rem(b, 2)
    y = lax.rem(b // 2, NY)
    z = b // (2 * NY)

    def at_x(d):
        return {"blk": b, "rep": lax.rem(x + d, NX)}

    def at_y(d):
        return {"blk": (z * NY + lax.rem(y + d, NY)) * 2 + c, "rep": x}

    def at_z(d):
        return {"blk": (lax.rem(z + d, NZ) * NY + y) * 2 + c, "rep": x}

    at_c = {"blk": b + 1 - 2 * c, "rep": x}
    partners = [at_x(d) for d in range(1, NX)] + [at_y(d) for d in range(1, NY)]
    partners += [at_z(d) for d in range(1, NZ)] + [at_c]
    loads = [pltpu.make_async_copy(blocks_ref.at[s], held_x.at[s], load.at[s]) for s in range(NB)]
    for copy in loads:
        copy.start()
    barrier = pltpu.get_barrier_semaphore()
    for partner in partners:
        pl.semaphore_signal(barrier, inc=1, device_id=partner, device_id_type=pl.DeviceIdType.MESH)
    pl.semaphore_wait(barrier, len(partners))

    started = []

    def push(source, target, device):
        k = len(started)
        copy = pltpu.make_async_remote_copy(
            src_ref=source,
            dst_ref=target,
            send_sem=send.at[k],
            recv_sem=recv.at[k],
            device_id=device,
            device_id_type=pl.DeviceIdType.MESH,
        )
        copy.start()
        started.append(copy)
        return copy

    quarter = BI // NX

    def piece(n, count):
        return pl.ds(pl.multiple_of(n * count, 8), count)

    wishes = [push(info_ref, infos.at[z], at_z(d)) for d in range(1, NZ)]
    tags = [push(info_ref, codes.at[x], at_x(d)) for d in range(1, NX)]
    infos[z] = info_ref[...]
    codes[x] = info_ref[...]

    own = y * 2 + c
    planes = ((plane_c, 4), (plane_b, 16))

    def part(n, place):
        plane, count = planes[n]
        return plane.at[pl.ds(pl.multiple_of(place * count, count), count)]

    for n, ref in ((0, fc_ref), (1, fb_ref)):
        plane, count = planes[n]
        for k in range(count):
            plane[own * count + k] = ref[:, 128 * k : 128 * k + 128]
    along_y = [[push(part(n, own), part(n, own), at_y(d)) for d in range(1, NY)] for n in range(2)]
    across = [[push(part(n, own), part(n, own), at_c)] for n in range(2)]
    space[...] = orthonormal_t(start_ref[...])
    for copy in wishes:
        copy.wait_recv()
    copy = pltpu.make_async_copy(infos, asked, load.at[NB])
    copy.start()
    copy.wait()

    def relay(n):
        for d in range(1, NY):
            along_y[n][d - 1].wait_recv()
            place = lax.rem(y + NY - d, NY) * 2 + c
            across[n].append(push(part(n, place), part(n, place), at_c))
        for copy in across[n]:
            copy.wait_recv()

    relay(0)
    def answer(plane, mode, shift, mask, give, got):
        sent = []
        for d in range(NZ):
            t = lax.rem(z + d, NZ)
            for s in range(NB):
                block = plane[(asked[t, 1, NB * mode + s] >> shift) & mask]
                if d == 0:
                    got[z * NB + s] = block
                else:
                    give[d - 1, s] = block
            if d > 0:
                target = got.at[pl.ds(pl.multiple_of(z * NB, NB), NB)]
                sent.append(push(give.at[d - 1], target, at_z(d)))
        return sent

    sent_c = answer(plane_c, 1, 1, 31, give_c, got_c)
    relay(1)
    sent_b = answer(plane_b, 0, 0, 127, give_b, got_b)
    for copy in loads:
        copy.wait()
    for copy in sent_c:
        copy.wait_recv()

    def fold_step(s, carry):
        wish = coords_ref[2, s]
        fold_slot(held_x, s, got_c[(wish >> 6) * NB + s], (wish & 1).astype(F32), folded)
        return carry

    lax.fori_loop(0, NB, fold_step, 0)
    for copy in sent_b:
        copy.wait_recv()

    def contract_step(s, carry):
        alive = jnp.clip(counts_ref[0] - s, 0, 1).astype(F32)
        total = contract_slot(folded, s, got_b[(coords_ref[1, s] >> 7) * NB + s], alive)
        high = total.astype(BF16)
        high_ref[s] = high
        low_ref[s] = (total - high.astype(F32)).astype(BF16)
        return carry

    lax.fori_loop(0, NB, contract_step, 0)

    moves = [
        push(high_ref.at[:, pl.ds(pl.multiple_of(lax.rem(x + d, NX) * quarter, quarter), quarter), :], rows.at[x], at_x(d))
        for d in range(1, NX)
    ]
    rows[x] = high_ref[:, pl.ds(pl.multiple_of(x * quarter, quarter), quarter), :]
    for copy in tags:
        copy.wait_recv()
    labels = [codes[n].astype(F32) for n in range(NX)]
    along = jnp.concatenate([label[0:1, :] for label in labels], axis=1)
    down = jnp.concatenate([label.T[:, 0:1] for label in labels], axis=0)
    same = (down == along).astype(F32).astype(BF16)
    for copy in moves:
        copy.wait_recv()
    held = rows[...].reshape(RR, RR)
    summed = jnp.dot(same, held, preferred_element_type=F32)
    high = summed.astype(BF16)
    low = (summed - high.astype(F32)).astype(BF16)
    at = 0
    for a in range(4):
        left = held[:, 128 * a : 128 * a + 128]
        strip = dot_tn(left, high[:, 128 * a :]) + dot_tn(left, low[:, 128 * a :])
        for n in range(4 - a):
            g[pl.ds(128 * at, 128), :] = strip[:, 128 * n : 128 * n + 128]
            at += 1

    base = c * HALF
    copy = push(g.at[piece(1 - c, HALF)], from_c, at_c)
    copy.wait_recv()
    g[piece(c, HALF), :] += from_c[...]

    copies = [
        push(g.at[pl.ds(pl.multiple_of(base + lax.rem(x + d, NX) * PART_X, 8), PART_X)], from_x.at[d - 1], at_x(d))
        for d in range(1, NX)
    ]
    for copy in copies:
        copy.wait_recv()
    base = base + x * PART_X
    mine = pl.ds(pl.multiple_of(base, 8), PART_X)
    g[mine, :] = g[mine, :] + from_x[0] + from_x[1] + from_x[2]

    copies = [
        push(g.at[pl.ds(pl.multiple_of(base + lax.rem(y + d, NY) * PART_Y, 8), PART_Y)], from_y.at[d - 1], at_y(d))
        for d in range(1, NY)
    ]
    for copy in copies:
        copy.wait_recv()
    base = base + y * PART_Y
    mine = pl.ds(pl.multiple_of(base, 8), PART_Y)
    from_z[z] = g[mine, :] + from_y[0] + from_y[1] + from_y[2]

    copies = [push(from_z.at[z], from_z.at[z], at_z(d)) for d in range(1, NZ)]
    for copy in copies:
        copy.wait_recv()
    total = from_z[0]
    for n in range(1, NZ):
        total = total + from_z[n]
    o[mine, :] = total

    copies = [push(o.at[mine], o.at[mine], at_y(d)) for d in range(1, NY)]
    for copy in copies:
        copy.wait_recv()
    mine = pl.ds(pl.multiple_of(c * HALF + x * PART_X, 8), PART_X)
    copies = [push(o.at[mine], o.at[mine], at_x(d)) for d in range(1, NX)]
    for copy in copies:
        copy.wait_recv()
    copy = push(o.at[piece(c, HALF)], o.at[piece(c, HALF)], at_c)
    copy.wait_recv()

    for n, (p, q) in enumerate(TILES):
        tile = o[pl.ds(128 * n, 128), :]
        for ref, part in zip((gh, gm, gl), split(tile)):
            ref[pl.ds(128 * p, 128), pl.ds(128 * q, 128)] = part
        if p != q:
            for ref, part in zip((gh, gm, gl), split(tile.T)):
                ref[pl.ds(128 * q, 128), pl.ds(128 * p, 128)] = part

    def step(n, carry):
        space[...] = orthonormal_t(fine_dot(space[...], gh[...], gm[...], gl[...]))
        return carry

    lax.fori_loop(0, ITERS, step, 0)
    last = space[...]
    small = inner_product(last, fine_dot(last, gh[...], gm[...], gl[...]))
    wide = fine_dot(inverse_lower(small), *split(last))
    wh, wm, _ = split(wide)
    high = high_ref[...].reshape(RR, RR)
    low = low_ref[...].reshape(RR, RR)
    both = dot_nt(jnp.concatenate([wh, wm], axis=0), high)
    maps[x] = both[:R2] + (both[R2:] + dot_nt(wh, low))
    copies = [push(maps.at[x], maps.at[x], at_x(d)) for d in range(1, NX)]
    first = (x * (IB_DEV // NX)).astype(F32)
    for copy in copies:
        copy.wait_recv()
    outs = [jnp.zeros((R2, BI), F32) for _ in range(IB_DEV // NX)]
    for n in range(NX):
        for s in range(NB):
            label = jnp.broadcast_to(labels[n][0:1, 32 * s : 32 * s + 1], (R2, BI)) * (1.0 / 32.0) - first
            term = maps[n, :, 128 * s : 128 * s + 128]
            for k in range(IB_DEV // NX):
                outs[k] = outs[k] + jnp.where(label == float(k), term, 0.0)
    for k in range(IB_DEV // NX):
        out_ref[:, 128 * k : 128 * k + 128] = outs[k]
    for copy in started:
        copy.wait_send()


def factor(blocks, coords, counts, info, slab_b, slab_c, start_t):
    copies = 65
    vmem = pl.BlockSpec(memory_space=pltpu.VMEM)
    smem = pl.BlockSpec(memory_space=pltpu.SMEM)
    hbm = pl.BlockSpec(memory_space=pltpu.HBM)
    return pl.pallas_call(
        factor_kernel,
        out_shape=jax.ShapeDtypeStruct((R2, IB_DEV * BI // NX), F32),
        in_specs=[hbm, smem, smem, vmem, vmem, vmem, vmem],
        out_specs=vmem,
        scratch_shapes=[
            pltpu.VMEM((NB, BI, BJ * BK), BF16),
            pltpu.VMEM((2 * NY * 16, R2, BJ), BF16),
            pltpu.VMEM((2 * NY * 4, R3, 2 * BK), BF16),
            pltpu.VMEM((NZ, 8, 128), jnp.int32),
            pltpu.SMEM((NZ, 8, 128), jnp.int32),
            pltpu.VMEM((NZ - 1, NB, R2, BJ), BF16),
            pltpu.VMEM((NZ - 1, NB, R3, 2 * BK), BF16),
            pltpu.VMEM((NZ * NB, R2, BJ), BF16),
            pltpu.VMEM((NZ * NB, R3, 2 * BK), BF16),
            pltpu.VMEM((NB, BI, BJ * R3), BF16),
            pltpu.VMEM((NB, BI, RR), BF16),
            pltpu.VMEM((NB, BI, RR), BF16),
            pltpu.VMEM((NX, NB, BI // NX, RR), BF16),
            pltpu.VMEM((NX, 8, 128), jnp.int32),
            pltpu.VMEM((PACKED, 128), F32),
            pltpu.VMEM((PACKED, 128), F32),
            pltpu.VMEM((HALF, 128), F32),
            pltpu.VMEM((NX - 1, PART_X, 128), F32),
            pltpu.VMEM((NY - 1, PART_Y, 128), F32),
            pltpu.VMEM((NZ, PART_Y, 128), F32),
            pltpu.VMEM((RR, RR), BF16),
            pltpu.VMEM((RR, RR), BF16),
            pltpu.VMEM((RR, RR), BF16),
            pltpu.VMEM((R2, RR), F32),
            pltpu.VMEM((NX, R2, RR), F32),
            pltpu.SemaphoreType.DMA((copies,)),
            pltpu.SemaphoreType.DMA((copies,)),
            pltpu.SemaphoreType.DMA((NB + 1,)),
        ],
        compiler_params=pltpu.CompilerParams(
            collective_id=0, has_side_effects=True, vmem_limit_bytes=48 * 1024 * 1024
        ),
        name="factor",
    )(blocks, coords, counts, info, slab_b, slab_c, start_t)


def body(blocks, coords, counts, factor_b, factor_c, start):
    code = ((coords[0] % IB_DEV)[:, None] * 32 + jnp.arange(32, dtype=jnp.int32)[None, :]).reshape(1, 128)
    asks = jnp.pad(coords[1:].reshape(1, 2 * NB), ((0, 6), (0, 128 - 2 * NB)))
    info = jnp.concatenate([code, asks], axis=0)
    return factor(blocks, coords, counts, info, factor_b.T, factor_c.T, start.T).T


def solution(mesh):
    return jax.shard_map(
        body,
        mesh=mesh,
        in_specs=(
            P(("blk", "rep"), None, None),
            P(None, ("blk", "rep")),
            P(("blk", "rep")),
            P("blk", None),
            P("blk", None),
            P(),
        ),
        out_specs=P(("blk", "rep"), None),
        check_vma=False,
    )
```

```python
import jax
import jax.numpy as jnp
from jax import lax
from jax.experimental import pallas as pl
from jax.experimental.pallas import tpu as pltpu
from jax.sharding import PartitionSpec as P

BI = 128
BJ = 128
BK = 64
R2 = 32
R3 = 16
RR = 512
IB_DEV = 32
NB = 4
ITERS = 4
NX = 4
NY = 4
NZ = 8
PACKED = 1280
HALF = PACKED // 2
PART_0 = 384
PART_1 = HALF - PART_0
F32 = jnp.float32
BF16 = jnp.bfloat16
TILES = [(a, b) for a in range(4) for b in range(a, 4)]


def dot_nt(left, right):
    return lax.dot_general(left, right, (((1,), (1,)), ((), ())), preferred_element_type=F32)


def dot_tn(left, right):
    return lax.dot_general(left, right, (((0,), (0,)), ((), ())), preferred_element_type=F32)


def iota(shape, dim):
    return lax.broadcasted_iota(jnp.int32, shape, dim)


def fold_slot(held_x, slot, pair, odd, folded):
    pair = pair.astype(F32)
    mode_c = pair[:, :BK] * (1.0 - odd) + pair[:, BK:] * odd
    wide = jnp.concatenate([mode_c] * 8, axis=1)
    tall = jnp.concatenate([wide] * 8, axis=0)
    fold_mask = iota((128, 512), 0) // R3 == iota((128, 512), 1) // BK
    fold_t = jnp.where(fold_mask, tall, 0.0).astype(BF16)
    for t in range(16):
        part = dot_nt(held_x[slot, :, 512 * t : 512 * t + 512], fold_t)
        folded[slot, :, 128 * t : 128 * t + 128] = part.astype(BF16)


def contract_slot(folded, slot, block_b, alive):
    spread_q = (iota((RR, R2), 0) // R3 == iota((RR, R2), 1)).astype(F32).astype(BF16)
    mode_b = jnp.dot(spread_q, block_b, preferred_element_type=F32).astype(BF16)
    keep = (iota((RR, 256), 0) % R3 == iota((RR, 256), 1) % R3).astype(F32)
    total = jnp.zeros((BI, RR), F32)
    for t in range(8):
        spread_j = (iota((BJ, 256), 0) == 16 * t + iota((BJ, 256), 1) // R3).astype(F32).astype(BF16)
        expanded = jnp.dot(mode_b, spread_j, preferred_element_type=F32) * keep
        total += dot_nt(folded[slot, :, 256 * t : 256 * t + 256], expanded.astype(BF16))
    return total * alive


def split(value):
    high = value.astype(BF16)
    rest = value - high.astype(F32)
    middle = rest.astype(BF16)
    low = (rest - middle.astype(F32)).astype(BF16)
    return high, middle, low


def inner_product(left, right):
    lh, lm, ll = split(left)
    rh, rm, rl = split(right)
    return dot_nt(
        jnp.concatenate([lh, lh, lm, lh, ll, lm], axis=1),
        jnp.concatenate([rh, rm, rh, rl, rh, rm], axis=1),
    )


def fine_dot(left, high, middle, low):
    lh, lm, ll = split(left)
    n = left.shape[0]
    first = jnp.dot(jnp.concatenate([lh, lm, ll], axis=0), high, preferred_element_type=F32)
    second = jnp.dot(jnp.concatenate([lh, lm], axis=0), middle, preferred_element_type=F32)
    third = jnp.dot(lh, low, preferred_element_type=F32)
    small = first[2 * n :] + second[n:] + third
    return first[:n] + (first[n : 2 * n] + second[:n] + small)


def inverse_lower(inner):
    n = inner.shape[0]
    unit = (iota((n, n), 0) == iota((n, n), 1)).astype(F32)
    work = jnp.concatenate([inner, unit], axis=1)
    row = iota((n, 2 * n), 0)
    for k in range(0, n, 4):
        columns = [jnp.broadcast_to(work[:, k + t : k + t + 1], (n, 2 * n)) for t in range(4)]
        for t in range(4):
            at = k + t
            inverse = 1.0 / columns[t][at : at + 1]
            for u in range(t + 1, 4):
                columns[u] = columns[u] - columns[t] * (columns[u][at : at + 1] * inverse)
            work = work - jnp.where(row > at, columns[t], 0.0) * (work[at : at + 1] * inverse)
    diagonal = jnp.sum(work[:, :n] * unit, axis=1, keepdims=True)
    return work[:, n:] * lax.rsqrt(diagonal)


def orthonormal_t(value):
    return fine_dot(inverse_lower(inner_product(value, value)), *split(value))


def factor_kernel(
    blocks_ref, coords_hbm, counts_hbm, fb_hbm, fc_hbm, start_hbm, out_ref,
    coords_ref, counts_ref, info_ref, fb_ref, fc_ref, start_ref,
    held_x, plane_b, plane_c, infos, asked, give_b, give_c, got_b, got_c, folded, high_ref, low_ref,
    rows, codes, g, o, from_c, from_u0, from_u1, from_v0, from_v1, from_z, gh, gm, gl, space, maps, far, send, recv, load, feed,
):
    b = lax.axis_index("blk")
    x = lax.axis_index("rep")
    c = lax.rem(b, 2)
    y = lax.rem(b // 2, NY)
    z = b // (2 * NY)

    def at_x(d):
        return {"blk": b, "rep": lax.rem(x + d, NX)}

    def at_y(d):
        return {"blk": (z * NY + lax.rem(y + d, NY)) * 2 + c, "rep": x}

    def at_z(d):
        return {"blk": (lax.rem(z + d, NZ) * NY + y) * 2 + c, "rep": x}

    at_c = {"blk": b + 1 - 2 * c, "rep": x}
    partners = [at_x(d) for d in range(1, NX)] + [at_y(d) for d in range(1, NY)]
    partners += [at_z(d) for d in range(1, NZ)] + [at_c]
    loads = [pltpu.make_async_copy(blocks_ref.at[s], held_x.at[s], load.at[s]) for s in range(NB)]
    inputs = (
        (coords_hbm, coords_ref), (counts_hbm, counts_ref), (fc_hbm, fc_ref), (fb_hbm, fb_ref), (start_hbm, start_ref),
    )
    feeds = [pltpu.make_async_copy(a, b, feed.at[n]) for n, (a, b) in enumerate(inputs)]
    for copy in feeds + loads:
        copy.start()
    barrier = pltpu.get_barrier_semaphore()
    for partner in partners:
        pl.semaphore_signal(barrier, inc=1, device_id=partner, device_id_type=pl.DeviceIdType.MESH)
    pl.semaphore_wait(barrier, len(partners))

    started = []

    def push(source, target, device):
        k = len(started)
        copy = pltpu.make_async_remote_copy(
            src_ref=source,
            dst_ref=target,
            send_sem=send.at[k],
            recv_sem=recv.at[k],
            device_id=device,
            device_id_type=pl.DeviceIdType.MESH,
        )
        copy.start()
        started.append(copy)
        return copy

    quarter = BI // NX

    feeds[0].wait()
    feeds[1].wait()
    lane = iota((8, 128), 1)
    label_row = lane & 31
    asks = jnp.zeros((8, 128), jnp.int32)
    for s in range(NB):
        label_row += jnp.where(lane >> 5 == s, (coords_ref[0, s] & (IB_DEV - 1)) * 32, 0)
        asks += jnp.where(lane == s, coords_ref[1, s], 0) + jnp.where(lane == NB + s, coords_ref[2, s], 0)
    level = iota((8, 128), 0)
    info_ref[...] = jnp.where(level == 0, label_row, jnp.where(level == 1, asks, 0))

    wishes = [push(info_ref, infos.at[z], at_z(d)) for d in range(1, NZ)]
    tags = [push(info_ref, codes.at[x], at_x(d)) for d in range(1, NX)]
    infos[z] = info_ref[...]
    codes[x] = info_ref[...]

    own = y * 2 + c
    planes = ((plane_c, 4), (plane_b, 16))

    def part(n, place):
        plane, count = planes[n]
        return plane.at[pl.ds(pl.multiple_of(place * count, count), count)]

    along_y, across = [], []
    for n, ref in ((0, fc_ref), (1, fb_ref)):
        plane, count = planes[n]
        feeds[2 + n].wait()
        for k in range(count):
            plane[own * count + k] = ref[:, 128 * k : 128 * k + 128]
        along_y.append([push(part(n, own), part(n, own), at_y(d)) for d in (2, 1, 3)])
        across.append([push(part(n, own), part(n, own), at_c)])
    feeds[4].wait()
    space[...] = orthonormal_t(start_ref[...])
    for copy in wishes:
        copy.wait_recv()
    copy = pltpu.make_async_copy(infos, asked, load.at[NB])
    copy.start()
    copy.wait()

    def relay(n):
        for k, d in ((1, 1), (2, 3), (0, 2)):
            along_y[n][k].wait_recv()
            place = lax.rem(y + NY - d, NY) * 2 + c
            across[n].append(push(part(n, place), part(n, place), at_c))
        for copy in across[n]:
            copy.wait_recv()

    relay(0)
    def answer(plane, mode, shift, mask, give, got):
        sent = []
        for d in range(NZ):
            t = lax.rem(z + d, NZ)
            for s in range(NB):
                block = plane[(asked[t, 1, NB * mode + s] >> shift) & mask]
                if d == 0:
                    got[z * NB + s] = block
                else:
                    give[d - 1, s] = block
            if d > 0:
                target = got.at[pl.ds(pl.multiple_of(z * NB, NB), NB)]
                sent.append(push(give.at[d - 1], target, at_z(d)))
        return sent

    sent_c = answer(plane_c, 1, 1, 31, give_c, got_c)
    relay(1)
    sent_b = answer(plane_b, 0, 0, 127, give_b, got_b)
    for copy in loads:
        copy.wait()
    for copy in sent_c:
        copy.wait_recv()

    def fold_step(s, carry):
        wish = coords_ref[2, s]
        fold_slot(held_x, s, got_c[(wish >> 6) * NB + s], (wish & 1).astype(F32), folded)
        return carry

    lax.fori_loop(0, NB, fold_step, 0)
    for copy in sent_b:
        copy.wait_recv()

    moves = []
    for s in range(NB):
        alive = jnp.clip(counts_ref[0] - s, 0, 1).astype(F32)
        total = contract_slot(folded, s, got_b[(coords_ref[1, s] >> 7) * NB + s], alive)
        high = total.astype(BF16)
        high_ref[s] = high
        for d in (2, 1, 3):
            there = pl.ds(pl.multiple_of(lax.rem(x + d, NX) * quarter, quarter), quarter)
            moves.append(push(high_ref.at[s, there, :], rows.at[x, s], at_x(d)))
        low_ref[s] = (total - high.astype(F32)).astype(BF16)
    rows[x] = high_ref[:, pl.ds(pl.multiple_of(x * quarter, quarter), quarter), :]
    for copy in tags:
        copy.wait_recv()
    labels = [codes[n].astype(F32) for n in range(NX)]
    along = jnp.concatenate([label[0:1, :] for label in labels], axis=1)
    down = jnp.concatenate([label.T[:, 0:1] for label in labels], axis=0)
    same = (down == along).astype(F32).astype(BF16)
    for copy in moves:
        copy.wait_recv()
    held = rows[...].reshape(RR, RR)
    summed = jnp.dot(same, held, preferred_element_type=F32)
    high = summed.astype(BF16)
    low = (summed - high.astype(F32)).astype(BF16)
    at = 0
    for a in range(4):
        left = held[:, 128 * a : 128 * a + 128]
        strip = dot_tn(left, high[:, 128 * a :]) + dot_tn(left, low[:, 128 * a :])
        for n in range(4 - a):
            g[pl.ds(128 * at, 128), :] = strip[:, 128 * n : 128 * n + 128]
            at += 1

    parts = ((0, PART_0, x, y, at_x, at_y, from_u0, from_v0), (PART_0, PART_1, y, x, at_y, at_x, from_u1, from_v1))

    def span(start, count):
        return pl.ds(pl.multiple_of(start, 8), count)

    def chunk(n, core, d):
        off, count, mu = parts[n][:3]
        return span(core * HALF + off + lax.rem(mu + d, 4) * (count // 4), count // 4)

    pieces = [(n, d) for d in (2, 1, 3, 0) for n in range(2)]
    crossed = [push(g.at[chunk(n, 1 - c, d)], from_c.at[chunk(n, 0, d)], at_c) for n, d in pieces]
    outgoing = [[], []]
    for copy, (n, d) in zip(crossed, pieces):
        copy.wait_recv()
        here = chunk(n, c, d)
        g[here, :] += from_c[chunk(n, 0, d), :]
        if d > 0:
            outgoing[n].append(push(g.at[here], parts[n][6].at[d - 1], parts[n][4](d)))

    def small(n, d):
        off, count, mu, mv = parts[n][:4]
        return span(c * HALF + off + mu * (count // 4) + lax.rem(mv + d, 4) * (count // 16), count // 16)

    second = [[], []]
    for n in range(2):
        for copy in outgoing[n]:
            copy.wait_recv()
        here = chunk(n, c, 0)
        got = parts[n][6]
        g[here, :] = g[here, :] + got[0] + got[1] + got[2]
        second[n] = [push(g.at[small(n, d)], parts[n][7].at[d - 1], parts[n][5](d)) for d in (2, 1, 3)]
    for n in range(2):
        for copy in second[n]:
            copy.wait_recv()
        got = parts[n][7]
        at = 0 if n == 0 else PART_0 // 16
        from_z[z, at : at + parts[n][1] // 16, :] = g[small(n, 0), :] + got[0] + got[1] + got[2]
    copies = [push(from_z.at[z], from_z.at[z], at_z(d)) for d in (4, 3, 5, 2, 6, 1, 7)]
    for copy in copies:
        copy.wait_recv()
    total = from_z[0]
    for n in range(1, NZ):
        total = total + from_z[n]

    back = [[], []]
    for n in range(2):
        at = 0 if n == 0 else PART_0 // 16
        here = small(n, 0)
        o[here, :] = total[at : at + parts[n][1] // 16]
        back[n] = [push(o.at[here], o.at[here], parts[n][5](d)) for d in (2, 1, 3)]
    wide_back = [[], []]
    relayed = []
    for n in range(2):
        for copy in back[n]:
            copy.wait_recv()
        here = chunk(n, c, 0)
        wide_back[n] = [push(o.at[here], o.at[here], parts[n][4](d)) for d in (2, 1, 3)]
        relayed.append(push(o.at[here], o.at[here], at_c))
    for k, d in ((1, 1), (2, 3), (0, 2)):
        for n in range(2):
            wide_back[n][k].wait_recv()
            here = chunk(n, c, 4 - d)
            relayed.append(push(o.at[here], o.at[here], at_c))
    for copy in relayed:
        copy.wait_recv()

    for n, (p, q) in enumerate(TILES):
        tile = o[pl.ds(128 * n, 128), :]
        for ref, part in zip((gh, gm, gl), split(tile)):
            ref[pl.ds(128 * p, 128), pl.ds(128 * q, 128)] = part
        if p != q:
            for ref, part in zip((gh, gm, gl), split(tile.T)):
                ref[pl.ds(128 * q, 128), pl.ds(128 * p, 128)] = part

    def step(n, carry):
        space[...] = orthonormal_t(fine_dot(space[...], gh[...], gm[...], gl[...]))
        return carry

    lax.fori_loop(0, ITERS, step, 0)
    last = space[...]
    small = inner_product(last, fine_dot(last, gh[...], gm[...], gl[...]))
    wide = fine_dot(inverse_lower(small), *split(last))
    wh, wm, _ = split(wide)
    high = high_ref[...].reshape(RR, RR)
    low = low_ref[...].reshape(RR, RR)
    both = dot_nt(jnp.concatenate([wh, wm], axis=0), high)
    mapped = both[:R2] + (both[R2:] + dot_nt(wh, low))
    maps[x] = mapped
    far[0] = mapped.astype(BF16)
    copies = [push(far.at[0], far.at[d], at_x(d)) for d in range(1, NX)]
    first = (x * (IB_DEV // NX)).astype(F32)
    for d in range(1, NX):
        copies[d - 1].wait_recv()
        maps[lax.rem(x + NX - d, NX)] = far[d].astype(F32)
    outs = [jnp.zeros((R2, BI), F32) for _ in range(IB_DEV // NX)]
    for n in range(NX):
        for s in range(NB):
            label = jnp.broadcast_to(labels[n][0:1, 32 * s : 32 * s + 1], (R2, BI)) * (1.0 / 32.0) - first
            term = maps[n, :, 128 * s : 128 * s + 128]
            for k in range(IB_DEV // NX):
                outs[k] = outs[k] + jnp.where(label == float(k), term, 0.0)
    for k in range(IB_DEV // NX):
        out_ref[:, 128 * k : 128 * k + 128] = outs[k]
    for copy in started:
        copy.wait_send()


def factor(blocks, coords, counts, slab_b, slab_c, start_t):
    copies = 100
    vmem = pl.BlockSpec(memory_space=pltpu.VMEM)
    hbm = pl.BlockSpec(memory_space=pltpu.HBM)
    return pl.pallas_call(
        factor_kernel,
        out_shape=jax.ShapeDtypeStruct((R2, IB_DEV * BI // NX), F32),
        in_specs=[hbm] * 6,
        out_specs=vmem,
        scratch_shapes=[
            pltpu.SMEM(coords.shape, jnp.int32),
            pltpu.SMEM(counts.shape, jnp.int32),
            pltpu.VMEM((8, 128), jnp.int32),
            pltpu.VMEM(slab_b.shape, BF16),
            pltpu.VMEM(slab_c.shape, BF16),
            pltpu.VMEM(start_t.shape, F32),
            pltpu.VMEM((NB, BI, BJ * BK), BF16),
            pltpu.VMEM((2 * NY * 16, R2, BJ), BF16),
            pltpu.VMEM((2 * NY * 4, R3, 2 * BK), BF16),
            pltpu.VMEM((NZ, 8, 128), jnp.int32),
            pltpu.SMEM((NZ, 8, 128), jnp.int32),
            pltpu.VMEM((NZ - 1, NB, R2, BJ), BF16),
            pltpu.VMEM((NZ - 1, NB, R3, 2 * BK), BF16),
            pltpu.VMEM((NZ * NB, R2, BJ), BF16),
            pltpu.VMEM((NZ * NB, R3, 2 * BK), BF16),
            pltpu.VMEM((NB, BI, BJ * R3), BF16),
            pltpu.VMEM((NB, BI, RR), BF16),
            pltpu.VMEM((NB, BI, RR), BF16),
            pltpu.VMEM((NX, NB, BI // NX, RR), BF16),
            pltpu.VMEM((NX, 8, 128), jnp.int32),
            pltpu.VMEM((PACKED, 128), F32),
            pltpu.VMEM((PACKED, 128), F32),
            pltpu.VMEM((HALF, 128), F32),
            pltpu.VMEM((3, PART_0 // 4, 128), F32),
            pltpu.VMEM((3, PART_1 // 4, 128), F32),
            pltpu.VMEM((3, PART_0 // 16, 128), F32),
            pltpu.VMEM((3, PART_1 // 16, 128), F32),
            pltpu.VMEM((NZ, HALF // 16, 128), F32),
            pltpu.VMEM((RR, RR), BF16),
            pltpu.VMEM((RR, RR), BF16),
            pltpu.VMEM((RR, RR), BF16),
            pltpu.VMEM((R2, RR), F32),
            pltpu.VMEM((NX, R2, RR), F32),
            pltpu.VMEM((NX, R2, RR), BF16),
            pltpu.SemaphoreType.DMA((copies,)),
            pltpu.SemaphoreType.DMA((copies,)),
            pltpu.SemaphoreType.DMA((NB + 1,)),
            pltpu.SemaphoreType.DMA((5,)),
        ],
        compiler_params=pltpu.CompilerParams(
            collective_id=0, has_side_effects=True, vmem_limit_bytes=60 * 1024 * 1024
        ),
        name="factor",
    )(blocks, coords, counts, slab_b, slab_c, start_t)


def body(blocks, coords, counts, factor_b, factor_c, start):
    return factor(blocks, coords, counts, factor_b.T, factor_c.T, start.T).T


def solution(mesh):
    return jax.shard_map(
        body,
        mesh=mesh,
        in_specs=(
            P(("blk", "rep"), None, None),
            P(None, ("blk", "rep")),
            P(("blk", "rep")),
            P("blk", None),
            P("blk", None),
            P(),
        ),
        out_specs=P(("blk", "rep"), None),
        check_vma=False,
    )
```

```python
import jax
import jax.numpy as jnp
from jax import lax
from jax.experimental import pallas as pl
from jax.experimental.pallas import tpu as pltpu
from jax.sharding import PartitionSpec as P

BI = 128
BJ = 128
BK = 64
R2 = 32
R3 = 16
RR = 512
IB_DEV = 32
NB = 4
ITERS = 4
NX = 4
NY = 4
NZ = 8
PACKED = 1280
HALF = PACKED // 2
PART_0 = 384
PART_1 = HALF - PART_0
F32 = jnp.float32
BF16 = jnp.bfloat16
TILES = [(a, b) for a in range(4) for b in range(a, 4)]


def dot_nt(left, right):
    return lax.dot_general(left, right, (((1,), (1,)), ((), ())), preferred_element_type=F32)


def dot_tn(left, right):
    return lax.dot_general(left, right, (((0,), (0,)), ((), ())), preferred_element_type=F32)


def iota(shape, dim):
    return lax.broadcasted_iota(jnp.int32, shape, dim)


def fold_slot(held_x, slot, pair, odd, folded):
    pair = pair.astype(F32)
    mode_c = (pair[:, :BK] * (1.0 - odd) + pair[:, BK:] * odd).astype(BF16)
    spread = (iota((128, R3), 0) // 8 == iota((128, R3), 1)).astype(F32).astype(BF16)
    tall = jnp.dot(spread, mode_c, preferred_element_type=F32)
    wide = jnp.concatenate([tall] * 8, axis=1)
    fold_mask = iota((128, 512), 0) % 8 == iota((128, 512), 1) // BK
    fold_t = jnp.where(fold_mask, wide, 0.0).astype(BF16)
    for t in range(8):
        halves = [dot_nt(fold_t, held_x[slot, :, 512 * h : 512 * h + 512]) for h in (2 * t, 2 * t + 1)]
        part = jnp.concatenate([half.reshape(R3, 8, BI) for half in halves], axis=1)
        folded[slot, :, 16 * t : 16 * t + 16, :] = part.astype(BF16)


def contract_slot(folded, slot, block_b, alive):
    none = jnp.zeros((R2, BJ), BF16)
    two = jnp.concatenate(
        [jnp.concatenate([block_b, none], axis=1), jnp.concatenate([none, block_b], axis=1)], axis=0
    )
    parts = [
        jnp.dot(two, folded[slot, 2 * t : 2 * t + 2].reshape(2 * BJ, BI), preferred_element_type=F32)
        for t in range(R3 // 2)
    ]
    return jnp.concatenate(parts, axis=0) * alive


def split(value):
    high = value.astype(BF16)
    rest = value - high.astype(F32)
    middle = rest.astype(BF16)
    low = (rest - middle.astype(F32)).astype(BF16)
    return high, middle, low


def inner_product(left, right):
    lh, lm, ll = split(left)
    rh, rm, rl = split(right)
    return dot_nt(
        jnp.concatenate([lh, lh, lm, lh, ll, lm], axis=1),
        jnp.concatenate([rh, rm, rh, rl, rh, rm], axis=1),
    )


def fine_dot(left, high, middle, low):
    lh, lm, ll = split(left)
    n = left.shape[0]
    first = jnp.dot(jnp.concatenate([lh, lm, ll], axis=0), high, preferred_element_type=F32)
    second = jnp.dot(jnp.concatenate([lh, lm], axis=0), middle, preferred_element_type=F32)
    third = jnp.dot(lh, low, preferred_element_type=F32)
    small = first[2 * n :] + second[n:] + third
    return first[:n] + (first[n : 2 * n] + second[:n] + small)


def inverse_lower(inner):
    n = inner.shape[0]
    unit = (iota((n, n), 0) == iota((n, n), 1)).astype(F32)
    work = jnp.concatenate([inner, unit], axis=1)
    row = iota((n, 2 * n), 0)
    for k in range(0, n, 4):
        columns = [jnp.broadcast_to(work[:, k + t : k + t + 1], (n, 2 * n)) for t in range(4)]
        for t in range(4):
            at = k + t
            inverse = 1.0 / columns[t][at : at + 1]
            for u in range(t + 1, 4):
                columns[u] = columns[u] - columns[t] * (columns[u][at : at + 1] * inverse)
            work = work - jnp.where(row > at, columns[t], 0.0) * (work[at : at + 1] * inverse)
    diagonal = jnp.sum(work[:, :n] * unit, axis=1, keepdims=True)
    return work[:, n:] * lax.rsqrt(diagonal)


def orthonormal_t(value):
    return fine_dot(inverse_lower(inner_product(value, value)), *split(value))


def factor_kernel(
    blocks_ref, coords_hbm, counts_hbm, fb_hbm, fc_hbm, start_hbm, out_ref,
    coords_ref, counts_ref, info_ref, fb_ref, fc_ref, start_ref,
    held_x, plane_b, plane_c, infos, asked, give_b, give_c, got_b, got_c, folded, high_ref, turned_high, turned_low,
    rows, codes, g, o, from_c, from_u0, from_u1, from_v0, from_v1, from_z, gh, gm, gl, space, maps, far, send, recv, load, feed,
):
    b = lax.axis_index("blk")
    x = lax.axis_index("rep")
    c = lax.rem(b, 2)
    y = lax.rem(b // 2, NY)
    z = b // (2 * NY)

    def at_x(d):
        return {"blk": b, "rep": lax.rem(x + d, NX)}

    def at_y(d):
        return {"blk": (z * NY + lax.rem(y + d, NY)) * 2 + c, "rep": x}

    def at_z(d):
        return {"blk": (lax.rem(z + d, NZ) * NY + y) * 2 + c, "rep": x}

    at_c = {"blk": b + 1 - 2 * c, "rep": x}
    partners = [at_x(d) for d in range(1, NX)] + [at_y(d) for d in range(1, NY)]
    partners += [at_z(d) for d in range(1, NZ)] + [at_c]
    loads = [pltpu.make_async_copy(blocks_ref.at[s], held_x.at[s], load.at[s]) for s in range(NB)]
    inputs = (
        (coords_hbm, coords_ref), (counts_hbm, counts_ref), (fc_hbm, fc_ref), (fb_hbm, fb_ref), (start_hbm, start_ref),
    )
    feeds = [pltpu.make_async_copy(a, b, feed.at[n]) for n, (a, b) in enumerate(inputs)]
    for copy in feeds + loads:
        copy.start()
    barrier = pltpu.get_barrier_semaphore()
    for partner in partners:
        pl.semaphore_signal(barrier, inc=1, device_id=partner, device_id_type=pl.DeviceIdType.MESH)
    pl.semaphore_wait(barrier, len(partners))

    started = []

    def push(source, target, device):
        k = len(started)
        copy = pltpu.make_async_remote_copy(
            src_ref=source,
            dst_ref=target,
            send_sem=send.at[k],
            recv_sem=recv.at[k],
            device_id=device,
            device_id_type=pl.DeviceIdType.MESH,
        )
        copy.start()
        started.append(copy)
        return copy

    quarter = BI // NX

    feeds[0].wait()
    feeds[1].wait()
    lane = iota((8, 128), 1)
    label_row = lane & 31
    asks = jnp.zeros((8, 128), jnp.int32)
    for s in range(NB):
        label_row += jnp.where(lane >> 5 == s, (coords_ref[0, s] & (IB_DEV - 1)) * 32, 0)
        asks += jnp.where(lane == s, coords_ref[1, s], 0) + jnp.where(lane == NB + s, coords_ref[2, s], 0)
    level = iota((8, 128), 0)
    info_ref[...] = jnp.where(level == 0, label_row, jnp.where(level == 1, asks, 0))

    wishes = [push(info_ref, infos.at[z], at_z(d)) for d in range(1, NZ)]
    tags = [push(info_ref, codes.at[x], at_x(d)) for d in range(1, NX)]
    infos[z] = info_ref[...]
    codes[x] = info_ref[...]

    own = y * 2 + c
    planes = ((plane_c, 4), (plane_b, 16))

    def part(n, place):
        plane, count = planes[n]
        return plane.at[pl.ds(pl.multiple_of(place * count, count), count)]

    def half(d, h):
        place = lax.rem(y + d, NY) * 2 + c
        return plane_b.at[pl.ds(pl.multiple_of(place * 16 + 8 * h, 8), 8)]

    feeds[2].wait()
    for k in range(4):
        plane_c[own * 4 + k] = fc_ref[:, 128 * k : 128 * k + 128]
    along_y = [push(part(0, own), part(0, own), at_y(d)) for d in (2, 1, 3)]
    across_c = [push(part(0, own), part(0, own), at_c)]
    feeds[3].wait()
    for k in range(16):
        plane_b[own * 16 + k] = fb_ref[:, 128 * k : 128 * k + 128]
    hops = {}
    for d, h in ((1, 0), (3, 1), (1, 1), (3, 0)):
        hops[d, h] = push(half(0, h), half(0, h), at_y(d))
    across_b = [push(part(1, own), part(1, own), at_c)]
    feeds[4].wait()
    order = (iota((RR, RR), 0) // R3 == iota((RR, RR), 1) % R2) & (iota((RR, RR), 0) % R3 == iota((RR, RR), 1) // R2)
    order = order.astype(F32).astype(BF16)
    moved = jnp.dot(jnp.concatenate(split(start_ref[...]), axis=0), order, preferred_element_type=F32)
    space[...] = orthonormal_t(moved[:R2] + (moved[R2 : 2 * R2] + moved[2 * R2 :]))

    def came(d, h):
        hops[d, h].wait_recv()
        here = half(4 - d, h)
        if (d, h) in ((1, 0), (3, 1)):
            hops[2, h] = push(here, here, at_y(d))
        across_b.append(push(here, here, at_c))

    came(1, 0)
    came(3, 1)
    for copy in wishes:
        copy.wait_recv()
    copy = pltpu.make_async_copy(infos, asked, load.at[NB])
    copy.start()
    copy.wait()

    for k, d in ((1, 1), (2, 3), (0, 2)):
        along_y[k].wait_recv()
        place = lax.rem(y + NY - d, NY) * 2 + c
        across_c.append(push(part(0, place), part(0, place), at_c))
    for copy in across_c:
        copy.wait_recv()

    def answer(plane, mode, shift, mask, give, got):
        sent = []
        for d in range(NZ):
            t = lax.rem(z + d, NZ)
            for s in range(NB):
                block = plane[(asked[t, 1, NB * mode + s] >> shift) & mask]
                if d == 0:
                    got[z * NB + s] = block
                else:
                    give[d - 1, s] = block
            if d > 0:
                target = got.at[pl.ds(pl.multiple_of(z * NB, NB), NB)]
                sent.append(push(give.at[d - 1], target, at_z(d)))
        return sent

    sent_c = answer(plane_c, 1, 1, 31, give_c, got_c)
    for d, h in ((1, 1), (3, 0), (2, 0), (2, 1)):
        came(d, h)
    for copy in across_b:
        copy.wait_recv()
    sent_b = answer(plane_b, 0, 0, 127, give_b, got_b)
    for copy in loads:
        copy.wait()
    for copy in sent_c:
        copy.wait_recv()

    def fold_step(s, carry):
        wish = coords_ref[2, s]
        fold_slot(held_x, s, got_c[(wish >> 6) * NB + s], (wish & 1).astype(F32), folded)
        return carry

    lax.fori_loop(0, NB, fold_step, 0)
    for copy in sent_b:
        copy.wait_recv()

    moves = []
    unit = (iota((BI, BI), 0) == iota((BI, BI), 1)).astype(F32).astype(BF16)
    for s in range(NB):
        alive = jnp.clip(counts_ref[0] - s, 0, 1).astype(F32)
        total = contract_slot(folded, s, got_b[(coords_ref[1, s] >> 7) * NB + s], alive)
        high = total.astype(BF16)
        for k in range(RR // 128):
            turned = dot_nt(unit, high[128 * k : 128 * k + 128])
            high_ref[s, :, 128 * k : 128 * k + 128] = turned.astype(BF16)
        for d in (2, 1, 3):
            there = pl.ds(pl.multiple_of(lax.rem(x + d, NX) * quarter, quarter), quarter)
            moves.append(push(high_ref.at[s, there, :], rows.at[x, s], at_x(d)))
        turned_high[:, 128 * s : 128 * s + 128] = high
        turned_low[:, 128 * s : 128 * s + 128] = (total - high.astype(F32)).astype(BF16)
    rows[x] = high_ref[:, pl.ds(pl.multiple_of(x * quarter, quarter), quarter), :]
    for copy in tags:
        copy.wait_recv()
    labels = [codes[n].astype(F32) for n in range(NX)]
    along = jnp.concatenate([label[0:1, :] for label in labels], axis=1)
    down = jnp.concatenate([label.T[:, 0:1] for label in labels], axis=0)
    same = (down == along).astype(F32).astype(BF16)
    for copy in moves:
        copy.wait_recv()
    held = rows[...].reshape(RR, RR)
    summed = jnp.dot(same, held, preferred_element_type=F32)
    high = summed.astype(BF16)
    low = (summed - high.astype(F32)).astype(BF16)
    at = 0
    for a in range(4):
        left = held[:, 128 * a : 128 * a + 128]
        strip = dot_tn(left, high[:, 128 * a :]) + dot_tn(left, low[:, 128 * a :])
        for n in range(4 - a):
            g[pl.ds(128 * at, 128), :] = strip[:, 128 * n : 128 * n + 128]
            at += 1

    parts = ((0, PART_0, x, y, at_x, at_y, from_u0, from_v0), (PART_0, PART_1, y, x, at_y, at_x, from_u1, from_v1))

    def span(start, count):
        return pl.ds(pl.multiple_of(start, 8), count)

    def chunk(n, core, d):
        off, count, mu = parts[n][:3]
        return span(core * HALF + off + lax.rem(mu + d, 4) * (count // 4), count // 4)

    pieces = [(n, d) for d in (2, 1, 3, 0) for n in range(2)]
    crossed = [push(g.at[chunk(n, 1 - c, d)], from_c.at[chunk(n, 0, d)], at_c) for n, d in pieces]
    outgoing = [[], []]
    for copy, (n, d) in zip(crossed, pieces):
        copy.wait_recv()
        here = chunk(n, c, d)
        g[here, :] += from_c[chunk(n, 0, d), :]
        if d > 0:
            outgoing[n].append(push(g.at[here], parts[n][6].at[d - 1], parts[n][4](d)))

    def small(n, d):
        off, count, mu, mv = parts[n][:4]
        return span(c * HALF + off + mu * (count // 4) + lax.rem(mv + d, 4) * (count // 16), count // 16)

    second = [[], []]
    for n in range(2):
        for copy in outgoing[n]:
            copy.wait_recv()
        here = chunk(n, c, 0)
        got = parts[n][6]
        g[here, :] = g[here, :] + got[0] + got[1] + got[2]
        second[n] = [push(g.at[small(n, d)], parts[n][7].at[d - 1], parts[n][5](d)) for d in (2, 1, 3)]
    for n in range(2):
        for copy in second[n]:
            copy.wait_recv()
        got = parts[n][7]
        at = 0 if n == 0 else PART_0 // 16
        from_z[z, at : at + parts[n][1] // 16, :] = g[small(n, 0), :] + got[0] + got[1] + got[2]
    copies = [push(from_z.at[z], from_z.at[z], at_z(d)) for d in (4, 3, 5, 2, 6, 1, 7)]
    for copy in copies:
        copy.wait_recv()
    total = from_z[0]
    for n in range(1, NZ):
        total = total + from_z[n]

    back = [[], []]
    for n in range(2):
        at = 0 if n == 0 else PART_0 // 16
        here = small(n, 0)
        o[here, :] = total[at : at + parts[n][1] // 16]
        back[n] = [push(o.at[here], o.at[here], parts[n][5](d)) for d in (2, 1, 3)]
    wide_back = [[], []]
    relayed = []
    for n in range(2):
        for copy in back[n]:
            copy.wait_recv()
        here = chunk(n, c, 0)
        wide_back[n] = [push(o.at[here], o.at[here], parts[n][4](d)) for d in (2, 1, 3)]
        relayed.append(push(o.at[here], o.at[here], at_c))
    for k, d in ((1, 1), (2, 3), (0, 2)):
        for n in range(2):
            wide_back[n][k].wait_recv()
            here = chunk(n, c, 4 - d)
            relayed.append(push(o.at[here], o.at[here], at_c))
    for copy in relayed:
        copy.wait_recv()

    for n, (p, q) in enumerate(TILES):
        tile = o[pl.ds(128 * n, 128), :]
        for ref, part in zip((gh, gm, gl), split(tile)):
            ref[pl.ds(128 * p, 128), pl.ds(128 * q, 128)] = part
        if p != q:
            for ref, part in zip((gh, gm, gl), split(tile.T)):
                ref[pl.ds(128 * q, 128), pl.ds(128 * p, 128)] = part

    def step(n, carry):
        space[...] = orthonormal_t(fine_dot(space[...], gh[...], gm[...], gl[...]))
        return carry

    lax.fori_loop(0, ITERS, step, 0)
    last = space[...]
    small = inner_product(last, fine_dot(last, gh[...], gm[...], gl[...]))
    wide = fine_dot(inverse_lower(small), *split(last))
    wh, wm, _ = split(wide)
    both = jnp.dot(jnp.concatenate([wh, wm], axis=0), turned_high[...], preferred_element_type=F32)
    mapped = both[:R2] + (both[R2:] + jnp.dot(wh, turned_low[...], preferred_element_type=F32))
    maps[x] = mapped
    far[0] = mapped.astype(BF16)
    copies = [push(far.at[0], far.at[d], at_x(d)) for d in range(1, NX)]
    first = (x * (IB_DEV // NX)).astype(F32)
    for d in range(1, NX):
        copies[d - 1].wait_recv()
        maps[lax.rem(x + NX - d, NX)] = far[d].astype(F32)
    outs = [jnp.zeros((R2, BI), F32) for _ in range(IB_DEV // NX)]
    for n in range(NX):
        for s in range(NB):
            label = jnp.broadcast_to(labels[n][0:1, 32 * s : 32 * s + 1], (R2, BI)) * (1.0 / 32.0) - first
            term = maps[n, :, 128 * s : 128 * s + 128]
            for k in range(IB_DEV // NX):
                outs[k] = outs[k] + jnp.where(label == float(k), term, 0.0)
    for k in range(IB_DEV // NX):
        out_ref[:, 128 * k : 128 * k + 128] = outs[k]
    for copy in started:
        copy.wait_send()


def factor(blocks, coords, counts, slab_b, slab_c, start_t):
    copies = 110
    vmem = pl.BlockSpec(memory_space=pltpu.VMEM)
    hbm = pl.BlockSpec(memory_space=pltpu.HBM)
    return pl.pallas_call(
        factor_kernel,
        out_shape=jax.ShapeDtypeStruct((R2, IB_DEV * BI // NX), F32),
        in_specs=[hbm] * 6,
        out_specs=vmem,
        scratch_shapes=[
            pltpu.SMEM(coords.shape, jnp.int32),
            pltpu.SMEM(counts.shape, jnp.int32),
            pltpu.VMEM((8, 128), jnp.int32),
            pltpu.VMEM(slab_b.shape, BF16),
            pltpu.VMEM(slab_c.shape, BF16),
            pltpu.VMEM(start_t.shape, F32),
            pltpu.VMEM((NB, BI, BJ * BK), BF16),
            pltpu.VMEM((2 * NY * 16, R2, BJ), BF16),
            pltpu.VMEM((2 * NY * 4, R3, 2 * BK), BF16),
            pltpu.VMEM((NZ, 8, 128), jnp.int32),
            pltpu.SMEM((NZ, 8, 128), jnp.int32),
            pltpu.VMEM((NZ - 1, NB, R2, BJ), BF16),
            pltpu.VMEM((NZ - 1, NB, R3, 2 * BK), BF16),
            pltpu.VMEM((NZ * NB, R2, BJ), BF16),
            pltpu.VMEM((NZ * NB, R3, 2 * BK), BF16),
            pltpu.VMEM((NB, R3, BJ, BI), BF16),
            pltpu.VMEM((NB, BI, RR), BF16),
            pltpu.VMEM((RR, NB * BI), BF16),
            pltpu.VMEM((RR, NB * BI), BF16),
            pltpu.VMEM((NX, NB, BI // NX, RR), BF16),
            pltpu.VMEM((NX, 8, 128), jnp.int32),
            pltpu.VMEM((PACKED, 128), F32),
            pltpu.VMEM((PACKED, 128), F32),
            pltpu.VMEM((HALF, 128), F32),
            pltpu.VMEM((3, PART_0 // 4, 128), F32),
            pltpu.VMEM((3, PART_1 // 4, 128), F32),
            pltpu.VMEM((3, PART_0 // 16, 128), F32),
            pltpu.VMEM((3, PART_1 // 16, 128), F32),
            pltpu.VMEM((NZ, HALF // 16, 128), F32),
            pltpu.VMEM((RR, RR), BF16),
            pltpu.VMEM((RR, RR), BF16),
            pltpu.VMEM((RR, RR), BF16),
            pltpu.VMEM((R2, RR), F32),
            pltpu.VMEM((NX, R2, RR), F32),
            pltpu.VMEM((NX, R2, RR), BF16),
            pltpu.SemaphoreType.DMA((copies,)),
            pltpu.SemaphoreType.DMA((copies,)),
            pltpu.SemaphoreType.DMA((NB + 1,)),
            pltpu.SemaphoreType.DMA((5,)),
        ],
        compiler_params=pltpu.CompilerParams(
            collective_id=0, has_side_effects=True, vmem_limit_bytes=60 * 1024 * 1024
        ),
        name="factor",
    )(blocks, coords, counts, slab_b, slab_c, start_t)


def body(blocks, coords, counts, factor_b, factor_c, start):
    return factor(blocks, coords, counts, factor_b.T, factor_c.T, start.T).T


def solution(mesh):
    return jax.shard_map(
        body,
        mesh=mesh,
        in_specs=(
            P(("blk", "rep"), None, None),
            P(None, ("blk", "rep")),
            P(("blk", "rep")),
            P("blk", None),
            P("blk", None),
            P(),
        ),
        out_specs=P(("blk", "rep"), None),
        check_vma=False,
    )
```

```python
import jax
import jax.numpy as jnp
from jax import lax
from jax.experimental import pallas as pl
from jax.experimental.pallas import tpu as pltpu
from jax.sharding import PartitionSpec as P

BI = 128
BJ = 128
BK = 64
R2 = 32
R3 = 16
RR = 512
IB_DEV = 32
NB = 4
ITERS = 4
NX = 4
NY = 4
NZ = 8
PACKED = 1280
HALF = PACKED // 2
PART_0 = 384
PART_1 = HALF - PART_0
F32 = jnp.float32
BF16 = jnp.bfloat16
TILES = [(a, b) for a in range(4) for b in range(a, 4)]


def dot_nt(left, right):
    return lax.dot_general(left, right, (((1,), (1,)), ((), ())), preferred_element_type=F32)


def dot_tn(left, right):
    return lax.dot_general(left, right, (((0,), (0,)), ((), ())), preferred_element_type=F32)


def iota(shape, dim):
    return lax.broadcasted_iota(jnp.int32, shape, dim)


def fold_slot(held_x, slot, pair, odd, folded):
    pair = pair.astype(F32)
    mode_c = (pair[:, :BK] * (1.0 - odd) + pair[:, BK:] * odd).astype(BF16)
    spread = (iota((128, R3), 0) // 8 == iota((128, R3), 1)).astype(F32).astype(BF16)
    tall = jnp.dot(spread, mode_c, preferred_element_type=F32)
    wide = jnp.concatenate([tall] * 8, axis=1)
    fold_mask = iota((128, 512), 0) % 8 == iota((128, 512), 1) // BK
    fold_t = jnp.where(fold_mask, wide, 0.0).astype(BF16)
    for t in range(8):
        halves = [dot_nt(fold_t, held_x[slot, :, 512 * h : 512 * h + 512]) for h in (2 * t, 2 * t + 1)]
        part = jnp.concatenate([half.reshape(R3, 8, BI) for half in halves], axis=1)
        folded[slot, :, 16 * t : 16 * t + 16, :] = part.astype(BF16)


def contract_slot(folded, slot, block_b, alive):
    none = jnp.zeros((R2, BJ), BF16)
    two = jnp.concatenate(
        [jnp.concatenate([block_b, none], axis=1), jnp.concatenate([none, block_b], axis=1)], axis=0
    )
    parts = [
        jnp.dot(two, folded[slot, 2 * t : 2 * t + 2].reshape(2 * BJ, BI), preferred_element_type=F32)
        for t in range(R3 // 2)
    ]
    return jnp.concatenate(parts, axis=0) * alive


def split(value):
    high = value.astype(BF16)
    rest = value - high.astype(F32)
    middle = rest.astype(BF16)
    low = (rest - middle.astype(F32)).astype(BF16)
    return high, middle, low


def inner_product(left, right):
    lh, lm, ll = split(left)
    rh, rm, rl = split(right)
    return dot_nt(
        jnp.concatenate([lh, lh, lm, lh, ll, lm], axis=1),
        jnp.concatenate([rh, rm, rh, rl, rh, rm], axis=1),
    )


def fine_dot(left, high, middle, low):
    lh, lm, ll = split(left)
    n = left.shape[0]
    first = jnp.dot(jnp.concatenate([lh, lm, ll], axis=0), high, preferred_element_type=F32)
    second = jnp.dot(jnp.concatenate([lh, lm], axis=0), middle, preferred_element_type=F32)
    third = jnp.dot(lh, low, preferred_element_type=F32)
    small = first[2 * n :] + second[n:] + third
    return first[:n] + (first[n : 2 * n] + second[:n] + small)


def inverse_lower(inner):
    n = inner.shape[0]
    unit = (iota((n, n), 0) == iota((n, n), 1)).astype(F32)
    work = jnp.concatenate([inner, unit], axis=1)
    row = iota((n, 2 * n), 0)
    for k in range(0, n, 4):
        columns = [jnp.broadcast_to(work[:, k + t : k + t + 1], (n, 2 * n)) for t in range(4)]
        for t in range(4):
            at = k + t
            inverse = 1.0 / columns[t][at : at + 1]
            for u in range(t + 1, 4):
                columns[u] = columns[u] - columns[t] * (columns[u][at : at + 1] * inverse)
            work = work - jnp.where(row > at, columns[t], 0.0) * (work[at : at + 1] * inverse)
    diagonal = jnp.sum(work[:, :n] * unit, axis=1, keepdims=True)
    return work[:, n:] * lax.rsqrt(diagonal)


def orthonormal_t(value):
    return fine_dot(inverse_lower(inner_product(value, value)), *split(value))


def factor_kernel(
    blocks_ref, coords_hbm, counts_hbm, fb_hbm, fc_hbm, start_hbm, out_ref,
    coords_ref, counts_ref, info_ref, fb_ref, fc_ref, start_ref,
    held_x, plane_b, plane_c, infos, asked, give_b, give_c, got_b, got_c, folded, high_ref, turned_high, turned_low,
    rows, codes, g, o, from_c, from_u0, from_u1, from_v0, from_v1, from_z, gh, gm, gl, space, maps, far, send, recv, load, feed,
):
    b = lax.axis_index("blk")
    x = lax.axis_index("rep")
    c = lax.rem(b, 2)
    y = lax.rem(b // 2, NY)
    z = b // (2 * NY)

    def at_x(d):
        return {"blk": b, "rep": lax.rem(x + d, NX)}

    def at_y(d):
        return {"blk": (z * NY + lax.rem(y + d, NY)) * 2 + c, "rep": x}

    def at_z(d):
        return {"blk": (lax.rem(z + d, NZ) * NY + y) * 2 + c, "rep": x}

    at_c = {"blk": b + 1 - 2 * c, "rep": x}
    partners = [at_x(d) for d in range(1, NX)] + [at_y(d) for d in range(1, NY)]
    partners += [at_z(d) for d in range(1, NZ)] + [at_c]
    loads = [pltpu.make_async_copy(blocks_ref.at[s], held_x.at[s], load.at[s]) for s in range(NB)]
    inputs = (
        (coords_hbm, coords_ref), (counts_hbm, counts_ref), (fc_hbm, fc_ref), (fb_hbm, fb_ref), (start_hbm, start_ref),
    )
    feeds = [pltpu.make_async_copy(a, b, feed.at[n]) for n, (a, b) in enumerate(inputs)]
    for copy in feeds + loads:
        copy.start()
    barrier = pltpu.get_barrier_semaphore()
    for partner in partners:
        pl.semaphore_signal(barrier, inc=1, device_id=partner, device_id_type=pl.DeviceIdType.MESH)

    started = []

    def push(source, target, device):
        k = len(started)
        copy = pltpu.make_async_remote_copy(
            src_ref=source,
            dst_ref=target,
            send_sem=send.at[k],
            recv_sem=recv.at[k],
            device_id=device,
            device_id_type=pl.DeviceIdType.MESH,
        )
        copy.start()
        started.append(copy)
        return copy

    quarter = BI // NX

    feeds[0].wait()
    feeds[1].wait()
    lane = iota((8, 128), 1)
    label_row = lane & 31
    asks = jnp.zeros((8, 128), jnp.int32)
    for s in range(NB):
        label_row += jnp.where(lane >> 5 == s, (coords_ref[0, s] & (IB_DEV - 1)) * 32, 0)
        asks += jnp.where(lane == s, coords_ref[1, s], 0) + jnp.where(lane == NB + s, coords_ref[2, s], 0)
    level = iota((8, 128), 0)
    info_ref[...] = jnp.where(level == 0, label_row, jnp.where(level == 1, asks, 0))

    infos[z] = info_ref[...]
    codes[x] = info_ref[...]
    own = y * 2 + c
    feeds[2].wait()
    for k in range(4):
        plane_c[own * 4 + k] = fc_ref[:, 128 * k : 128 * k + 128]
    feeds[3].wait()
    for k in range(16):
        plane_b[own * 16 + k] = fb_ref[:, 128 * k : 128 * k + 128]
    pl.semaphore_wait(barrier, len(partners))

    wishes = [push(info_ref, infos.at[z], at_z(d)) for d in range(1, NZ)]
    tags = [push(info_ref, codes.at[x], at_x(d)) for d in range(1, NX)]

    planes = ((plane_c, 4), (plane_b, 16))

    def part(n, place):
        plane, count = planes[n]
        return plane.at[pl.ds(pl.multiple_of(place * count, count), count)]

    def half(d, h):
        place = lax.rem(y + d, NY) * 2 + c
        return plane_b.at[pl.ds(pl.multiple_of(place * 16 + 8 * h, 8), 8)]

    along_y = [push(part(0, own), part(0, own), at_y(d)) for d in (2, 1, 3)]
    across_c = [push(part(0, own), part(0, own), at_c)]
    hops = {}
    for d, h in ((1, 0), (3, 1), (1, 1), (3, 0)):
        hops[d, h] = push(half(0, h), half(0, h), at_y(d))
    across_b = [push(part(1, own), part(1, own), at_c)]
    def came(d, h):
        hops[d, h].wait_recv()
        here = half(4 - d, h)
        if (d, h) in ((1, 0), (3, 1)):
            hops[2, h] = push(here, here, at_y(d))
        across_b.append(push(here, here, at_c))

    for k, d in ((1, 1), (2, 3), (0, 2)):
        along_y[k].wait_recv()
        place = lax.rem(y + NY - d, NY) * 2 + c
        across_c.append(push(part(0, place), part(0, place), at_c))
    came(1, 0)
    came(3, 1)
    for copy in wishes:
        copy.wait_recv()
    copy = pltpu.make_async_copy(infos, asked, load.at[NB])
    copy.start()
    copy.wait()
    for copy in across_c:
        copy.wait_recv()

    def answer(pick, count, give, got):
        sent = []
        for d in (0, 4, 3, 5, 2, 6, 1, 7):
            t = lax.rem(z + d, NZ)
            for s in range(count):
                if d == 0:
                    got[z * count + s] = pick(t, s)
                else:
                    give[d - 1, s] = pick(t, s)
            if d > 0:
                target = got.at[pl.ds(pl.multiple_of(z * count, count), count)]
                sent.append((d, push(give.at[d - 1], target, at_z(d))))
        return [copy for _, copy in sorted(sent, key=lambda item: item[0])]

    left_half = iota((R3, 2 * BK), 1) < BK

    def half_c(t, s):
        picked = []
        for n in range(2):
            wish = asked[t, 1, NB + 2 * s + n]
            pair = plane_c[(wish >> 1) & 31].astype(F32)
            swapped = jnp.concatenate([pair[:, BK:], pair[:, :BK]], axis=1)
            move = ((wish & 1) ^ n).astype(F32)
            picked.append(pair * (1.0 - move) + swapped * move)
        return jnp.where(left_half, picked[0], picked[1]).astype(BF16)

    sent_c = answer(half_c, NB // 2, give_c, got_c)
    for d, h in ((1, 1), (3, 0), (2, 0), (2, 1)):
        came(d, h)
    for copy in across_b:
        copy.wait_recv()
    sent_b = answer(lambda t, s: plane_b[asked[t, 1, s] & 127], NB, give_b, got_b)
    for copy in loads:
        copy.wait()
    for copy in sent_c:
        copy.wait_recv()

    def fold_step(s, carry):
        wish = coords_ref[2, s]
        fold_slot(held_x, s, got_c[(wish >> 6) * (NB // 2) + (s >> 1)], (s & 1).astype(F32), folded)
        return carry

    lax.fori_loop(0, NB, fold_step, 0)
    for copy in sent_b:
        copy.wait_recv()

    moves = []
    unit = (iota((BI, BI), 0) == iota((BI, BI), 1)).astype(F32).astype(BF16)
    for s in range(NB):
        alive = jnp.clip(counts_ref[0] - s, 0, 1).astype(F32)
        total = contract_slot(folded, s, got_b[(coords_ref[1, s] >> 7) * NB + s], alive)
        high = total.astype(BF16)
        for k in range(RR // 128):
            turned = dot_nt(unit, high[128 * k : 128 * k + 128])
            high_ref[s, :, 128 * k : 128 * k + 128] = turned.astype(BF16)
        for d in (2, 1, 3):
            there = pl.ds(pl.multiple_of(lax.rem(x + d, NX) * quarter, quarter), quarter)
            moves.append(push(high_ref.at[s, there, :], rows.at[x, s], at_x(d)))
        turned_high[:, 128 * s : 128 * s + 128] = high
        turned_low[:, 128 * s : 128 * s + 128] = (total - high.astype(F32)).astype(BF16)
    feeds[4].wait()
    order = (iota((RR, RR), 0) // R3 == iota((RR, RR), 1) % R2) & (iota((RR, RR), 0) % R3 == iota((RR, RR), 1) // R2)
    order = order.astype(F32).astype(BF16)
    moved = jnp.dot(jnp.concatenate(split(start_ref[...]), axis=0), order, preferred_element_type=F32)
    space[...] = orthonormal_t(moved[:R2] + (moved[R2 : 2 * R2] + moved[2 * R2 :]))

    rows[x] = high_ref[:, pl.ds(pl.multiple_of(x * quarter, quarter), quarter), :]
    for copy in tags:
        copy.wait_recv()
    labels = [codes[n].astype(F32) for n in range(NX)]
    along = jnp.concatenate([label[0:1, :] for label in labels], axis=1)
    down = jnp.concatenate([label.T[:, 0:1] for label in labels], axis=0)
    same = (down == along).astype(F32).astype(BF16)
    for copy in moves:
        copy.wait_recv()
    held = rows[...].reshape(RR, RR)
    summed = jnp.dot(same, held, preferred_element_type=F32)
    high = summed.astype(BF16)
    low = (summed - high.astype(F32)).astype(BF16)
    at = 0
    for a in range(4):
        left = held[:, 128 * a : 128 * a + 128]
        strip = dot_tn(left, high[:, 128 * a :]) + dot_tn(left, low[:, 128 * a :])
        for n in range(4 - a):
            g[pl.ds(128 * at, 128), :] = strip[:, 128 * n : 128 * n + 128]
            at += 1

    parts = ((0, PART_0, x, y, at_x, at_y, from_u0, from_v0), (PART_0, PART_1, y, x, at_y, at_x, from_u1, from_v1))

    def span(start, count):
        return pl.ds(pl.multiple_of(start, 8), count)

    def chunk(n, core, d):
        off, count, mu = parts[n][:3]
        return span(core * HALF + off + lax.rem(mu + d, 4) * (count // 4), count // 4)

    pieces = [(n, d) for d in (2, 1, 3, 0) for n in range(2)]
    crossed = [push(g.at[chunk(n, 1 - c, d)], from_c.at[chunk(n, 0, d)], at_c) for n, d in pieces]
    outgoing = [[], []]
    for copy, (n, d) in zip(crossed, pieces):
        copy.wait_recv()
        here = chunk(n, c, d)
        g[here, :] += from_c[chunk(n, 0, d), :]
        if d > 0:
            outgoing[n].append(push(g.at[here], parts[n][6].at[d - 1], parts[n][4](d)))

    def small(n, d):
        off, count, mu, mv = parts[n][:4]
        return span(c * HALF + off + mu * (count // 4) + lax.rem(mv + d, 4) * (count // 16), count // 16)

    second = [[], []]
    for n in range(2):
        for copy in outgoing[n]:
            copy.wait_recv()
        here = chunk(n, c, 0)
        got = parts[n][6]
        g[here, :] = g[here, :] + got[0] + got[1] + got[2]
        second[n] = [push(g.at[small(n, d)], parts[n][7].at[d - 1], parts[n][5](d)) for d in (2, 1, 3)]
    for n in range(2):
        for copy in second[n]:
            copy.wait_recv()
        got = parts[n][7]
        at = 0 if n == 0 else PART_0 // 16
        from_z[z, at : at + parts[n][1] // 16, :] = g[small(n, 0), :] + got[0] + got[1] + got[2]
    copies = [push(from_z.at[z], from_z.at[z], at_z(d)) for d in (4, 3, 5, 2, 6, 1, 7)]
    for copy in copies:
        copy.wait_recv()
    total = from_z[0]
    for n in range(1, NZ):
        total = total + from_z[n]

    back = [[], []]
    for n in range(2):
        at = 0 if n == 0 else PART_0 // 16
        here = small(n, 0)
        o[here, :] = total[at : at + parts[n][1] // 16]
        back[n] = [push(o.at[here], o.at[here], parts[n][5](d)) for d in (2, 1, 3)]
    wide_back = [[], []]
    relayed = []
    for n in range(2):
        for copy in back[n]:
            copy.wait_recv()
        here = chunk(n, c, 0)
        wide_back[n] = [push(o.at[here], o.at[here], parts[n][4](d)) for d in (2, 1, 3)]
        relayed.append(push(o.at[here], o.at[here], at_c))
    for k, d in ((1, 1), (2, 3), (0, 2)):
        for n in range(2):
            wide_back[n][k].wait_recv()
            here = chunk(n, c, 4 - d)
            relayed.append(push(o.at[here], o.at[here], at_c))
    for copy in relayed:
        copy.wait_recv()

    for n, (p, q) in enumerate(TILES):
        tile = o[pl.ds(128 * n, 128), :]
        for ref, part in zip((gh, gm, gl), split(tile)):
            ref[pl.ds(128 * p, 128), pl.ds(128 * q, 128)] = part
        if p != q:
            for ref, part in zip((gh, gm, gl), split(tile.T)):
                ref[pl.ds(128 * q, 128), pl.ds(128 * p, 128)] = part

    def step(n, carry):
        space[...] = orthonormal_t(fine_dot(space[...], gh[...], gm[...], gl[...]))
        return carry

    lax.fori_loop(0, ITERS, step, 0)
    last = space[...]
    small = inner_product(last, fine_dot(last, gh[...], gm[...], gl[...]))
    wh, wm, _ = split(last)
    both = jnp.dot(jnp.concatenate([wh, wm], axis=0), turned_high[...], preferred_element_type=F32)
    product = both[:R2] + (both[R2:] + jnp.dot(wh, turned_low[...], preferred_element_type=F32))
    mapped = fine_dot(inverse_lower(small), *split(product))
    maps[x] = mapped
    far[0] = mapped.astype(BF16)
    copies = [push(far.at[0], far.at[d], at_x(d)) for d in range(1, NX)]
    first = (x * (IB_DEV // NX)).astype(F32)
    for d in range(1, NX):
        copies[d - 1].wait_recv()
        maps[lax.rem(x + NX - d, NX)] = far[d].astype(F32)
    outs = [jnp.zeros((R2, BI), F32) for _ in range(IB_DEV // NX)]
    for n in range(NX):
        for s in range(NB):
            label = jnp.broadcast_to(labels[n][0:1, 32 * s : 32 * s + 1], (R2, BI)) * (1.0 / 32.0) - first
            term = maps[n, :, 128 * s : 128 * s + 128]
            for k in range(IB_DEV // NX):
                outs[k] = outs[k] + jnp.where(label == float(k), term, 0.0)
    for k in range(IB_DEV // NX):
        out_ref[:, 128 * k : 128 * k + 128] = outs[k]
    for copy in started:
        copy.wait_send()


def factor(blocks, coords, counts, slab_b, slab_c, start_t):
    copies = 110
    vmem = pl.BlockSpec(memory_space=pltpu.VMEM)
    hbm = pl.BlockSpec(memory_space=pltpu.HBM)
    return pl.pallas_call(
        factor_kernel,
        out_shape=jax.ShapeDtypeStruct((R2, IB_DEV * BI // NX), F32),
        in_specs=[hbm] * 6,
        out_specs=vmem,
        scratch_shapes=[
            pltpu.SMEM(coords.shape, jnp.int32),
            pltpu.SMEM(counts.shape, jnp.int32),
            pltpu.VMEM((8, 128), jnp.int32),
            pltpu.VMEM(slab_b.shape, BF16),
            pltpu.VMEM(slab_c.shape, BF16),
            pltpu.VMEM(start_t.shape, F32),
            pltpu.VMEM((NB, BI, BJ * BK), BF16),
            pltpu.VMEM((2 * NY * 16, R2, BJ), BF16),
            pltpu.VMEM((2 * NY * 4, R3, 2 * BK), BF16),
            pltpu.VMEM((NZ, 8, 128), jnp.int32),
            pltpu.SMEM((NZ, 8, 128), jnp.int32),
            pltpu.VMEM((NZ - 1, NB, R2, BJ), BF16),
            pltpu.VMEM((NZ - 1, NB // 2, R3, 2 * BK), BF16),
            pltpu.VMEM((NZ * NB, R2, BJ), BF16),
            pltpu.VMEM((NZ * NB // 2, R3, 2 * BK), BF16),
            pltpu.VMEM((NB, R3, BJ, BI), BF16),
            pltpu.VMEM((NB, BI, RR), BF16),
            pltpu.VMEM((RR, NB * BI), BF16),
            pltpu.VMEM((RR, NB * BI), BF16),
            pltpu.VMEM((NX, NB, BI // NX, RR), BF16),
            pltpu.VMEM((NX, 8, 128), jnp.int32),
            pltpu.VMEM((PACKED, 128), F32),
            pltpu.VMEM((PACKED, 128), F32),
            pltpu.VMEM((HALF, 128), F32),
            pltpu.VMEM((3, PART_0 // 4, 128), F32),
            pltpu.VMEM((3, PART_1 // 4, 128), F32),
            pltpu.VMEM((3, PART_0 // 16, 128), F32),
            pltpu.VMEM((3, PART_1 // 16, 128), F32),
            pltpu.VMEM((NZ, HALF // 16, 128), F32),
            pltpu.VMEM((RR, RR), BF16),
            pltpu.VMEM((RR, RR), BF16),
            pltpu.VMEM((RR, RR), BF16),
            pltpu.VMEM((R2, RR), F32),
            pltpu.VMEM((NX, R2, RR), F32),
            pltpu.VMEM((NX, R2, RR), BF16),
            pltpu.SemaphoreType.DMA((copies,)),
            pltpu.SemaphoreType.DMA((copies,)),
            pltpu.SemaphoreType.DMA((NB + 1,)),
            pltpu.SemaphoreType.DMA((5,)),
        ],
        compiler_params=pltpu.CompilerParams(
            collective_id=0, has_side_effects=True, vmem_limit_bytes=60 * 1024 * 1024
        ),
        name="factor",
    )(blocks, coords, counts, slab_b, slab_c, start_t)


def body(blocks, coords, counts, factor_b, factor_c, start):
    return factor(blocks, coords, counts, factor_b.T, factor_c.T, start.T).T


def solution(mesh):
    return jax.shard_map(
        body,
        mesh=mesh,
        in_specs=(
            P(("blk", "rep"), None, None),
            P(None, ("blk", "rep")),
            P(("blk", "rep")),
            P("blk", None),
            P("blk", None),
            P(),
        ),
        out_specs=P(("blk", "rep"), None),
        check_vma=False,
    )
```

```python
import functools

import jax
import jax.numpy as jnp
from jax import lax
from jax.experimental import pallas as pl
from jax.experimental.pallas import tpu as pltpu
from jax.sharding import PartitionSpec as P

BI = 128
BJ = 128
BK = 64
R2 = 32
R3 = 16
RR = 512
IB_DEV = 32
NB = 4
ITERS = 4
NX = 4
NY = 4
NZ = 8
PACKED = 1280
HALF = PACKED // 2
PART_0 = 384
PART_1 = HALF - PART_0
F32 = jnp.float32
BF16 = jnp.bfloat16
TILES = [(a, b) for a in range(4) for b in range(a, 4)]


def dot_nt(left, right):
    return lax.dot_general(left, right, (((1,), (1,)), ((), ())), preferred_element_type=F32)


def dot_tn(left, right):
    return lax.dot_general(left, right, (((0,), (0,)), ((), ())), preferred_element_type=F32)


def iota(shape, dim):
    return lax.broadcasted_iota(jnp.int32, shape, dim)


def fold_slot(held_x, slot, pair, odd, folded):
    pair = pair.astype(F32)
    mode_c = (pair[:, :BK] * (1.0 - odd) + pair[:, BK:] * odd).astype(BF16)
    spread = (iota((128, R3), 0) // 8 == iota((128, R3), 1)).astype(F32).astype(BF16)
    tall = jnp.dot(spread, mode_c, preferred_element_type=F32)
    wide = jnp.concatenate([tall] * 8, axis=1)
    fold_mask = iota((128, 512), 0) % 8 == iota((128, 512), 1) // BK
    fold_t = jnp.where(fold_mask, wide, 0.0).astype(BF16)
    for t in range(8):
        halves = [dot_nt(fold_t, held_x[slot, :, 512 * h : 512 * h + 512]) for h in (2 * t, 2 * t + 1)]
        part = jnp.concatenate([half.reshape(R3, 8, BI) for half in halves], axis=1)
        folded[slot, :, 16 * t : 16 * t + 16, :] = part.astype(BF16)


def contract_slot(folded, slot, block_b, alive):
    none = jnp.zeros((R2, BJ), BF16)
    two = jnp.concatenate(
        [jnp.concatenate([block_b, none], axis=1), jnp.concatenate([none, block_b], axis=1)], axis=0
    )
    parts = [
        jnp.dot(two, folded[slot, 2 * t : 2 * t + 2].reshape(2 * BJ, BI), preferred_element_type=F32)
        for t in range(R3 // 2)
    ]
    return jnp.concatenate(parts, axis=0) * alive


def split(value):
    high = value.astype(BF16)
    rest = value - high.astype(F32)
    middle = rest.astype(BF16)
    low = (rest - middle.astype(F32)).astype(BF16)
    return high, middle, low


def inner_product(left, right):
    lh, lm, ll = split(left)
    rh, rm, rl = split(right)
    return dot_nt(
        jnp.concatenate([lh, lh, lm, lh, ll, lm], axis=1),
        jnp.concatenate([rh, rm, rh, rl, rh, rm], axis=1),
    )


def fine_dot(left, high, middle, low):
    lh, lm, ll = split(left)
    n = left.shape[0]
    first = jnp.dot(jnp.concatenate([lh, lm, ll], axis=0), high, preferred_element_type=F32)
    second = jnp.dot(jnp.concatenate([lh, lm], axis=0), middle, preferred_element_type=F32)
    third = jnp.dot(lh, low, preferred_element_type=F32)
    small = first[2 * n :] + second[n:] + third
    return first[:n] + (first[n : 2 * n] + second[:n] + small)


def inverse_lower(inner):
    n = inner.shape[0]
    unit = (iota((n, n), 0) == iota((n, n), 1)).astype(F32)
    work = jnp.concatenate([inner, unit], axis=1)
    row = iota((n, 2 * n), 0)
    for k in range(0, n, 4):
        columns = [jnp.broadcast_to(work[:, k + t : k + t + 1], (n, 2 * n)) for t in range(4)]
        for t in range(4):
            at = k + t
            inverse = 1.0 / columns[t][at : at + 1]
            for u in range(t + 1, 4):
                columns[u] = columns[u] - columns[t] * (columns[u][at : at + 1] * inverse)
            work = work - jnp.where(row > at, columns[t], 0.0) * (work[at : at + 1] * inverse)
    diagonal = jnp.sum(work[:, :n] * unit, axis=1, keepdims=True)
    return work[:, n:] * lax.rsqrt(diagonal)


def orthonormal_t(value):
    return fine_dot(inverse_lower(inner_product(value, value)), *split(value))


def factor_kernel(
    blocks_ref, coords_hbm, counts_hbm, fb_hbm, fc_hbm, start_hbm, out_ref,
    coords_ref, counts_ref, info_ref, fb_ref, fc_ref, start_ref,
    held_x, plane_b, plane_c, infos, asked, give_b, give_c, got_b, got_c, folded, high_ref, turned_high, turned_low, via,
    rows, codes, g, o, from_c, from_u0, from_u1, from_v0, from_v1, from_z, gh, gm, gl, space, maps, far, send, recv, load, feed,
):
    b = lax.axis_index("blk")
    x = lax.axis_index("rep")
    c = lax.rem(b, 2)
    y = lax.rem(b // 2, NY)
    z = b // (2 * NY)

    def at_x(d):
        return {"blk": b, "rep": lax.rem(x + d, NX)}

    def at_y(d):
        return {"blk": (z * NY + lax.rem(y + d, NY)) * 2 + c, "rep": x}

    def at_z(d):
        return {"blk": (lax.rem(z + d, NZ) * NY + y) * 2 + c, "rep": x}

    at_c = {"blk": b + 1 - 2 * c, "rep": x}
    partners = [at_x(d) for d in range(1, NX)] + [at_y(d) for d in range(1, NY)]
    partners += [at_z(d) for d in range(1, NZ)] + [at_c]
    loads = [pltpu.make_async_copy(blocks_ref.at[s], held_x.at[s], load.at[s]) for s in range(NB)]
    inputs = (
        (coords_hbm, coords_ref), (counts_hbm, counts_ref), (fc_hbm, fc_ref), (fb_hbm, fb_ref), (start_hbm, start_ref),
    )
    feeds = [pltpu.make_async_copy(a, b, feed.at[n]) for n, (a, b) in enumerate(inputs)]
    for copy in feeds + loads:
        copy.start()
    barrier = pltpu.get_barrier_semaphore()
    for partner in partners:
        pl.semaphore_signal(barrier, inc=1, device_id=partner, device_id_type=pl.DeviceIdType.MESH)

    started = []

    def push(source, target, device):
        k = len(started)
        copy = pltpu.make_async_remote_copy(
            src_ref=source,
            dst_ref=target,
            send_sem=send.at[k],
            recv_sem=recv.at[k],
            device_id=device,
            device_id_type=pl.DeviceIdType.MESH,
        )
        copy.start()
        started.append(copy)
        return copy

    quarter = BI // NX

    feeds[0].wait()
    feeds[1].wait()
    lane = iota((8, 128), 1)
    label_row = lane & 31
    asks = jnp.zeros((8, 128), jnp.int32)
    for s in range(NB):
        label_row += jnp.where(lane >> 5 == s, (coords_ref[0, s] & (IB_DEV - 1)) * 32, 0)
        asks += jnp.where(lane == s, coords_ref[1, s], 0) + jnp.where(lane == NB + s, coords_ref[2, s], 0)
    level = iota((8, 128), 0)
    info_ref[...] = jnp.where(level == 0, label_row, jnp.where(level == 1, asks, 0))

    infos[z] = info_ref[...]
    codes[x] = info_ref[...]
    own = y * 2 + c
    feeds[2].wait()
    for k in range(4):
        plane_c[own * 4 + k] = fc_ref[:, 128 * k : 128 * k + 128]
    feeds[3].wait()
    for k in range(16):
        plane_b[own * 16 + k] = fb_ref[:, 128 * k : 128 * k + 128]
    pl.semaphore_wait(barrier, len(partners))

    wishes = [push(info_ref, infos.at[z], at_z(d)) for d in range(1, NZ)]
    tags = [push(info_ref, codes.at[x], at_x(d)) for d in range(1, NX)]

    planes = ((plane_c, 4), (plane_b, 16))

    def part(n, place):
        plane, count = planes[n]
        return plane.at[pl.ds(pl.multiple_of(place * count, count), count)]

    def half(d, h):
        place = lax.rem(y + d, NY) * 2 + c
        return plane_b.at[pl.ds(pl.multiple_of(place * 16 + 8 * h, 8), 8)]

    along_y = [push(part(0, own), part(0, own), at_y(d)) for d in (2, 1, 3)]
    across_c = [push(part(0, own), part(0, own), at_c)]
    hops = {}
    for d, h in ((1, 0), (3, 1), (1, 1), (3, 0)):
        hops[d, h] = push(half(0, h), half(0, h), at_y(d))
    across_b = [push(part(1, own), part(1, own), at_c)]
    def came(d, h):
        hops[d, h].wait_recv()
        here = half(4 - d, h)
        if (d, h) in ((1, 0), (3, 1)):
            hops[2, h] = push(here, here, at_y(d))
        across_b.append(push(here, here, at_c))

    for k, d in ((1, 1), (2, 3), (0, 2)):
        along_y[k].wait_recv()
        place = lax.rem(y + NY - d, NY) * 2 + c
        across_c.append(push(part(0, place), part(0, place), at_c))
    came(1, 0)
    came(3, 1)
    for copy in wishes:
        copy.wait_recv()
    copy = pltpu.make_async_copy(infos, asked, load.at[NB])
    copy.start()
    copy.wait()
    for copy in across_c:
        copy.wait_recv()

    def answer(pick, count, give, got):
        sent = []
        for d in (0, 4, 3, 5, 2, 6, 1, 7):
            t = lax.rem(z + d, NZ)
            for s in range(count):
                if d == 0:
                    got[z * count + s] = pick(t, s)
                else:
                    give[d - 1, s] = pick(t, s)
            if d > 0:
                target = got.at[pl.ds(pl.multiple_of(z * count, count), count)]
                sent.append((d, push(give.at[d - 1], target, at_z(d))))
        return [copy for _, copy in sorted(sent, key=lambda item: item[0])]

    left_half = iota((R3, 2 * BK), 1) < BK

    def half_c(t, s):
        picked = []
        for n in range(2):
            wish = asked[t, 1, NB + 2 * s + n]
            pair = plane_c[(wish >> 1) & 31].astype(F32)
            swapped = jnp.concatenate([pair[:, BK:], pair[:, :BK]], axis=1)
            move = ((wish & 1) ^ n).astype(F32)
            picked.append(pair * (1.0 - move) + swapped * move)
        return jnp.where(left_half, picked[0], picked[1]).astype(BF16)

    sent_c = answer(half_c, NB // 2, give_c, got_c)
    for d, h in ((1, 1), (3, 0), (2, 0), (2, 1)):
        came(d, h)
    for copy in across_b:
        copy.wait_recv()
    sent_b = answer(lambda t, s: plane_b[asked[t, 1, s] & 127], NB, give_b, got_b)
    for copy in loads:
        copy.wait()
    for copy in sent_c:
        copy.wait_recv()

    def fold_step(s, carry):
        wish = coords_ref[2, s]
        fold_slot(held_x, s, got_c[(wish >> 6) * (NB // 2) + (s >> 1)], (s & 1).astype(F32), folded)
        return carry

    lax.fori_loop(0, NB, fold_step, 0)
    for copy in sent_b:
        copy.wait_recv()

    moves, staged = [], []

    def forward(s):
        for k in range(2):
            staged[s][k].wait_recv()
            origin = lax.rem(x + 3 - 2 * k, NX)
            moves.append(push(via.at[k, s], rows.at[origin, s, pl.ds(16 * k, 16), :], at_x(2 * k + 1)))

    unit = (iota((BI, BI), 0) == iota((BI, BI), 1)).astype(F32).astype(BF16)
    for s in range(NB):
        alive = jnp.clip(counts_ref[0] - s, 0, 1).astype(F32)
        total = contract_slot(folded, s, got_b[(coords_ref[1, s] >> 7) * NB + s], alive)
        high = total.astype(BF16)
        for k in range(RR // 128):
            turned = dot_nt(unit, high[128 * k : 128 * k + 128])
            high_ref[s, :, 128 * k : 128 * k + 128] = turned.astype(BF16)
        ends = [pl.ds(pl.multiple_of(lax.rem(x + 2, NX) * quarter + 16 * k, 16), 16) for k in range(2)]
        staged.append([push(high_ref.at[s, ends[k], :], via.at[k, s], at_x(2 * k + 1)) for k in range(2)])
        for d in (1, 3):
            there = pl.ds(pl.multiple_of(lax.rem(x + d, NX) * quarter, quarter), quarter)
            moves.append(push(high_ref.at[s, there, :], rows.at[x, s], at_x(d)))
        if s > 1:
            forward(s - 2)
        turned_high[:, 128 * s : 128 * s + 128] = high
        turned_low[:, 128 * s : 128 * s + 128] = (total - high.astype(F32)).astype(BF16)
    forward(NB - 2)
    forward(NB - 1)
    rows[x] = high_ref[:, pl.ds(pl.multiple_of(x * quarter, quarter), quarter), :]
    for copy in tags:
        copy.wait_recv()
    labels = [codes[n].astype(F32) for n in range(NX)]
    along = jnp.concatenate([label[0:1, :] for label in labels], axis=1)
    down = jnp.concatenate([label.T[:, 0:1] for label in labels], axis=0)
    same = (down == along).astype(F32).astype(BF16)
    for copy in moves:
        copy.wait_recv()
    held = rows[...].reshape(RR, RR)
    summed = jnp.dot(same, held, preferred_element_type=F32)
    high = summed.astype(BF16)
    low = (summed - high.astype(F32)).astype(BF16)
    at = 0
    for a in range(4):
        left = held[:, 128 * a : 128 * a + 128]
        strip = dot_tn(left, high[:, 128 * a :]) + dot_tn(left, low[:, 128 * a :])
        for n in range(4 - a):
            g[pl.ds(128 * at, 128), :] = strip[:, 128 * n : 128 * n + 128]
            at += 1

    parts = ((0, PART_0, x, y, at_x, at_y, from_u0, from_v0), (PART_0, PART_1, y, x, at_y, at_x, from_u1, from_v1))

    def span(start, count):
        return pl.ds(pl.multiple_of(start, 8), count)

    def chunk(n, core, d):
        off, count, mu = parts[n][:3]
        return span(core * HALF + off + lax.rem(mu + d, 4) * (count // 4), count // 4)

    pieces = [(n, d) for d in (2, 1, 3, 0) for n in range(2)]
    crossed = [push(g.at[chunk(n, 1 - c, d)], from_c.at[chunk(n, 0, d)], at_c) for n, d in pieces]
    outgoing = [[], []]
    for copy, (n, d) in zip(crossed, pieces):
        copy.wait_recv()
        here = chunk(n, c, d)
        g[here, :] += from_c[chunk(n, 0, d), :]
        if d > 0:
            outgoing[n].append(push(g.at[here], parts[n][6].at[d - 1], parts[n][4](d)))

    def small(n, d):
        off, count, mu, mv = parts[n][:4]
        return span(c * HALF + off + mu * (count // 4) + lax.rem(mv + d, 4) * (count // 16), count // 16)

    second = [[], []]
    for n in range(2):
        for copy in outgoing[n]:
            copy.wait_recv()
        here = chunk(n, c, 0)
        got = parts[n][6]
        g[here, :] = g[here, :] + got[0] + got[1] + got[2]
        second[n] = [push(g.at[small(n, d)], parts[n][7].at[d - 1], parts[n][5](d)) for d in (2, 1, 3)]
    for n in range(2):
        for copy in second[n]:
            copy.wait_recv()
        got = parts[n][7]
        at = 0 if n == 0 else PART_0 // 16
        from_z[z, at : at + parts[n][1] // 16, :] = g[small(n, 0), :] + got[0] + got[1] + got[2]
    copies = [push(from_z.at[z], from_z.at[z], at_z(d)) for d in (4, 3, 5, 2, 6, 1, 7)]
    feeds[4].wait()
    order = (iota((RR, RR), 0) // R3 == iota((RR, RR), 1) % R2) & (iota((RR, RR), 0) % R3 == iota((RR, RR), 1) // R2)
    order = order.astype(F32).astype(BF16)
    moved = jnp.dot(jnp.concatenate(split(start_ref[...]), axis=0), order, preferred_element_type=F32)
    space[...] = orthonormal_t(moved[:R2] + (moved[R2 : 2 * R2] + moved[2 * R2 :]))

    for copy in copies:
        copy.wait_recv()
    total = from_z[0]
    for n in range(1, NZ):
        total = total + from_z[n]

    back = [[], []]
    for n in range(2):
        at = 0 if n == 0 else PART_0 // 16
        here = small(n, 0)
        o[here, :] = total[at : at + parts[n][1] // 16]
        back[n] = [push(o.at[here], o.at[here], parts[n][5](d)) for d in (2, 1, 3)]
    wide_back = [[], []]
    relayed = []
    for n in range(2):
        for copy in back[n]:
            copy.wait_recv()
        here = chunk(n, c, 0)
        wide_back[n] = [push(o.at[here], o.at[here], parts[n][4](d)) for d in (2, 1, 3)]
        relayed.append(push(o.at[here], o.at[here], at_c))
    for k, d in ((1, 1), (2, 3), (0, 2)):
        for n in range(2):
            wide_back[n][k].wait_recv()
            here = chunk(n, c, 4 - d)
            relayed.append(push(o.at[here], o.at[here], at_c))
    for copy in relayed:
        copy.wait_recv()

    for n, (p, q) in enumerate(TILES):
        tile = o[pl.ds(128 * n, 128), :]
        for ref, part in zip((gh, gm, gl), split(tile)):
            ref[pl.ds(128 * p, 128), pl.ds(128 * q, 128)] = part
        if p != q:
            for ref, part in zip((gh, gm, gl), split(tile.T)):
                ref[pl.ds(128 * q, 128), pl.ds(128 * p, 128)] = part

    def step(n, carry):
        space[...] = orthonormal_t(fine_dot(space[...], gh[...], gm[...], gl[...]))
        return carry

    lax.fori_loop(0, ITERS, step, 0)
    last = space[...]
    small = inner_product(last, fine_dot(last, gh[...], gm[...], gl[...]))
    wh, wm, _ = split(last)
    both = jnp.dot(jnp.concatenate([wh, wm], axis=0), turned_high[...], preferred_element_type=F32)
    product = both[:R2] + (both[R2:] + jnp.dot(wh, turned_low[...], preferred_element_type=F32))
    mapped = fine_dot(inverse_lower(small), *split(product))
    maps[x] = mapped
    far[0] = mapped.astype(BF16)
    copies = [push(far.at[0], far.at[d], at_x(d)) for d in range(1, NX)]
    first = (x * (IB_DEV // NX)).astype(F32)
    for d in range(1, NX):
        copies[d - 1].wait_recv()
        maps[lax.rem(x + NX - d, NX)] = far[d].astype(F32)
    outs = [jnp.zeros((R2, BI), F32) for _ in range(IB_DEV // NX)]
    for n in range(NX):
        for s in range(NB):
            label = jnp.broadcast_to(labels[n][0:1, 32 * s : 32 * s + 1], (R2, BI)) * (1.0 / 32.0) - first
            term = maps[n, :, 128 * s : 128 * s + 128]
            for k in range(IB_DEV // NX):
                outs[k] = outs[k] + jnp.where(label == float(k), term, 0.0)
    for k in range(IB_DEV // NX):
        out_ref[:, 128 * k : 128 * k + 128] = outs[k]
    for copy in started:
        copy.wait_send()


def factor(blocks, coords, counts, slab_b, slab_c, start_t):
    copies = 120
    vmem = pl.BlockSpec(memory_space=pltpu.VMEM)
    hbm = pl.BlockSpec(memory_space=pltpu.HBM)
    return pl.pallas_call(
        factor_kernel,
        out_shape=jax.ShapeDtypeStruct((R2, IB_DEV * BI // NX), F32),
        in_specs=[hbm] * 6,
        out_specs=vmem,
        scratch_shapes=[
            pltpu.SMEM(coords.shape, jnp.int32),
            pltpu.SMEM(counts.shape, jnp.int32),
            pltpu.VMEM((8, 128), jnp.int32),
            pltpu.VMEM(slab_b.shape, BF16),
            pltpu.VMEM(slab_c.shape, BF16),
            pltpu.VMEM(start_t.shape, F32),
            pltpu.VMEM((NB, BI, BJ * BK), BF16),
            pltpu.VMEM((2 * NY * 16, R2, BJ), BF16),
            pltpu.VMEM((2 * NY * 4, R3, 2 * BK), BF16),
            pltpu.VMEM((NZ, 8, 128), jnp.int32),
            pltpu.SMEM((NZ, 8, 128), jnp.int32),
            pltpu.VMEM((NZ - 1, NB, R2, BJ), BF16),
            pltpu.VMEM((NZ - 1, NB // 2, R3, 2 * BK), BF16),
            pltpu.VMEM((NZ * NB, R2, BJ), BF16),
            pltpu.VMEM((NZ * NB // 2, R3, 2 * BK), BF16),
            pltpu.VMEM((NB, R3, BJ, BI), BF16),
            pltpu.VMEM((NB, BI, RR), BF16),
            pltpu.VMEM((RR, NB * BI), BF16),
            pltpu.VMEM((RR, NB * BI), BF16),
            pltpu.VMEM((2, NB, 16, RR), BF16),
            pltpu.VMEM((NX, NB, BI // NX, RR), BF16),
            pltpu.VMEM((NX, 8, 128), jnp.int32),
            pltpu.VMEM((PACKED, 128), F32),
            pltpu.VMEM((PACKED, 128), F32),
            pltpu.VMEM((HALF, 128), F32),
            pltpu.VMEM((3, PART_0 // 4, 128), F32),
            pltpu.VMEM((3, PART_1 // 4, 128), F32),
            pltpu.VMEM((3, PART_0 // 16, 128), F32),
            pltpu.VMEM((3, PART_1 // 16, 128), F32),
            pltpu.VMEM((NZ, HALF // 16, 128), F32),
            pltpu.VMEM((RR, RR), BF16),
            pltpu.VMEM((RR, RR), BF16),
            pltpu.VMEM((RR, RR), BF16),
            pltpu.VMEM((R2, RR), F32),
            pltpu.VMEM((NX, R2, RR), F32),
            pltpu.VMEM((NX, R2, RR), BF16),
            pltpu.SemaphoreType.DMA((copies,)),
            pltpu.SemaphoreType.DMA((copies,)),
            pltpu.SemaphoreType.DMA((NB + 1,)),
            pltpu.SemaphoreType.DMA((5,)),
        ],
        compiler_params=pltpu.CompilerParams(
            collective_id=0, has_side_effects=True, vmem_limit_bytes=53 * 1024 * 1024
        ),
        name="factor",
    )(blocks, coords, counts, slab_b, slab_c, start_t)


def body(blocks, coords, counts, factor_b, factor_c, start):
    hold = functools.partial(pltpu.with_memory_space_constraint, memory_space=pltpu.HBM)
    return factor(blocks, hold(coords), counts, hold(factor_b.T), hold(factor_c.T), hold(start.T)).T


def solution(mesh):
    return jax.shard_map(
        body,
        mesh=mesh,
        in_specs=(
            P(("blk", "rep"), None, None),
            P(None, ("blk", "rep")),
            P(("blk", "rep")),
            P("blk", None),
            P("blk", None),
            P(),
        ),
        out_specs=P(("blk", "rep"), None),
        check_vma=False,
    )
```

```python
import functools

import jax
import jax.numpy as jnp
from jax import lax
from jax.experimental import pallas as pl
from jax.experimental.pallas import tpu as pltpu
from jax.sharding import PartitionSpec as P

BI = 128
BJ = 128
BK = 64
R2 = 32
R3 = 16
RR = 512
IB_DEV = 32
NB = 4
ITERS = 4
NX = 4
NY = 4
NZ = 8
PACKED = 1280
HALF = PACKED // 2
PART_0 = 384
PART_1 = HALF - PART_0
F32 = jnp.float32
BF16 = jnp.bfloat16
TILES = [(a, b) for a in range(4) for b in range(a, 4)]


def dot_nt(left, right):
    return lax.dot_general(left, right, (((1,), (1,)), ((), ())), preferred_element_type=F32)


def dot_tn(left, right):
    return lax.dot_general(left, right, (((0,), (0,)), ((), ())), preferred_element_type=F32)


def iota(shape, dim):
    return lax.broadcasted_iota(jnp.int32, shape, dim)


def fold_slot(held_x, slot, pair, odd, folded):
    pair = pair.astype(F32)
    mode_c = (pair[:, :BK] * (1.0 - odd) + pair[:, BK:] * odd).astype(BF16)
    spread = (iota((128, R3), 0) // 8 == iota((128, R3), 1)).astype(F32).astype(BF16)
    tall = jnp.dot(spread, mode_c, preferred_element_type=F32)
    wide = jnp.concatenate([tall] * 8, axis=1)
    fold_mask = iota((128, 512), 0) % 8 == iota((128, 512), 1) // BK
    fold_t = jnp.where(fold_mask, wide, 0.0).astype(BF16)
    for t in range(8):
        halves = [dot_nt(fold_t, held_x[slot, :, 512 * h : 512 * h + 512]) for h in (2 * t, 2 * t + 1)]
        part = jnp.concatenate([half.reshape(R3, 8, BI) for half in halves], axis=1)
        folded[slot, :, 16 * t : 16 * t + 16, :] = part.astype(BF16)


def contract_slot(folded, slot, block_b, alive):
    none = jnp.zeros((R2, BJ), BF16)
    two = jnp.concatenate(
        [jnp.concatenate([block_b, none], axis=1), jnp.concatenate([none, block_b], axis=1)], axis=0
    )
    parts = [
        jnp.dot(two, folded[slot, 2 * t : 2 * t + 2].reshape(2 * BJ, BI), preferred_element_type=F32)
        for t in range(R3 // 2)
    ]
    return jnp.concatenate(parts, axis=0) * alive


def split(value):
    high = value.astype(BF16)
    rest = value - high.astype(F32)
    middle = rest.astype(BF16)
    low = (rest - middle.astype(F32)).astype(BF16)
    return high, middle, low


def inner_product(left, right):
    lh, lm, ll = split(left)
    rh, rm, rl = split(right)
    return dot_nt(
        jnp.concatenate([lh, lh, lm, lh, ll, lm], axis=1),
        jnp.concatenate([rh, rm, rh, rl, rh, rm], axis=1),
    )


def fine_dot(left, high, middle, low):
    lh, lm, ll = split(left)
    n = left.shape[0]
    first = jnp.dot(jnp.concatenate([lh, lm, ll], axis=0), high, preferred_element_type=F32)
    second = jnp.dot(jnp.concatenate([lh, lm], axis=0), middle, preferred_element_type=F32)
    third = jnp.dot(lh, low, preferred_element_type=F32)
    small = first[2 * n :] + second[n:] + third
    return first[:n] + (first[n : 2 * n] + second[:n] + small)


def inverse_lower(inner):
    n = inner.shape[0]
    unit = (iota((n, n), 0) == iota((n, n), 1)).astype(F32)
    work = jnp.concatenate([inner, unit], axis=1)
    row = iota((n, 2 * n), 0)
    for k in range(0, n, 4):
        columns = [jnp.broadcast_to(work[:, k + t : k + t + 1], (n, 2 * n)) for t in range(4)]
        for t in range(4):
            at = k + t
            inverse = 1.0 / columns[t][at : at + 1]
            for u in range(t + 1, 4):
                columns[u] = columns[u] - columns[t] * (columns[u][at : at + 1] * inverse)
            work = work - jnp.where(row > at, columns[t], 0.0) * (work[at : at + 1] * inverse)
    diagonal = jnp.sum(work[:, :n] * unit, axis=1, keepdims=True)
    return work[:, n:] * lax.rsqrt(diagonal)


def orthonormal_t(value):
    return fine_dot(inverse_lower(inner_product(value, value)), *split(value))


def factor_kernel(
    blocks_ref, coords_hbm, counts_hbm, fb_hbm, fc_hbm, start_hbm, out_ref,
    coords_ref, counts_ref, info_ref, fb_ref, fc_ref, start_ref,
    held_x, plane_b, plane_c, infos, asked, give_b, give_c, got_b, got_c, folded, high_ref, turned_high, turned_low,
    rows, codes, g, o, from_c, from_u0, from_u1, from_v0, from_v1, from_z, gh, gm, gl, space, maps, far, send, recv, load, feed,
):
    b = lax.axis_index("blk")
    x = lax.axis_index("rep")
    c = lax.rem(b, 2)
    y = lax.rem(b // 2, NY)
    z = b // (2 * NY)

    def at_x(d):
        return {"blk": b, "rep": lax.rem(x + d, NX)}

    def at_y(d):
        return {"blk": (z * NY + lax.rem(y + d, NY)) * 2 + c, "rep": x}

    def at_z(d):
        return {"blk": (lax.rem(z + d, NZ) * NY + y) * 2 + c, "rep": x}

    at_c = {"blk": b + 1 - 2 * c, "rep": x}
    partners = [at_x(d) for d in range(1, NX)] + [at_y(d) for d in range(1, NY)]
    partners += [at_z(d) for d in range(1, NZ)] + [at_c]
    loads = [pltpu.make_async_copy(blocks_ref.at[s], held_x.at[s], load.at[s]) for s in range(NB)]
    inputs = (
        (coords_hbm, coords_ref), (counts_hbm, counts_ref), (fc_hbm, fc_ref), (fb_hbm, fb_ref), (start_hbm, start_ref),
    )
    feeds = [pltpu.make_async_copy(a, b, feed.at[n]) for n, (a, b) in enumerate(inputs)]
    for copy in feeds + loads:
        copy.start()
    barrier = pltpu.get_barrier_semaphore()
    for partner in partners:
        pl.semaphore_signal(barrier, inc=1, device_id=partner, device_id_type=pl.DeviceIdType.MESH)

    started = []

    def push(source, target, device):
        k = len(started)
        copy = pltpu.make_async_remote_copy(
            src_ref=source,
            dst_ref=target,
            send_sem=send.at[k],
            recv_sem=recv.at[k],
            device_id=device,
            device_id_type=pl.DeviceIdType.MESH,
        )
        copy.start()
        started.append(copy)
        return copy

    quarter = BI // NX

    feeds[0].wait()
    feeds[1].wait()
    lane = iota((8, 128), 1)
    label_row = lane & 31
    asks = jnp.zeros((8, 128), jnp.int32)
    for s in range(NB):
        label_row += jnp.where(lane >> 5 == s, (coords_ref[0, s] & (IB_DEV - 1)) * 32, 0)
        asks += jnp.where(lane == s, coords_ref[1, s], 0) + jnp.where(lane == NB + s, coords_ref[2, s], 0)
    level = iota((8, 128), 0)
    info_ref[...] = jnp.where(level == 0, label_row, jnp.where(level == 1, asks, 0))

    infos[z] = info_ref[...]
    codes[x] = info_ref[...]
    own = y * 2 + c
    feeds[2].wait()
    for k in range(4):
        plane_c[own * 4 + k] = fc_ref[:, 128 * k : 128 * k + 128]
    feeds[3].wait()
    for k in range(16):
        plane_b[own * 16 + k] = fb_ref[:, 128 * k : 128 * k + 128]
    pl.semaphore_wait(barrier, len(partners))

    wishes = [push(info_ref, infos.at[z], at_z(d)) for d in range(1, NZ)]
    tags = [push(info_ref, codes.at[x], at_x(d)) for d in range(1, NX)]

    planes = ((plane_c, 4), (plane_b, 16))

    def part(n, place):
        plane, count = planes[n]
        return plane.at[pl.ds(pl.multiple_of(place * count, count), count)]

    def half(d, h):
        place = lax.rem(y + d, NY) * 2 + c
        return plane_b.at[pl.ds(pl.multiple_of(place * 16 + 8 * h, 8), 8)]

    along_y = [push(part(0, own), part(0, own), at_y(d)) for d in (2, 1, 3)]
    across_c = [push(part(0, own), part(0, own), at_c)]
    hops = {}
    for d, h in ((1, 0), (3, 1), (1, 1), (3, 0)):
        hops[d, h] = push(half(0, h), half(0, h), at_y(d))
    across_b = [push(part(1, own), part(1, own), at_c)]
    def came(d, h):
        hops[d, h].wait_recv()
        here = half(4 - d, h)
        if (d, h) in ((1, 0), (3, 1)):
            hops[2, h] = push(here, here, at_y(d))
        across_b.append(push(here, here, at_c))

    for k, d in ((1, 1), (2, 3), (0, 2)):
        along_y[k].wait_recv()
        place = lax.rem(y + NY - d, NY) * 2 + c
        across_c.append(push(part(0, place), part(0, place), at_c))
    came(1, 0)
    came(3, 1)
    for copy in wishes:
        copy.wait_recv()
    copy = pltpu.make_async_copy(infos, asked, load.at[NB])
    copy.start()
    copy.wait()
    for copy in across_c:
        copy.wait_recv()

    def answer(pick, count, give, got):
        sent = []
        for d in (0, 4, 3, 5, 2, 6, 1, 7):
            t = lax.rem(z + d, NZ)
            for s in range(count):
                if d == 0:
                    got[z * count + s] = pick(t, s)
                else:
                    give[d - 1, s] = pick(t, s)
            if d > 0:
                target = got.at[pl.ds(pl.multiple_of(z * count, count), count)]
                sent.append((d, push(give.at[d - 1], target, at_z(d))))
        return [copy for _, copy in sorted(sent, key=lambda item: item[0])]

    left_half = iota((R3, 2 * BK), 1) < BK

    def half_c(t, s):
        picked = []
        for n in range(2):
            wish = asked[t, 1, NB + 2 * s + n]
            pair = plane_c[(wish >> 1) & 31].astype(F32)
            swapped = jnp.concatenate([pair[:, BK:], pair[:, :BK]], axis=1)
            move = ((wish & 1) ^ n).astype(F32)
            picked.append(pair * (1.0 - move) + swapped * move)
        return jnp.where(left_half, picked[0], picked[1]).astype(BF16)

    sent_c = answer(half_c, NB // 2, give_c, got_c)
    for d, h in ((1, 1), (3, 0), (2, 0), (2, 1)):
        came(d, h)
    for copy in across_b:
        copy.wait_recv()
    sent_b = answer(lambda t, s: plane_b[asked[t, 1, s] & 127], NB, give_b, got_b)
    for copy in loads:
        copy.wait()
    for copy in sent_c:
        copy.wait_recv()

    def fold_step(s, carry):
        wish = coords_ref[2, s]
        fold_slot(held_x, s, got_c[(wish >> 6) * (NB // 2) + (s >> 1)], (s & 1).astype(F32), folded)
        return carry

    lax.fori_loop(0, NB, fold_step, 0)
    for copy in sent_b:
        copy.wait_recv()

    moves = []

    unit = (iota((BI, BI), 0) == iota((BI, BI), 1)).astype(F32).astype(BF16)
    for s in range(NB):
        alive = jnp.clip(counts_ref[0] - s, 0, 1).astype(F32)
        total = contract_slot(folded, s, got_b[(coords_ref[1, s] >> 7) * NB + s], alive)
        high = total.astype(BF16)
        for k in range(RR // 128):
            turned = dot_nt(unit, high[128 * k : 128 * k + 128])
            high_ref[s, :, 128 * k : 128 * k + 128] = turned.astype(BF16)
        for d in (2, 1, 3):
            there = pl.ds(pl.multiple_of(lax.rem(x + d, NX) * quarter, quarter), quarter)
            moves.append(push(high_ref.at[s, there, :], rows.at[x, s], at_x(d)))
        turned_high[:, 128 * s : 128 * s + 128] = high
        turned_low[:, 128 * s : 128 * s + 128] = (total - high.astype(F32)).astype(BF16)
    rows[x] = high_ref[:, pl.ds(pl.multiple_of(x * quarter, quarter), quarter), :]
    for copy in tags:
        copy.wait_recv()
    labels = [codes[n].astype(F32) for n in range(NX)]
    along = jnp.concatenate([label[0:1, :] for label in labels], axis=1)
    down = jnp.concatenate([label.T[:, 0:1] for label in labels], axis=0)
    same = (down == along).astype(F32).astype(BF16)
    for copy in moves:
        copy.wait_recv()
    held = rows[...].reshape(RR, RR)
    summed = jnp.dot(same, held, preferred_element_type=F32)
    high = summed.astype(BF16)
    low = (summed - high.astype(F32)).astype(BF16)
    at = 0
    for a in range(4):
        left = held[:, 128 * a : 128 * a + 128]
        strip = dot_tn(left, high[:, 128 * a :]) + dot_tn(left, low[:, 128 * a :])
        for n in range(4 - a):
            g[pl.ds(128 * at, 128), :] = strip[:, 128 * n : 128 * n + 128]
            at += 1

    parts = ((0, PART_0, x, y, at_x, at_y, from_u0, from_v0), (PART_0, PART_1, y, x, at_y, at_x, from_u1, from_v1))

    def span(start, count):
        return pl.ds(pl.multiple_of(start, 8), count)

    def chunk(n, core, d):
        off, count, mu = parts[n][:3]
        return span(core * HALF + off + lax.rem(mu + d, 4) * (count // 4), count // 4)

    pieces = [(n, d) for d in (2, 1, 3, 0) for n in range(2)]
    crossed = [push(g.at[chunk(n, 1 - c, d)], from_c.at[chunk(n, 0, d)], at_c) for n, d in pieces]
    outgoing = [[], []]
    for copy, (n, d) in zip(crossed, pieces):
        copy.wait_recv()
        here = chunk(n, c, d)
        g[here, :] += from_c[chunk(n, 0, d), :]
        if d > 0:
            outgoing[n].append(push(g.at[here], parts[n][6].at[d - 1], parts[n][4](d)))

    def small(n, d):
        off, count, mu, mv = parts[n][:4]
        return span(c * HALF + off + mu * (count // 4) + lax.rem(mv + d, 4) * (count // 16), count // 16)

    second = [[], []]
    for n in range(2):
        for copy in outgoing[n]:
            copy.wait_recv()
        here = chunk(n, c, 0)
        got = parts[n][6]
        g[here, :] = g[here, :] + got[0] + got[1] + got[2]
        second[n] = [push(g.at[small(n, d)], parts[n][7].at[d - 1], parts[n][5](d)) for d in (2, 1, 3)]
    summed_z = [[], []]
    for n in range(2):
        for copy in second[n]:
            copy.wait_recv()
        got = parts[n][7]
        at = 0 if n == 0 else PART_0 // 16
        lines = slice(at, at + parts[n][1] // 16)
        from_z[z, lines, :] = g[small(n, 0), :] + got[0] + got[1] + got[2]
        place = from_z.at[z, lines]
        summed_z[n] = [push(place, place, at_z(d)) for d in (4, 3, 5, 2, 6, 1, 7)]
    feeds[4].wait()
    order = (iota((RR, RR), 0) // R3 == iota((RR, RR), 1) % R2) & (iota((RR, RR), 0) % R3 == iota((RR, RR), 1) // R2)
    order = order.astype(F32).astype(BF16)
    moved = jnp.dot(jnp.concatenate(split(start_ref[...]), axis=0), order, preferred_element_type=F32)
    space[...] = orthonormal_t(moved[:R2] + (moved[R2 : 2 * R2] + moved[2 * R2 :]))


    back = [[], []]
    for n in range(2):
        at = 0 if n == 0 else PART_0 // 16
        here = small(n, 0)
        for copy in summed_z[n]:
            copy.wait_recv()
        lines = slice(at, at + parts[n][1] // 16)
        total = from_z[0, lines]
        for k in range(1, NZ):
            total = total + from_z[k, lines]
        o[here, :] = total
        back[n] = [push(o.at[here], o.at[here], parts[n][5](d)) for d in (2, 1, 3)]
    wide_back = [[], []]
    relayed = []
    for n in range(2):
        for copy in back[n]:
            copy.wait_recv()
        here = chunk(n, c, 0)
        wide_back[n] = [push(o.at[here], o.at[here], parts[n][4](d)) for d in (2, 1, 3)]
        relayed.append(push(o.at[here], o.at[here], at_c))
    for k, d in ((1, 1), (2, 3), (0, 2)):
        for n in range(2):
            wide_back[n][k].wait_recv()
            here = chunk(n, c, 4 - d)
            relayed.append(push(o.at[here], o.at[here], at_c))
    for copy in relayed:
        copy.wait_recv()

    for n, (p, q) in enumerate(TILES):
        tile = o[pl.ds(128 * n, 128), :]
        for ref, part in zip((gh, gm, gl), split(tile)):
            ref[pl.ds(128 * p, 128), pl.ds(128 * q, 128)] = part
        if p != q:
            for ref, part in zip((gh, gm, gl), split(tile.T)):
                ref[pl.ds(128 * q, 128), pl.ds(128 * p, 128)] = part

    def step(n, carry):
        space[...] = orthonormal_t(fine_dot(space[...], gh[...], gm[...], gl[...]))
        return carry

    lax.fori_loop(0, ITERS, step, 0)
    last = space[...]
    small = inner_product(last, fine_dot(last, gh[...], gm[...], gl[...]))
    wh, wm, _ = split(last)
    both = jnp.dot(jnp.concatenate([wh, wm], axis=0), turned_high[...], preferred_element_type=F32)
    product = both[:R2] + (both[R2:] + jnp.dot(wh, turned_low[...], preferred_element_type=F32))
    mapped = fine_dot(inverse_lower(small), *split(product))
    maps[x] = mapped
    far[0] = mapped.astype(BF16)
    copies = [push(far.at[0], far.at[d], at_x(d)) for d in range(1, NX)]
    first = (x * (IB_DEV // NX)).astype(F32)
    for d in range(1, NX):
        copies[d - 1].wait_recv()
        maps[lax.rem(x + NX - d, NX)] = far[d].astype(F32)
    outs = [jnp.zeros((R2, BI), F32) for _ in range(IB_DEV // NX)]
    for n in range(NX):
        for s in range(NB):
            label = jnp.broadcast_to(labels[n][0:1, 32 * s : 32 * s + 1], (R2, BI)) * (1.0 / 32.0) - first
            term = maps[n, :, 128 * s : 128 * s + 128]
            for k in range(IB_DEV // NX):
                outs[k] = outs[k] + jnp.where(label == float(k), term, 0.0)
    for k in range(IB_DEV // NX):
        out_ref[:, 128 * k : 128 * k + 128] = outs[k]
    for copy in started:
        copy.wait_send()


def factor(blocks, coords, counts, slab_b, slab_c, start_t):
    copies = 120
    vmem = pl.BlockSpec(memory_space=pltpu.VMEM)
    hbm = pl.BlockSpec(memory_space=pltpu.HBM)
    return pl.pallas_call(
        factor_kernel,
        out_shape=jax.ShapeDtypeStruct((R2, IB_DEV * BI // NX), F32),
        in_specs=[hbm] * 6,
        out_specs=vmem,
        scratch_shapes=[
            pltpu.SMEM(coords.shape, jnp.int32),
            pltpu.SMEM(counts.shape, jnp.int32),
            pltpu.VMEM((8, 128), jnp.int32),
            pltpu.VMEM(slab_b.shape, BF16),
            pltpu.VMEM(slab_c.shape, BF16),
            pltpu.VMEM(start_t.shape, F32),
            pltpu.VMEM((NB, BI, BJ * BK), BF16),
            pltpu.VMEM((2 * NY * 16, R2, BJ), BF16),
            pltpu.VMEM((2 * NY * 4, R3, 2 * BK), BF16),
            pltpu.VMEM((NZ, 8, 128), jnp.int32),
            pltpu.SMEM((NZ, 8, 128), jnp.int32),
            pltpu.VMEM((NZ - 1, NB, R2, BJ), BF16),
            pltpu.VMEM((NZ - 1, NB // 2, R3, 2 * BK), BF16),
            pltpu.VMEM((NZ * NB, R2, BJ), BF16),
            pltpu.VMEM((NZ * NB // 2, R3, 2 * BK), BF16),
            pltpu.VMEM((NB, R3, BJ, BI), BF16),
            pltpu.VMEM((NB, BI, RR), BF16),
            pltpu.VMEM((RR, NB * BI), BF16),
            pltpu.VMEM((RR, NB * BI), BF16),
            pltpu.VMEM((NX, NB, BI // NX, RR), BF16),
            pltpu.VMEM((NX, 8, 128), jnp.int32),
            pltpu.VMEM((PACKED, 128), F32),
            pltpu.VMEM((PACKED, 128), F32),
            pltpu.VMEM((HALF, 128), F32),
            pltpu.VMEM((3, PART_0 // 4, 128), F32),
            pltpu.VMEM((3, PART_1 // 4, 128), F32),
            pltpu.VMEM((3, PART_0 // 16, 128), F32),
            pltpu.VMEM((3, PART_1 // 16, 128), F32),
            pltpu.VMEM((NZ, HALF // 16, 128), F32),
            pltpu.VMEM((RR, RR), BF16),
            pltpu.VMEM((RR, RR), BF16),
            pltpu.VMEM((RR, RR), BF16),
            pltpu.VMEM((R2, RR), F32),
            pltpu.VMEM((NX, R2, RR), F32),
            pltpu.VMEM((NX, R2, RR), BF16),
            pltpu.SemaphoreType.DMA((copies,)),
            pltpu.SemaphoreType.DMA((copies,)),
            pltpu.SemaphoreType.DMA((NB + 1,)),
            pltpu.SemaphoreType.DMA((5,)),
        ],
        compiler_params=pltpu.CompilerParams(
            collective_id=0, has_side_effects=True, vmem_limit_bytes=53 * 1024 * 1024
        ),
        name="factor",
    )(blocks, coords, counts, slab_b, slab_c, start_t)


def body(blocks, coords, counts, factor_b, factor_c, start):
    hold = functools.partial(pltpu.with_memory_space_constraint, memory_space=pltpu.HBM)
    return factor(blocks, hold(coords), counts, hold(factor_b.T), hold(factor_c.T), hold(start.T)).T


def solution(mesh):
    return jax.shard_map(
        body,
        mesh=mesh,
        in_specs=(
            P(("blk", "rep"), None, None),
            P(None, ("blk", "rep")),
            P(("blk", "rep")),
            P("blk", None),
            P("blk", None),
            P(),
        ),
        out_specs=P(("blk", "rep"), None),
        check_vma=False,
    )
```

```python
import functools

import jax
import jax.numpy as jnp
from jax import lax
from jax.experimental import pallas as pl
from jax.experimental.pallas import tpu as pltpu
from jax.sharding import PartitionSpec as P

BI = 128
BJ = 128
BK = 64
R2 = 32
R3 = 16
RR = 512
IB_DEV = 32
NB = 4
ITERS = 4
NX = 4
NY = 4
NZ = 8
PACKED = 1280
HALF = PACKED // 2
PART_0 = 384
PART_1 = HALF - PART_0
F32 = jnp.float32
BF16 = jnp.bfloat16
TILES = [(a, b) for a in range(4) for b in range(a, 4)]


def dot_nt(left, right):
    return lax.dot_general(left, right, (((1,), (1,)), ((), ())), preferred_element_type=F32)


def dot_tn(left, right):
    return lax.dot_general(left, right, (((0,), (0,)), ((), ())), preferred_element_type=F32)


def iota(shape, dim):
    return lax.broadcasted_iota(jnp.int32, shape, dim)


def fold_slot(held_x, slot, pair, odd, folded):
    pair = pair.astype(F32)
    mode_c = (pair[:, :BK] * (1.0 - odd) + pair[:, BK:] * odd).astype(BF16)
    spread = (iota((128, R3), 0) // 8 == iota((128, R3), 1)).astype(F32).astype(BF16)
    tall = jnp.dot(spread, mode_c, preferred_element_type=F32)
    wide = jnp.concatenate([tall] * 8, axis=1)
    fold_mask = iota((128, 512), 0) % 8 == iota((128, 512), 1) // BK
    fold_t = jnp.where(fold_mask, wide, 0.0).astype(BF16)
    for t in range(8):
        halves = [dot_nt(fold_t, held_x[slot, :, 512 * h : 512 * h + 512]) for h in (2 * t, 2 * t + 1)]
        part = jnp.concatenate([half.reshape(R3, 8, BI) for half in halves], axis=1)
        folded[slot, :, 16 * t : 16 * t + 16, :] = part.astype(BF16)


def contract_slot(folded, slot, block_b, alive):
    none = jnp.zeros((R2, BJ), BF16)
    two = jnp.concatenate(
        [jnp.concatenate([block_b, none], axis=1), jnp.concatenate([none, block_b], axis=1)], axis=0
    )
    parts = [
        jnp.dot(two, folded[slot, 2 * t : 2 * t + 2].reshape(2 * BJ, BI), preferred_element_type=F32)
        for t in range(R3 // 2)
    ]
    return jnp.concatenate(parts, axis=0) * alive


def split(value):
    high = value.astype(BF16)
    rest = value - high.astype(F32)
    middle = rest.astype(BF16)
    low = (rest - middle.astype(F32)).astype(BF16)
    return high, middle, low


def inner_product(left, right):
    lh, lm, ll = split(left)
    rh, rm, rl = split(right)
    return dot_nt(
        jnp.concatenate([lh, lh, lm, lh, ll, lm], axis=1),
        jnp.concatenate([rh, rm, rh, rl, rh, rm], axis=1),
    )


def fine_dot(left, high, middle, low):
    lh, lm, ll = split(left)
    n = left.shape[0]
    first = jnp.dot(jnp.concatenate([lh, lm, ll], axis=0), high, preferred_element_type=F32)
    second = jnp.dot(jnp.concatenate([lh, lm], axis=0), middle, preferred_element_type=F32)
    third = jnp.dot(lh, low, preferred_element_type=F32)
    small = first[2 * n :] + second[n:] + third
    return first[:n] + (first[n : 2 * n] + second[:n] + small)


def inverse_lower(inner):
    n = inner.shape[0]
    unit = (iota((n, n), 0) == iota((n, n), 1)).astype(F32)
    work = jnp.concatenate([inner, unit], axis=1)
    row = iota((n, 2 * n), 0)
    for k in range(0, n, 4):
        columns = [jnp.broadcast_to(work[:, k + t : k + t + 1], (n, 2 * n)) for t in range(4)]
        for t in range(4):
            at = k + t
            inverse = 1.0 / columns[t][at : at + 1]
            for u in range(t + 1, 4):
                columns[u] = columns[u] - columns[t] * (columns[u][at : at + 1] * inverse)
            work = work - jnp.where(row > at, columns[t], 0.0) * (work[at : at + 1] * inverse)
    diagonal = jnp.sum(work[:, :n] * unit, axis=1, keepdims=True)
    return work[:, n:] * lax.rsqrt(diagonal)


def orthonormal_t(value):
    return fine_dot(inverse_lower(inner_product(value, value)), *split(value))


def factor_kernel(
    blocks_ref, coords_hbm, counts_hbm, fb_hbm, fc_hbm, start_hbm, out_ref,
    coords_ref, counts_ref, info_ref, fb_ref, fc_ref, start_ref,
    held_x, plane_b, plane_c, infos, asked, give_b, give_c, got_b, got_c, folded, high_ref, turned_high, turned_low,
    rows, codes, g, o, from_c, from_u0, from_u1, from_v0, from_v1, from_z, gh, gm, gl, space, maps, far, send, recv, load, feed,
):
    b = lax.axis_index("blk")
    x = lax.axis_index("rep")
    c = lax.rem(b, 2)
    y = lax.rem(b // 2, NY)
    z = b // (2 * NY)

    def at_x(d):
        return {"blk": b, "rep": lax.rem(x + d, NX)}

    def at_y(d):
        return {"blk": (z * NY + lax.rem(y + d, NY)) * 2 + c, "rep": x}

    def at_z(d):
        return {"blk": (lax.rem(z + d, NZ) * NY + y) * 2 + c, "rep": x}

    at_c = {"blk": b + 1 - 2 * c, "rep": x}
    partners = [at_x(d) for d in range(1, NX)] + [at_y(d) for d in range(1, NY)]
    partners += [at_z(d) for d in range(1, NZ)] + [at_c]
    loads = [pltpu.make_async_copy(blocks_ref.at[s], held_x.at[s], load.at[s]) for s in range(NB)]
    inputs = (
        (coords_hbm, coords_ref), (counts_hbm, counts_ref), (fc_hbm, fc_ref), (fb_hbm, fb_ref), (start_hbm, start_ref),
    )
    feeds = [pltpu.make_async_copy(a, b, feed.at[n]) for n, (a, b) in enumerate(inputs)]
    for copy in feeds + loads:
        copy.start()
    barrier = pltpu.get_barrier_semaphore()
    for partner in partners:
        pl.semaphore_signal(barrier, inc=1, device_id=partner, device_id_type=pl.DeviceIdType.MESH)

    started = []

    def push(source, target, device):
        k = len(started)
        copy = pltpu.make_async_remote_copy(
            src_ref=source,
            dst_ref=target,
            send_sem=send.at[k],
            recv_sem=recv.at[k],
            device_id=device,
            device_id_type=pl.DeviceIdType.MESH,
        )
        copy.start()
        started.append(copy)
        return copy

    quarter = BI // NX

    feeds[0].wait()
    feeds[1].wait()
    lane = iota((8, 128), 1)
    label_row = lane & 31
    asks = jnp.zeros((8, 128), jnp.int32)
    for s in range(NB):
        label_row += jnp.where(lane >> 5 == s, (coords_ref[0, s] & (IB_DEV - 1)) * 32, 0)
        asks += jnp.where(lane == s, coords_ref[1, s], 0) + jnp.where(lane == NB + s, coords_ref[2, s], 0)
    level = iota((8, 128), 0)
    info_ref[...] = jnp.where(level == 0, label_row, jnp.where(level == 1, asks, 0))

    infos[z] = info_ref[...]
    codes[x] = info_ref[...]
    own = y * 2 + c
    feeds[2].wait()
    for k in range(4):
        plane_c[own * 4 + k] = fc_ref[:, 128 * k : 128 * k + 128]
    feeds[3].wait()
    for k in range(16):
        plane_b[own * 16 + k] = fb_ref[:, 128 * k : 128 * k + 128]
    pl.semaphore_wait(barrier, len(partners))

    planes = ((plane_c, 4), (plane_b, 16))

    def part(n, place):
        plane, count = planes[n]
        return plane.at[pl.ds(pl.multiple_of(place * count, count), count)]

    def half(d, h):
        place = lax.rem(y + d, NY) * 2 + c
        return plane_b.at[pl.ds(pl.multiple_of(place * 16 + 8 * h, 8), 8)]

    along_y = [push(part(0, own), part(0, own), at_y(d)) for d in (2, 1, 3)]
    across_c = [push(part(0, own), part(0, own), at_c)]
    wishes = [push(info_ref, infos.at[z], at_z(d)) for d in (4, 3, 5, 2, 6, 1, 7)]
    hops = {}
    for d, h in ((1, 0), (3, 1), (1, 1), (3, 0)):
        hops[d, h] = push(half(0, h), half(0, h), at_y(d))
    across_b = [push(part(1, own), part(1, own), at_c)]
    tags = [push(info_ref, codes.at[x], at_x(d)) for d in range(1, NX)]

    def came(d, h):
        hops[d, h].wait_recv()
        here = half(4 - d, h)
        if (d, h) in ((1, 0), (3, 1)):
            hops[2, h] = push(here, here, at_y(d))
        across_b.append(push(here, here, at_c))

    for k, d in ((1, 1), (2, 3), (0, 2)):
        along_y[k].wait_recv()
        place = lax.rem(y + NY - d, NY) * 2 + c
        across_c.append(push(part(0, place), part(0, place), at_c))
    came(1, 0)
    came(3, 1)
    for copy in wishes:
        copy.wait_recv()
    copy = pltpu.make_async_copy(infos, asked, load.at[NB])
    copy.start()
    copy.wait()
    for copy in across_c:
        copy.wait_recv()

    def answer(pick, count, give, got):
        sent = []
        for d in (0, 4, 3, 5, 2, 6, 1, 7):
            t = lax.rem(z + d, NZ)
            for s in range(count):
                if d == 0:
                    got[z * count + s] = pick(t, s)
                else:
                    give[d - 1, s] = pick(t, s)
            if d > 0:
                target = got.at[pl.ds(pl.multiple_of(z * count, count), count)]
                sent.append((d, push(give.at[d - 1], target, at_z(d))))
        return [copy for _, copy in sorted(sent, key=lambda item: item[0])]

    left_half = iota((R3, 2 * BK), 1) < BK

    def half_c(t, s):
        picked = []
        for n in range(2):
            wish = asked[t, 1, NB + 2 * s + n]
            pair = plane_c[(wish >> 1) & 31].astype(F32)
            swapped = jnp.concatenate([pair[:, BK:], pair[:, :BK]], axis=1)
            move = ((wish & 1) ^ n).astype(F32)
            picked.append(pair * (1.0 - move) + swapped * move)
        return jnp.where(left_half, picked[0], picked[1]).astype(BF16)

    sent_c = answer(half_c, NB // 2, give_c, got_c)
    for d, h in ((1, 1), (3, 0), (2, 0), (2, 1)):
        came(d, h)
    for copy in across_b:
        copy.wait_recv()
    sent_b = answer(lambda t, s: plane_b[asked[t, 1, s] & 127], NB, give_b, got_b)
    for copy in loads:
        copy.wait()
    for copy in sent_c:
        copy.wait_recv()

    def fold_step(s, carry):
        wish = coords_ref[2, s]
        fold_slot(held_x, s, got_c[(wish >> 6) * (NB // 2) + (s >> 1)], (s & 1).astype(F32), folded)
        return carry

    lax.fori_loop(0, NB, fold_step, 0)
    for copy in sent_b:
        copy.wait_recv()

    moves = []

    unit = (iota((BI, BI), 0) == iota((BI, BI), 1)).astype(F32).astype(BF16)
    for s in range(NB):
        alive = jnp.clip(counts_ref[0] - s, 0, 1).astype(F32)
        total = contract_slot(folded, s, got_b[(coords_ref[1, s] >> 7) * NB + s], alive)
        high = total.astype(BF16)
        for k in range(RR // 128):
            turned = dot_nt(unit, high[128 * k : 128 * k + 128])
            high_ref[s, :, 128 * k : 128 * k + 128] = turned.astype(BF16)
        for d in (2, 1, 3):
            there = pl.ds(pl.multiple_of(lax.rem(x + d, NX) * quarter, quarter), quarter)
            moves.append(push(high_ref.at[s, there, :], rows.at[x, s], at_x(d)))
        turned_high[:, 128 * s : 128 * s + 128] = high
        turned_low[:, 128 * s : 128 * s + 128] = (total - high.astype(F32)).astype(BF16)
    rows[x] = high_ref[:, pl.ds(pl.multiple_of(x * quarter, quarter), quarter), :]
    for copy in tags:
        copy.wait_recv()
    labels = [codes[n].astype(F32) for n in range(NX)]
    along = jnp.concatenate([label[0:1, :] for label in labels], axis=1)
    down = jnp.concatenate([label.T[:, 0:1] for label in labels], axis=0)
    same = (down == along).astype(F32).astype(BF16)
    for copy in moves:
        copy.wait_recv()
    held = rows[...].reshape(RR, RR)
    summed = jnp.dot(same, held, preferred_element_type=F32)
    high = summed.astype(BF16)
    low = (summed - high.astype(F32)).astype(BF16)
    at = 0
    for a in range(4):
        left = held[:, 128 * a : 128 * a + 128]
        strip = dot_tn(left, high[:, 128 * a :]) + dot_tn(left, low[:, 128 * a :])
        for n in range(4 - a):
            g[pl.ds(128 * at, 128), :] = strip[:, 128 * n : 128 * n + 128]
            at += 1

    parts = ((0, PART_0, x, y, at_x, at_y, from_u0, from_v0), (PART_0, PART_1, y, x, at_y, at_x, from_u1, from_v1))

    def span(start, count):
        return pl.ds(pl.multiple_of(start, 8), count)

    def chunk(n, core, d):
        off, count, mu = parts[n][:3]
        return span(core * HALF + off + lax.rem(mu + d, 4) * (count // 4), count // 4)

    pieces = [(n, d) for d in (2, 1, 3, 0) for n in range(2)]
    crossed = [push(g.at[chunk(n, 1 - c, d)], from_c.at[chunk(n, 0, d)], at_c) for n, d in pieces]
    outgoing = [[], []]
    for copy, (n, d) in zip(crossed, pieces):
        copy.wait_recv()
        here = chunk(n, c, d)
        g[here, :] += from_c[chunk(n, 0, d), :]
        if d > 0:
            outgoing[n].append(push(g.at[here], parts[n][6].at[d - 1], parts[n][4](d)))

    def small(n, d):
        off, count, mu, mv = parts[n][:4]
        return span(c * HALF + off + mu * (count // 4) + lax.rem(mv + d, 4) * (count // 16), count // 16)

    second = [[], []]
    for n in range(2):
        for copy in outgoing[n]:
            copy.wait_recv()
        here = chunk(n, c, 0)
        got = parts[n][6]
        g[here, :] = g[here, :] + got[0] + got[1] + got[2]
        second[n] = [push(g.at[small(n, d)], parts[n][7].at[d - 1], parts[n][5](d)) for d in (2, 1, 3)]
    summed_z = [[], []]
    for n in range(2):
        for copy in second[n]:
            copy.wait_recv()
        got = parts[n][7]
        at = 0 if n == 0 else PART_0 // 16
        lines = slice(at, at + parts[n][1] // 16)
        from_z[z, lines, :] = g[small(n, 0), :] + got[0] + got[1] + got[2]
        place = from_z.at[z, lines]
        summed_z[n] = [push(place, place, at_z(d)) for d in (4, 3, 5, 2, 6, 1, 7)]
    feeds[4].wait()
    order = (iota((RR, RR), 0) // R3 == iota((RR, RR), 1) % R2) & (iota((RR, RR), 0) % R3 == iota((RR, RR), 1) // R2)
    order = order.astype(F32).astype(BF16)
    moved = jnp.dot(jnp.concatenate(split(start_ref[...]), axis=0), order, preferred_element_type=F32)
    space[...] = orthonormal_t(moved[:R2] + (moved[R2 : 2 * R2] + moved[2 * R2 :]))


    back = [[], []]
    for n in range(2):
        at = 0 if n == 0 else PART_0 // 16
        here = small(n, 0)
        for copy in summed_z[n]:
            copy.wait_recv()
        lines = slice(at, at + parts[n][1] // 16)
        total = from_z[0, lines]
        for k in range(1, NZ):
            total = total + from_z[k, lines]
        o[here, :] = total
        back[n] = [push(o.at[here], o.at[here], parts[n][5](d)) for d in (2, 1, 3)]
    wide_back = [[], []]
    relayed = []
    for n in range(2):
        for copy in back[n]:
            copy.wait_recv()
        here = chunk(n, c, 0)
        wide_back[n] = [push(o.at[here], o.at[here], parts[n][4](d)) for d in (2, 1, 3)]
        relayed.append(push(o.at[here], o.at[here], at_c))
    for k, d in ((1, 1), (2, 3), (0, 2)):
        for n in range(2):
            wide_back[n][k].wait_recv()
            here = chunk(n, c, 4 - d)
            relayed.append(push(o.at[here], o.at[here], at_c))
    for copy in relayed:
        copy.wait_recv()

    for n, (p, q) in enumerate(TILES):
        tile = o[pl.ds(128 * n, 128), :]
        for ref, part in zip((gh, gm, gl), split(tile)):
            ref[pl.ds(128 * p, 128), pl.ds(128 * q, 128)] = part
        if p != q:
            for ref, part in zip((gh, gm, gl), split(tile.T)):
                ref[pl.ds(128 * q, 128), pl.ds(128 * p, 128)] = part

    def step(n, carry):
        space[...] = orthonormal_t(fine_dot(space[...], gh[...], gm[...], gl[...]))
        return carry

    lax.fori_loop(0, ITERS, step, 0)
    last = space[...]
    small = inner_product(last, fine_dot(last, gh[...], gm[...], gl[...]))
    wh, wm, _ = split(last)
    both = jnp.dot(jnp.concatenate([wh, wm], axis=0), turned_high[...], preferred_element_type=F32)
    product = both[:R2] + (both[R2:] + jnp.dot(wh, turned_low[...], preferred_element_type=F32))
    mapped = fine_dot(inverse_lower(small), *split(product))
    maps[x] = mapped
    far[0] = mapped.astype(BF16)
    copies = [push(far.at[0], far.at[d], at_x(d)) for d in range(1, NX)]
    first = (x * (IB_DEV // NX)).astype(F32)
    for d in range(1, NX):
        copies[d - 1].wait_recv()
        maps[lax.rem(x + NX - d, NX)] = far[d].astype(F32)
    outs = [jnp.zeros((R2, BI), F32) for _ in range(IB_DEV // NX)]
    for n in range(NX):
        for s in range(NB):
            label = jnp.broadcast_to(labels[n][0:1, 32 * s : 32 * s + 1], (R2, BI)) * (1.0 / 32.0) - first
            term = maps[n, :, 128 * s : 128 * s + 128]
            for k in range(IB_DEV // NX):
                outs[k] = outs[k] + jnp.where(label == float(k), term, 0.0)
    for k in range(IB_DEV // NX):
        out_ref[:, 128 * k : 128 * k + 128] = outs[k]
    for copy in started:
        copy.wait_send()


def factor(blocks, coords, counts, slab_b, slab_c, start_t):
    copies = 120
    vmem = pl.BlockSpec(memory_space=pltpu.VMEM)
    hbm = pl.BlockSpec(memory_space=pltpu.HBM)
    return pl.pallas_call(
        factor_kernel,
        out_shape=jax.ShapeDtypeStruct((R2, IB_DEV * BI // NX), F32),
        in_specs=[hbm] * 6,
        out_specs=vmem,
        scratch_shapes=[
            pltpu.SMEM(coords.shape, jnp.int32),
            pltpu.SMEM(counts.shape, jnp.int32),
            pltpu.VMEM((8, 128), jnp.int32),
            pltpu.VMEM(slab_b.shape, BF16),
            pltpu.VMEM(slab_c.shape, BF16),
            pltpu.VMEM(start_t.shape, F32),
            pltpu.VMEM((NB, BI, BJ * BK), BF16),
            pltpu.VMEM((2 * NY * 16, R2, BJ), BF16),
            pltpu.VMEM((2 * NY * 4, R3, 2 * BK), BF16),
            pltpu.VMEM((NZ, 8, 128), jnp.int32),
            pltpu.SMEM((NZ, 8, 128), jnp.int32),
            pltpu.VMEM((NZ - 1, NB, R2, BJ), BF16),
            pltpu.VMEM((NZ - 1, NB // 2, R3, 2 * BK), BF16),
            pltpu.VMEM((NZ * NB, R2, BJ), BF16),
            pltpu.VMEM((NZ * NB // 2, R3, 2 * BK), BF16),
            pltpu.VMEM((NB, R3, BJ, BI), BF16),
            pltpu.VMEM((NB, BI, RR), BF16),
            pltpu.VMEM((RR, NB * BI), BF16),
            pltpu.VMEM((RR, NB * BI), BF16),
            pltpu.VMEM((NX, NB, BI // NX, RR), BF16),
            pltpu.VMEM((NX, 8, 128), jnp.int32),
            pltpu.VMEM((PACKED, 128), F32),
            pltpu.VMEM((PACKED, 128), F32),
            pltpu.VMEM((HALF, 128), F32),
            pltpu.VMEM((3, PART_0 // 4, 128), F32),
            pltpu.VMEM((3, PART_1 // 4, 128), F32),
            pltpu.VMEM((3, PART_0 // 16, 128), F32),
            pltpu.VMEM((3, PART_1 // 16, 128), F32),
            pltpu.VMEM((NZ, HALF // 16, 128), F32),
            pltpu.VMEM((RR, RR), BF16),
            pltpu.VMEM((RR, RR), BF16),
            pltpu.VMEM((RR, RR), BF16),
            pltpu.VMEM((R2, RR), F32),
            pltpu.VMEM((NX, R2, RR), F32),
            pltpu.VMEM((NX, R2, RR), BF16),
            pltpu.SemaphoreType.DMA((copies,)),
            pltpu.SemaphoreType.DMA((copies,)),
            pltpu.SemaphoreType.DMA((NB + 1,)),
            pltpu.SemaphoreType.DMA((5,)),
        ],
        compiler_params=pltpu.CompilerParams(
            collective_id=0, has_side_effects=True, vmem_limit_bytes=53 * 1024 * 1024
        ),
        name="factor",
    )(blocks, coords, counts, slab_b, slab_c, start_t)


def body(blocks, coords, counts, factor_b, factor_c, start):
    hold = functools.partial(pltpu.with_memory_space_constraint, memory_space=pltpu.HBM)
    return factor(blocks, hold(coords), counts, hold(factor_b.T), hold(factor_c.T), hold(start.T)).T


def solution(mesh):
    return jax.shard_map(
        body,
        mesh=mesh,
        in_specs=(
            P(("blk", "rep"), None, None),
            P(None, ("blk", "rep")),
            P(("blk", "rep")),
            P("blk", None),
            P("blk", None),
            P(),
        ),
        out_specs=P(("blk", "rep"), None),
        check_vma=False,
    )
```

```python
import functools

import jax
import jax.numpy as jnp
from jax import lax
from jax.experimental import pallas as pl
from jax.experimental.pallas import tpu as pltpu
from jax.sharding import PartitionSpec as P

BI = 128
BJ = 128
BK = 64
R2 = 32
R3 = 16
RR = 512
IB_DEV = 32
NB = 4
ITERS = 4
NX = 4
NY = 4
NZ = 8
PACKED = 1280
HALF = PACKED // 2
PART_0 = 384
PART_1 = HALF - PART_0
F32 = jnp.float32
BF16 = jnp.bfloat16
TILES = [(a, b) for a in range(4) for b in range(a, 4)]


def dot_nt(left, right):
    return lax.dot_general(left, right, (((1,), (1,)), ((), ())), preferred_element_type=F32)


def dot_tn(left, right):
    return lax.dot_general(left, right, (((0,), (0,)), ((), ())), preferred_element_type=F32)


def iota(shape, dim):
    return lax.broadcasted_iota(jnp.int32, shape, dim)


def fold_slot(held_x, slot, pair, odd, folded):
    pair = pair.astype(F32)
    mode_c = (pair[:, :BK] * (1.0 - odd) + pair[:, BK:] * odd).astype(BF16)
    spread = (iota((128, R3), 0) // 8 == iota((128, R3), 1)).astype(F32).astype(BF16)
    tall = jnp.dot(spread, mode_c, preferred_element_type=F32)
    wide = jnp.concatenate([tall] * 8, axis=1)
    fold_mask = iota((128, 512), 0) % 8 == iota((128, 512), 1) // BK
    fold_t = jnp.where(fold_mask, wide, 0.0).astype(BF16)
    for t in range(8):
        halves = [dot_nt(fold_t, held_x[slot, :, 512 * h : 512 * h + 512]) for h in (2 * t, 2 * t + 1)]
        part = jnp.concatenate([half.reshape(R3, 8, BI) for half in halves], axis=1)
        folded[slot, :, 16 * t : 16 * t + 16, :] = part.astype(BF16)


def contract_slot(folded, slot, block_b, alive):
    none = jnp.zeros((R2, BJ), BF16)
    two = jnp.concatenate(
        [jnp.concatenate([block_b, none], axis=1), jnp.concatenate([none, block_b], axis=1)], axis=0
    )
    parts = [
        jnp.dot(two, folded[slot, 2 * t : 2 * t + 2].reshape(2 * BJ, BI), preferred_element_type=F32)
        for t in range(R3 // 2)
    ]
    return jnp.concatenate(parts, axis=0) * alive


def split(value):
    high = value.astype(BF16)
    rest = value - high.astype(F32)
    middle = rest.astype(BF16)
    low = (rest - middle.astype(F32)).astype(BF16)
    return high, middle, low


def inner_product(left, right):
    lh, lm, ll = split(left)
    rh, rm, rl = split(right)
    return dot_nt(
        jnp.concatenate([lh, lh, lm, lh, ll, lm], axis=1),
        jnp.concatenate([rh, rm, rh, rl, rh, rm], axis=1),
    )


def fine_dot(left, high, middle, low):
    lh, lm, ll = split(left)
    n = left.shape[0]
    first = jnp.dot(jnp.concatenate([lh, lm, ll], axis=0), high, preferred_element_type=F32)
    second = jnp.dot(jnp.concatenate([lh, lm], axis=0), middle, preferred_element_type=F32)
    third = jnp.dot(lh, low, preferred_element_type=F32)
    small = first[2 * n :] + second[n:] + third
    return first[:n] + (first[n : 2 * n] + second[:n] + small)


def inverse_lower(inner):
    n = inner.shape[0]
    unit = (iota((n, n), 0) == iota((n, n), 1)).astype(F32)
    work = jnp.concatenate([inner, unit], axis=1)
    row = iota((n, 2 * n), 0)
    for k in range(0, n, 4):
        columns = [jnp.broadcast_to(work[:, k + t : k + t + 1], (n, 2 * n)) for t in range(4)]
        for t in range(4):
            at = k + t
            inverse = 1.0 / columns[t][at : at + 1]
            for u in range(t + 1, 4):
                columns[u] = columns[u] - columns[t] * (columns[u][at : at + 1] * inverse)
            work = work - jnp.where(row > at, columns[t], 0.0) * (work[at : at + 1] * inverse)
    diagonal = jnp.sum(work[:, :n] * unit, axis=1, keepdims=True)
    return work[:, n:] * lax.rsqrt(diagonal)


def orthonormal_t(value):
    return fine_dot(inverse_lower(inner_product(value, value)), *split(value))


def factor_kernel(
    blocks_ref, coords_hbm, counts_hbm, fb_hbm, fc_hbm, start_hbm, out_ref,
    coords_ref, counts_ref, info_ref, fb_ref, fc_ref, start_ref,
    held_x, plane_b, plane_c, infos, asked, give_b, give_c, got_b, got_c, folded, high_ref, turned_high, turned_low,
    rows, codes, g, o, from_c, from_u0, from_u1, from_v0, from_v1, from_z, gh, gm, gl, space, maps, send, recv, load, feed,
):
    b = lax.axis_index("blk")
    x = lax.axis_index("rep")
    c = lax.rem(b, 2)
    y = lax.rem(b // 2, NY)
    z = b // (2 * NY)

    def at_x(d):
        return {"blk": b, "rep": lax.rem(x + d, NX)}

    def at_y(d):
        return {"blk": (z * NY + lax.rem(y + d, NY)) * 2 + c, "rep": x}

    def at_z(d):
        return {"blk": (lax.rem(z + d, NZ) * NY + y) * 2 + c, "rep": x}

    at_c = {"blk": b + 1 - 2 * c, "rep": x}
    partners = [at_x(d) for d in range(1, NX)] + [at_y(d) for d in range(1, NY)]
    partners += [at_z(d) for d in range(1, NZ)] + [at_c]
    loads = [pltpu.make_async_copy(blocks_ref.at[s], held_x.at[s], load.at[s]) for s in range(NB)]
    inputs = (
        (coords_hbm, coords_ref), (counts_hbm, counts_ref), (fc_hbm, fc_ref), (fb_hbm, fb_ref), (start_hbm, start_ref),
    )
    feeds = [pltpu.make_async_copy(a, b, feed.at[n]) for n, (a, b) in enumerate(inputs)]
    for copy in feeds + loads:
        copy.start()
    barrier = pltpu.get_barrier_semaphore()
    for partner in partners:
        pl.semaphore_signal(barrier, inc=1, device_id=partner, device_id_type=pl.DeviceIdType.MESH)

    started = []

    def push(source, target, device):
        k = len(started)
        copy = pltpu.make_async_remote_copy(
            src_ref=source,
            dst_ref=target,
            send_sem=send.at[k],
            recv_sem=recv.at[k],
            device_id=device,
            device_id_type=pl.DeviceIdType.MESH,
        )
        copy.start()
        started.append(copy)
        return copy

    quarter = BI // NX

    feeds[0].wait()
    feeds[1].wait()
    lane = iota((8, 128), 1)
    label_row = lane & 31
    asks = jnp.zeros((8, 128), jnp.int32)
    for s in range(NB):
        label_row += jnp.where(lane >> 5 == s, (coords_ref[0, s] & (IB_DEV - 1)) * 32, 0)
        asks += jnp.where(lane == s, coords_ref[1, s], 0) + jnp.where(lane == NB + s, coords_ref[2, s], 0)
    level = iota((8, 128), 0)
    info_ref[...] = jnp.where(level == 0, label_row, jnp.where(level == 1, asks, 0))

    infos[z] = info_ref[...]
    codes[x] = info_ref[...]
    own = y * 2 + c
    feeds[2].wait()
    for k in range(4):
        plane_c[own * 4 + k] = fc_ref[:, 128 * k : 128 * k + 128]
    feeds[3].wait()
    for k in range(16):
        plane_b[own * 16 + k] = fb_ref[:, 128 * k : 128 * k + 128]
    pl.semaphore_wait(barrier, len(partners))

    planes = ((plane_c, 4), (plane_b, 16))

    def part(n, place):
        plane, count = planes[n]
        return plane.at[pl.ds(pl.multiple_of(place * count, count), count)]

    def half(d, h):
        place = lax.rem(y + d, NY) * 2 + c
        return plane_b.at[pl.ds(pl.multiple_of(place * 16 + 8 * h, 8), 8)]

    along_y = [push(part(0, own), part(0, own), at_y(d)) for d in (2, 1, 3)]
    across_c = [push(part(0, own), part(0, own), at_c)]
    wishes = [push(info_ref, infos.at[z], at_z(d)) for d in (4, 3, 5, 2, 6, 1, 7)]
    hops = {}
    for d, h in ((1, 0), (3, 1), (1, 1), (3, 0)):
        hops[d, h] = push(half(0, h), half(0, h), at_y(d))
    across_b = [push(part(1, own), part(1, own), at_c)]
    tags = [push(info_ref, codes.at[x], at_x(d)) for d in range(1, NX)]

    def came(d, h):
        hops[d, h].wait_recv()
        here = half(4 - d, h)
        if (d, h) in ((1, 0), (3, 1)):
            hops[2, h] = push(here, here, at_y(d))
        across_b.append(push(here, here, at_c))

    for k, d in ((1, 1), (2, 3), (0, 2)):
        along_y[k].wait_recv()
        place = lax.rem(y + NY - d, NY) * 2 + c
        across_c.append(push(part(0, place), part(0, place), at_c))
    came(1, 0)
    came(3, 1)
    for copy in wishes:
        copy.wait_recv()
    copy = pltpu.make_async_copy(infos, asked, load.at[NB])
    copy.start()
    copy.wait()
    for copy in across_c:
        copy.wait_recv()

    def answer(pick, count, give, got):
        sent = []
        for d in (0, 4, 3, 5, 2, 6, 1, 7):
            t = lax.rem(z + d, NZ)
            for s in range(count):
                if d == 0:
                    got[z * count + s] = pick(t, s)
                else:
                    give[d - 1, s] = pick(t, s)
            if d > 0:
                target = got.at[pl.ds(pl.multiple_of(z * count, count), count)]
                sent.append((d, push(give.at[d - 1], target, at_z(d))))
        return [copy for _, copy in sorted(sent, key=lambda item: item[0])]

    left_half = iota((R3, 2 * BK), 1) < BK

    def half_c(t, s):
        picked = []
        for n in range(2):
            wish = asked[t, 1, NB + 2 * s + n]
            pair = plane_c[(wish >> 1) & 31].astype(F32)
            swapped = jnp.concatenate([pair[:, BK:], pair[:, :BK]], axis=1)
            move = ((wish & 1) ^ n).astype(F32)
            picked.append(pair * (1.0 - move) + swapped * move)
        return jnp.where(left_half, picked[0], picked[1]).astype(BF16)

    sent_c = answer(half_c, NB // 2, give_c, got_c)
    for d, h in ((1, 1), (3, 0), (2, 0), (2, 1)):
        came(d, h)
    for copy in across_b:
        copy.wait_recv()
    sent_b = answer(lambda t, s: plane_b[asked[t, 1, s] & 127], NB, give_b, got_b)
    for copy in loads:
        copy.wait()
    for copy in sent_c:
        copy.wait_recv()

    def fold_step(s, carry):
        wish = coords_ref[2, s]
        fold_slot(held_x, s, got_c[(wish >> 6) * (NB // 2) + (s >> 1)], (s & 1).astype(F32), folded)
        return carry

    lax.fori_loop(0, NB, fold_step, 0)
    for copy in sent_b:
        copy.wait_recv()

    moves = []

    unit = (iota((BI, BI), 0) == iota((BI, BI), 1)).astype(F32).astype(BF16)
    for s in range(NB):
        alive = jnp.clip(counts_ref[0] - s, 0, 1).astype(F32)
        total = contract_slot(folded, s, got_b[(coords_ref[1, s] >> 7) * NB + s], alive)
        high = total.astype(BF16)
        for k in range(RR // 128):
            turned = dot_nt(unit, high[128 * k : 128 * k + 128])
            high_ref[s, :, 128 * k : 128 * k + 128] = turned.astype(BF16)
        for d in (2, 1, 3):
            there = pl.ds(pl.multiple_of(lax.rem(x + d, NX) * quarter, quarter), quarter)
            moves.append(push(high_ref.at[s, there, :], rows.at[x, s], at_x(d)))
        turned_high[:, 128 * s : 128 * s + 128] = high
        turned_low[:, 128 * s : 128 * s + 128] = (total - high.astype(F32)).astype(BF16)
    rows[x] = high_ref[:, pl.ds(pl.multiple_of(x * quarter, quarter), quarter), :]
    for copy in tags:
        copy.wait_recv()
    labels = [codes[n].astype(F32) for n in range(NX)]
    along = jnp.concatenate([label[0:1, :] for label in labels], axis=1)
    down = jnp.concatenate([label.T[:, 0:1] for label in labels], axis=0)
    same = (down == along).astype(F32).astype(BF16)
    for copy in moves:
        copy.wait_recv()
    held = rows[...].reshape(RR, RR)
    summed = jnp.dot(same, held, preferred_element_type=F32)
    high = summed.astype(BF16)
    low = (summed - high.astype(F32)).astype(BF16)
    at = 0
    for a in range(4):
        left = held[:, 128 * a : 128 * a + 128]
        strip = dot_tn(left, high[:, 128 * a :]) + dot_tn(left, low[:, 128 * a :])
        for n in range(4 - a):
            g[pl.ds(128 * at, 128), :] = strip[:, 128 * n : 128 * n + 128]
            at += 1

    parts = ((0, PART_0, x, y, at_x, at_y, from_u0, from_v0), (PART_0, PART_1, y, x, at_y, at_x, from_u1, from_v1))

    def span(start, count):
        return pl.ds(pl.multiple_of(start, 8), count)

    def chunk(n, core, d):
        off, count, mu = parts[n][:3]
        return span(core * HALF + off + lax.rem(mu + d, 4) * (count // 4), count // 4)

    pieces = [(n, d) for d in (2, 1, 3, 0) for n in range(2)]
    crossed = [push(g.at[chunk(n, 1 - c, d)], from_c.at[chunk(n, 0, d)], at_c) for n, d in pieces]
    outgoing = [[], []]
    for copy, (n, d) in zip(crossed, pieces):
        copy.wait_recv()
        here = chunk(n, c, d)
        g[here, :] += from_c[chunk(n, 0, d), :]
        if d > 0:
            outgoing[n].append(push(g.at[here], parts[n][6].at[d - 1], parts[n][4](d)))

    def small(n, d):
        off, count, mu, mv = parts[n][:4]
        return span(c * HALF + off + mu * (count // 4) + lax.rem(mv + d, 4) * (count // 16), count // 16)

    second = [[], []]
    for n in range(2):
        for copy in outgoing[n]:
            copy.wait_recv()
        here = chunk(n, c, 0)
        got = parts[n][6]
        g[here, :] = g[here, :] + got[0] + got[1] + got[2]
        second[n] = [push(g.at[small(n, d)], parts[n][7].at[d - 1], parts[n][5](d)) for d in (2, 1, 3)]
    summed_z = [[], []]
    for n in range(2):
        for copy in second[n]:
            copy.wait_recv()
        got = parts[n][7]
        at = 0 if n == 0 else PART_0 // 16
        lines = slice(at, at + parts[n][1] // 16)
        from_z[z, lines, :] = g[small(n, 0), :] + got[0] + got[1] + got[2]
        place = from_z.at[z, lines]
        summed_z[n] = [push(place, place, at_z(d)) for d in (4, 3, 5, 2, 6, 1, 7)]
    feeds[4].wait()
    order = (iota((RR, RR), 0) // R3 == iota((RR, RR), 1) % R2) & (iota((RR, RR), 0) % R3 == iota((RR, RR), 1) // R2)
    order = order.astype(F32).astype(BF16)
    moved = jnp.dot(jnp.concatenate(split(start_ref[...]), axis=0), order, preferred_element_type=F32)
    space[...] = orthonormal_t(moved[:R2] + (moved[R2 : 2 * R2] + moved[2 * R2 :]))


    back = [[], []]
    for n in range(2):
        at = 0 if n == 0 else PART_0 // 16
        here = small(n, 0)
        for copy in summed_z[n]:
            copy.wait_recv()
        lines = slice(at, at + parts[n][1] // 16)
        total = from_z[0, lines]
        for k in range(1, NZ):
            total = total + from_z[k, lines]
        o[here, :] = total
        back[n] = [push(o.at[here], o.at[here], parts[n][5](d)) for d in (2, 1, 3)]
    wide_back = [[], []]
    relayed = []
    for n in range(2):
        for copy in back[n]:
            copy.wait_recv()
        here = chunk(n, c, 0)
        wide_back[n] = [push(o.at[here], o.at[here], parts[n][4](d)) for d in (2, 1, 3)]
        relayed.append(push(o.at[here], o.at[here], at_c))
    for k, d in ((1, 1), (2, 3), (0, 2)):
        for n in range(2):
            wide_back[n][k].wait_recv()
            here = chunk(n, c, 4 - d)
            relayed.append(push(o.at[here], o.at[here], at_c))
    for copy in relayed:
        copy.wait_recv()

    for n, (p, q) in enumerate(TILES):
        tile = o[pl.ds(128 * n, 128), :]
        for ref, part in zip((gh, gm, gl), split(tile)):
            ref[pl.ds(128 * p, 128), pl.ds(128 * q, 128)] = part
        if p != q:
            for ref, part in zip((gh, gm, gl), split(tile.T)):
                ref[pl.ds(128 * q, 128), pl.ds(128 * p, 128)] = part

    def step(n, carry):
        space[...] = orthonormal_t(fine_dot(space[...], gh[...], gm[...], gl[...]))
        return carry

    lax.fori_loop(0, ITERS, step, 0)
    last = space[...]
    wh, wm, _ = split(last)
    both = jnp.dot(jnp.concatenate([wh, wm], axis=0), turned_high[...], preferred_element_type=F32)
    maps[x] = both[:R2] + (both[R2:] + jnp.dot(wh, turned_low[...], preferred_element_type=F32))
    copies = [push(maps.at[x], maps.at[x], at_x(d)) for d in (2, 1, 3)]
    lower = inverse_lower(inner_product(last, fine_dot(last, gh[...], gm[...], gl[...])))
    first = (x * (IB_DEV // NX)).astype(F32)
    for copy in copies:
        copy.wait_recv()
    outs = [jnp.zeros((R2, BI), F32) for _ in range(IB_DEV // NX)]
    for n in range(NX):
        for s in range(NB):
            label = jnp.broadcast_to(labels[n][0:1, 32 * s : 32 * s + 1], (R2, BI)) * (1.0 / 32.0) - first
            term = maps[n, :, 128 * s : 128 * s + 128]
            for k in range(IB_DEV // NX):
                outs[k] = outs[k] + jnp.where(label == float(k), term, 0.0)
    out_ref[...] = fine_dot(lower, *split(jnp.concatenate(outs, axis=1)))
    for copy in started:
        copy.wait_send()


def factor(blocks, coords, counts, slab_b, slab_c, start_t):
    copies = 120
    vmem = pl.BlockSpec(memory_space=pltpu.VMEM)
    hbm = pl.BlockSpec(memory_space=pltpu.HBM)
    return pl.pallas_call(
        factor_kernel,
        out_shape=jax.ShapeDtypeStruct((R2, IB_DEV * BI // NX), F32),
        in_specs=[hbm] * 6,
        out_specs=vmem,
        scratch_shapes=[
            pltpu.SMEM(coords.shape, jnp.int32),
            pltpu.SMEM(counts.shape, jnp.int32),
            pltpu.VMEM((8, 128), jnp.int32),
            pltpu.VMEM(slab_b.shape, BF16),
            pltpu.VMEM(slab_c.shape, BF16),
            pltpu.VMEM(start_t.shape, F32),
            pltpu.VMEM((NB, BI, BJ * BK), BF16),
            pltpu.VMEM((2 * NY * 16, R2, BJ), BF16),
            pltpu.VMEM((2 * NY * 4, R3, 2 * BK), BF16),
            pltpu.VMEM((NZ, 8, 128), jnp.int32),
            pltpu.SMEM((NZ, 8, 128), jnp.int32),
            pltpu.VMEM((NZ - 1, NB, R2, BJ), BF16),
            pltpu.VMEM((NZ - 1, NB // 2, R3, 2 * BK), BF16),
            pltpu.VMEM((NZ * NB, R2, BJ), BF16),
            pltpu.VMEM((NZ * NB // 2, R3, 2 * BK), BF16),
            pltpu.VMEM((NB, R3, BJ, BI), BF16),
            pltpu.VMEM((NB, BI, RR), BF16),
            pltpu.VMEM((RR, NB * BI), BF16),
            pltpu.VMEM((RR, NB * BI), BF16),
            pltpu.VMEM((NX, NB, BI // NX, RR), BF16),
            pltpu.VMEM((NX, 8, 128), jnp.int32),
            pltpu.VMEM((PACKED, 128), F32),
            pltpu.VMEM((PACKED, 128), F32),
            pltpu.VMEM((HALF, 128), F32),
            pltpu.VMEM((3, PART_0 // 4, 128), F32),
            pltpu.VMEM((3, PART_1 // 4, 128), F32),
            pltpu.VMEM((3, PART_0 // 16, 128), F32),
            pltpu.VMEM((3, PART_1 // 16, 128), F32),
            pltpu.VMEM((NZ, HALF // 16, 128), F32),
            pltpu.VMEM((RR, RR), BF16),
            pltpu.VMEM((RR, RR), BF16),
            pltpu.VMEM((RR, RR), BF16),
            pltpu.VMEM((R2, RR), F32),
            pltpu.VMEM((NX, R2, RR), F32),
            pltpu.SemaphoreType.DMA((copies,)),
            pltpu.SemaphoreType.DMA((copies,)),
            pltpu.SemaphoreType.DMA((NB + 1,)),
            pltpu.SemaphoreType.DMA((5,)),
        ],
        compiler_params=pltpu.CompilerParams(
            collective_id=0, has_side_effects=True, vmem_limit_bytes=53 * 1024 * 1024
        ),
        name="factor",
    )(blocks, coords, counts, slab_b, slab_c, start_t)


def body(blocks, coords, counts, factor_b, factor_c, start):
    hold = functools.partial(pltpu.with_memory_space_constraint, memory_space=pltpu.HBM)
    return factor(blocks, hold(coords), counts, hold(factor_b.T), hold(factor_c.T), hold(start.T)).T


def solution(mesh):
    return jax.shard_map(
        body,
        mesh=mesh,
        in_specs=(
            P(("blk", "rep"), None, None),
            P(None, ("blk", "rep")),
            P(("blk", "rep")),
            P("blk", None),
            P("blk", None),
            P(),
        ),
        out_specs=P(("blk", "rep"), None),
        check_vma=False,
    )
```
